32 devices in a mesh: region: 4 (over x, core), sub: 8 (over z, y).
Axes of the slice: x: 2, y: 2, z: 4, core: 2. Of those that a mesh axis runs over, the one named last changes fastest.
Arguments:
- multipliers: float32 [32, 3, 3, 256], P(('region', 'sub')), may hold values from -6 to 6
- direction: float32 [32, 3, 3, 256], P(('region', 'sub')), may hold values from -12 to 12
- residual: float32 [32, 3, 3, 256], P(('region', 'sub')), may hold values from -12 to 12
- reaction: float32 [32, 16, 256], P(('region', 'sub')), may hold values from 0.1 to 2
- viscosity: float32 [32, 16, 256], P(('region', 'sub')), may hold values from 0.5 to 5
- primal_index: int32 [32, 96], P(('region', 'sub')), may hold values from 17 to 2286, as said below
- region_inverse: float32 [4, 768, 768], P('region', 'sub'), as said below
- coarse_map: float32 [32, 96, 384], P(('region', 'sub')), may hold values from -0.4375 to 0.4375
- global_inverse: float32 [384, 384], replicated, as said below
Outputs:
- new_multipliers: float32 [32, 3, 3, 256], P(('region', 'sub'))
- new_residual: float32 [32, 3, 3, 256], P(('region', 'sub'))
- velocity: float32 [32, 3, 16, 256], P(('region', 'sub'))
- pressure: float32 [32, 16, 256], P(('region', 'sub'))
The draws below stay inside these ranges and needn't reach their ends.
Inputs may be any that keep to these rules, and one draw needn't show every extreme that they name: `primal_index`: each row holds 96 different positions, each in the interior of a face (neither face index 0 nor 16 - 1); every row contains the first such position and the last one. `region_inverse`: each region's matrix is symmetric positive definite. `global_inverse`: symmetric positive definite.
All inputs are finite; a program needn't handle non-finite values.
Results may differ from the reference program's by a relative error of at most 0.0001.
Values sent between devices are 32-bit elements; how exact they have to be, the bound alone decides.
No kernel may reach another device: no remote copies, remote signals or barrier semaphores. Data moves between devices by JAX's collectives and lax.ppermute only.
A program may use at most 64 MiB of HBM per device.

```python
import math
import jax
import jax.numpy as jnp
from jax import lax

CELLS = 16
DOM_Z = 4
PRIMAL = 96
GLOBAL_DOFS = 384
LEVELS = 3
SWEEPS = 1
COARSE_SWEEPS = 8
VCYCLES = 2
DOMAINS = 32
FACE = 256
REGION_DOFS = 768
N_REGION = 4
N_SUB = 8


def face_values(key):
    shape = (DOMAINS, 3, 3, FACE)
    position = jnp.arange(DOMAINS, dtype=jnp.float32) / max(DOMAINS - 1, 1)
    values = jnp.clip(jax.random.normal(key, shape, jnp.float32), -4.0, 4.0)
    growth = 1.0 + 2.0 * position
    return values * growth[:, None, None, None]


def draw_direction(key, part):
    return face_values(jax.random.fold_in(key, 11))


def draw_residual(key, part):
    return face_values(jax.random.fold_in(key, 13))


def draw_primal_index(key, part):
    inner = CELLS - 2
    count = 9 * inner * inner
    keys = jax.random.split(jax.random.fold_in(key, 23), DOMAINS)

    def one_row(subkey):
        middle = jax.random.permutation(subkey, count - 2)[:PRIMAL - 2].astype(jnp.int32) + 1
        order = jnp.concatenate([jnp.zeros((1,), jnp.int32), middle, jnp.full((1,), count - 1, jnp.int32)])
        block = order // (inner * inner)
        rest = order % (inner * inner)
        return block * (CELLS * CELLS) + (rest // inner + 1) * CELLS + rest % inner + 1
    return jax.vmap(one_row)(keys)


def spd_matrix(key, order):
    factor = jax.random.normal(key, (order, order), jnp.float32) / jnp.sqrt(jnp.float32(order))
    product = jnp.dot(factor, factor.T, precision=lax.Precision.HIGHEST)
    return 0.5 * (product + product.T) + 0.5 * jnp.eye(order, dtype=jnp.float32)


def draw_region_inverse(key, part):
    keys = jax.random.split(jax.random.fold_in(key, 31), N_REGION)
    return jax.vmap(lambda subkey: spd_matrix(subkey, REGION_DOFS))(keys)


def draw_global_inverse(key, part):
    return spd_matrix(jax.random.fold_in(key, 37), GLOBAL_DOFS)


def with_spikes(values, own_key, source, target, blocks, factor):
    def block_of(dim):
        return (jnp.arange(values.shape[dim]) // (values.shape[dim] // blocks)).reshape((-1,) + (1,) * (values.ndim - 1 - dim))

    one_side = jax.random.permutation(own_key, blocks)[block_of(target)]
    second = (block_of(target) + blocks // 2) % blocks
    return jnp.where((block_of(source) == one_side) | (block_of(source) == second), factor * values, values)


def steps_of(stream_key, dims, cuts, low, largest):
    loudness, own = 1.0, jax.random.fold_in(stream_key, 6)
    for dim, blocks in cuts:
        heights = jnp.exp(jax.random.uniform(jax.random.fold_in(own, dim), (blocks,), jnp.float32, low / len(cuts), largest / len(cuts)))
        loudness = loudness * jnp.repeat(heights, dims[dim] // blocks).reshape([-1 if axis == dim else 1 for axis in range(len(dims))])
    return loudness


def noise(own_key, dims, width, bound, shards=(), kind=jnp.bfloat16):
    result = width * jax.random.normal(own_key, dims, jnp.float32)
    if shards:
        result = result * steps_of(own_key, dims, shards, -0.22, 0.18)
    return jnp.clip(result, -bound, bound).astype(kind)


def bell_draw_with(rng, shape, scale, bound, cuts, heavy, held_as=jnp.bfloat16):
    values = scale * jax.random.normal(rng, shape, jnp.float32)
    if cuts:
        values = values * steps_of(rng, shape, cuts, -0.22, 0.18)
    return jnp.clip(with_spikes(values, jax.random.fold_in(rng, 3), *heavy), -bound, bound).astype(held_as)


def setup_inputs(seed: int = 0) -> dict:
    streams_of = jax.random.split(jax.random.key(seed), 10)
    multipliers = noise(streams_of[0], (DOMAINS, 3, 3, FACE), 1.0, 6.0, ((0, 32),), jnp.float32)
    direction = draw_direction(jax.random.fold_in(streams_of[9], 71), 0)
    residual = draw_residual(jax.random.fold_in(streams_of[9], 71), 0)
    reaction = jnp.clip(jnp.exp(math.log(2.0) - 2.9957323 * jax.random.uniform(streams_of[3], (DOMAINS, CELLS, FACE), jnp.float32) ** steps_of(streams_of[3], (DOMAINS, CELLS, FACE), ((0, 32),), -0.2, 0.2)), 0.1, 2.0)
    viscosity = jnp.clip(jnp.exp(math.log(5.0) - 2.3025851 * jax.random.uniform(streams_of[4], (DOMAINS, CELLS, FACE), jnp.float32) ** steps_of(streams_of[4], (DOMAINS, CELLS, FACE), ((0, 32),), -0.2, 0.2)), 0.5, 5.0)
    primal_index = draw_primal_index(jax.random.fold_in(streams_of[9], 71), 0)
    region_inverse = draw_region_inverse(jax.random.fold_in(streams_of[9], 71), 0)
    coarse_map = bell_draw_with(streams_of[7], (DOMAINS, PRIMAL, GLOBAL_DOFS), REGION_DOFS ** -0.5, 0.4375, ((0, 32),), (0, 2, 32, 2.75), jnp.float32)
    global_inverse = draw_global_inverse(jax.random.fold_in(streams_of[9], 71), 0)
    return dict(multipliers=multipliers, direction=direction, residual=residual, reaction=reaction, viscosity=viscosity, primal_index=primal_index, region_inverse=region_inverse, coarse_map=coarse_map, global_inverse=global_inverse)


damping = 0.8


def operate(field, react, weight):
    padded = jnp.pad(field, ((0, 0), (1, 1), (1, 1), (1, 1)))
    beside = padded[:, 2:, 1:-1, 1:-1] + padded[:, :-2, 1:-1, 1:-1]
    beside = beside + padded[:, 1:-1, 2:, 1:-1] + padded[:, 1:-1, :-2, 1:-1]
    beside = beside + padded[:, 1:-1, 1:-1, 2:] + padded[:, 1:-1, 1:-1, :-2]
    return react * field + weight * (6.0 * field - beside)


def restrict(array):
    shape = array.shape
    lead = shape[:-3]
    return array.reshape(lead + (shape[-3] // 2, 2, shape[-2] // 2, 2, shape[-1] // 2, 2)).mean(axis=(-5, -3, -1))


def prolong(array):
    return jnp.repeat(jnp.repeat(jnp.repeat(array, 2, axis=-3), 2, axis=-2), 2, axis=-1)


def relax(field, source, react, weight, count):
    diagonal = react + 6.0 * weight
    for _ in range(count):
        field = field + damping * (source - operate(field, react, weight)) / diagonal
    return field


def vcycle(field, source, reacts, level):
    weight = 0.25 ** level
    if level == LEVELS - 1:
        return relax(field, source, reacts[level], weight, COARSE_SWEEPS)
    field = relax(field, source, reacts[level], weight, SWEEPS)
    remain = restrict(source - operate(field, reacts[level], weight))
    coarse = vcycle(jnp.zeros_like(remain), remain, reacts, level + 1)
    field = field + prolong(coarse)
    return relax(field, source, reacts[level], weight, SWEEPS)


def local_solve(source, react):
    reacts = [react]
    for _ in range(LEVELS - 1):
        reacts.append(restrict(reacts[-1]))
    field = jnp.zeros_like(source)
    for _ in range(VCYCLES):
        field = vcycle(field, source, reacts, 0)
    return field


def face_cells(picked):
    face = CELLS * CELLS
    block = picked // (3 * face)
    component = (picked // face) % 3
    spot = picked % face
    first = spot // CELLS
    second = spot % CELLS
    upper = CELLS - 1
    place = jnp.where(block == 0, upper * face + spot, jnp.where(block == 1, first * face + upper * CELLS + second, first * face + second * CELLS + upper))
    return component * (CELLS * face) + place


def reference(multipliers, direction, residual, reaction, viscosity, primal_index, region_inverse, coarse_map, global_inverse):
    highest = lax.Precision.HIGHEST
    face = CELLS * CELLS
    rows_y = N_SUB // DOM_Z
    active = direction
    grid = active.reshape(N_REGION, rows_y, DOM_Z, 3, 3, face)
    below_x = jnp.roll(grid[:, :, :, 0], 1, axis=0)
    below_y = jnp.roll(grid[:, :, :, 1], 1, axis=1)
    below_z = jnp.roll(active.reshape(N_REGION, N_SUB, 3, 3, face)[:, :, 2], 1, axis=1).reshape(N_REGION, rows_y, DOM_Z, 3, face)
    below = jnp.stack([below_x, below_y, below_z], axis=3).reshape(DOMAINS, 3, 3, face)
    reacts = reaction.reshape(DOMAINS, CELLS, CELLS, CELLS)

    def one_domain(pieces):
        own, under, react = pieces
        cubic = (3, CELLS, CELLS)
        source = jnp.zeros((3, CELLS, CELLS, CELLS), jnp.float32)
        source = source.at[:, CELLS - 1, :, :].add(own[0].reshape(cubic))
        source = source.at[:, :, CELLS - 1, :].add(own[1].reshape(cubic))
        source = source.at[:, :, :, CELLS - 1].add(own[2].reshape(cubic))
        source = source.at[:, 0, :, :].add(-under[0].reshape(cubic))
        source = source.at[:, :, 0, :].add(-under[1].reshape(cubic))
        source = source.at[:, :, :, 0].add(-under[2].reshape(cubic))
        return local_solve(source, react)

    base = lax.map(one_domain, (active, below, reacts))
    primal = jnp.take_along_axis(active.reshape(DOMAINS, -1), primal_index, axis=1)
    grouped = primal.reshape(N_REGION, REGION_DOFS)
    region_part = jnp.einsum("rij,rj->ri", region_inverse, grouped, precision=highest).reshape(DOMAINS, PRIMAL)
    total = jnp.einsum("skg,sk->g", coarse_map, primal, precision=highest)
    top = jnp.dot(global_inverse, total, precision=highest)
    lifted = region_part + jnp.einsum("skg,g->sk", coarse_map, top, precision=highest)
    spots = face_cells(primal_index)
    flat = base.reshape(DOMAINS, -1)
    flat = jax.vmap(lambda row, where_to, values: row.at[where_to].add(values))(flat, spots, lifted)
    fields = flat.reshape(DOMAINS, 3, CELLS, CELLS, CELLS)
    upper = jnp.stack([fields[:, :, CELLS - 1, :, :], fields[:, :, :, CELLS - 1, :], fields[:, :, :, :, CELLS - 1]], axis=1).reshape(DOMAINS, 3, 3, face)
    lower_flat = jnp.stack([fields[:, :, 0, :, :], fields[:, :, :, 0, :], fields[:, :, :, :, 0]], axis=1).reshape(DOMAINS, 3, 3, face)
    lower = lower_flat.reshape(N_REGION, rows_y, DOM_Z, 3, 3, face)
    after_x = jnp.roll(lower[:, :, :, 0], -1, axis=0)
    after_y = jnp.roll(lower[:, :, :, 1], -1, axis=1)
    after_z = jnp.roll(lower_flat.reshape(N_REGION, N_SUB, 3, 3, face)[:, :, 2], -1, axis=1).reshape(N_REGION, rows_y, DOM_Z, 3, face)
    after = jnp.stack([after_x, after_y, after_z], axis=3).reshape(DOMAINS, 3, 3, face)
    jump = upper - after
    views = viscosity.reshape(DOMAINS, CELLS, CELLS, CELLS)

    def pressure_one(pieces):
        field, ahead, visc = pieces
        step_x = jnp.concatenate([field[0, 1:], ahead[0, 0].reshape(1, CELLS, CELLS)], axis=0) - field[0]
        step_y = jnp.concatenate([field[1, :, 1:], ahead[1, 1].reshape(CELLS, 1, CELLS)], axis=1) - field[1]
        step_z = jnp.concatenate([field[2, :, :, 1:], ahead[2, 2].reshape(CELLS, CELLS, 1)], axis=2) - field[2]
        return -visc * (step_x + step_y + step_z)

    pressure = lax.map(pressure_one, (fields, after, views)).reshape(DOMAINS, CELLS, face)
    velocity = fields.reshape(DOMAINS, 3, CELLS, face)
    curvature = jnp.sum(active * jump)
    squares = jnp.sum(residual * residual)
    alpha = squares / curvature
    return (multipliers + alpha * active, residual - alpha * jump, velocity, pressure)
```

```python
import functools

import jax
import jax.numpy as jnp
from jax import lax
from jax.experimental import pallas as pl
from jax.experimental.pallas import tpu as pltpu
from jax.sharding import PartitionSpec as P

DOM_Z = 4
LEVELS = 3
SWEEPS = 1
COARSE_SWEEPS = 8
VCYCLES = 2
LANES = 128

damping = 0.8


def shifted_2(x, axis, by):
    count = lax.axis_size(axis)
    return lax.ppermute(x, axis, [(i, (i + by) % count) for i in range(count)])


def iota(shape, dim):
    return lax.broadcasted_iota(jnp.int32, shape, dim)


def parts_of(x, count=3):
    result = []
    for step in range(count):
        piece = x.astype(jnp.bfloat16)
        result.append(piece)
        if step < count - 1:
            x = x - piece.astype(jnp.float32)
    return result


def times_choice(x, choice):
    rows = x.shape[0]
    stacked = jnp.concatenate(parts_of(x), axis=0)
    y = jnp.dot(stacked, choice, preferred_element_type=jnp.float32)
    return y[:rows] + y[rows : 2 * rows] + y[2 * rows :]


def choice_times(choice, x):
    width = x.shape[1]
    stacked = jnp.concatenate(parts_of(x), axis=1)
    y = jnp.dot(choice, stacked, preferred_element_type=jnp.float32)
    return y[:, :width] + y[:, width : 2 * width] + y[:, 2 * width :]


def one_hot(condition):
    return jnp.where(condition, 1.0, 0.0).astype(jnp.bfloat16)


def decode(picked, cells):
    face = cells * cells
    zero = jnp.zeros_like(picked)
    one = zero + 1
    block = jnp.where(picked >= 3 * face, one, zero) + jnp.where(picked >= 6 * face, one, zero)
    rest = picked - 3 * face * block
    component = jnp.where(rest >= face, one, zero) + jnp.where(rest >= 2 * face, one, zero)
    spot = rest - face * component
    first = lax.div(spot, zero + cells)
    second = spot - first * cells
    end = cells - 1
    x = jnp.where(block == 0, end, first)
    y = jnp.where(block == 0, first, jnp.where(block == 1, end, second))
    z = jnp.where(block == 2, end, second)
    return 3 * block + component, spot, component * cells + x, y * cells + z


def spread(faces, cells):
    face = cells * cells
    here = lax.div(iota((cells, face), 1), jnp.full((cells, face), cells, jnp.int32)) == iota((cells, face), 0)
    rows = [jnp.where(here, jnp.broadcast_to(faces[c : c + 1], (cells, face)), 0.0) for c in range(faces.shape[0])]
    return jnp.concatenate(rows, axis=0)


def mask_sum(x, cells):
    face = cells * cells
    here = lax.div(iota((cells, face), 1), jnp.full((cells, face), cells, jnp.int32)) == iota((cells, face), 0)
    rows = [
        jnp.sum(jnp.where(here, x[c * cells : (c + 1) * cells], 0.0), axis=0, keepdims=True)
        for c in range(x.shape[0] // cells)
    ]
    return jnp.concatenate(rows, axis=0)


def place_matrices(cells):
    face = cells * cells
    row = iota((face, face), 0)
    column = iota((face, face), 1)
    second = row - lax.div(row, jnp.full((face, face), cells, jnp.int32)) * cells
    end = cells - 1
    lower = jnp.concatenate([one_hot(column == second), one_hot(column == second * cells)], axis=0)
    upper = jnp.concatenate(
        [one_hot(column == second + end * cells), one_hot(column == second * cells + end)], axis=0
    )
    return lower, upper


def pick_matrices(cells):
    face = cells * cells
    row = iota((face, face), 0)
    column = iota((face, face), 1)
    second = column - lax.div(column, jnp.full((face, face), cells, jnp.int32)) * cells
    end = cells - 1
    return jnp.concatenate(
        [
            one_hot(row == second),
            one_hot(row == second * cells),
            one_hot(row == second + end * cells),
            one_hot(row == second * cells + end),
        ],
        axis=1,
    )


def shift(field, by, dim):
    size = field.shape[dim]
    return pltpu.roll(field, by % size, dim)


def pair_mean(field, cells, step, where_x, where_y, where_z):
    for position, dim, reach in ((where_z, 1, step), (where_y, 1, step * cells), (where_x, 0, step)):
        even = (position & step) == 0
        field = 0.5 * (field + jnp.where(even, shift(field, -reach, dim), shift(field, reach, dim)))
    return field


def positions(rows, cells):
    face = cells * cells
    shape = (rows, face)
    lane = iota(shape, 1)
    row = iota(shape, 0)
    where_x = row & (cells - 1)
    where_z = lane & (cells - 1)
    where_y = lax.shift_right_logical(lane, jnp.full(shape, cells.bit_length() - 1, jnp.int32))
    return where_x, where_y, where_z


def before_kernel(
    cells,
    columns,
    direction,
    residual,
    reaction,
    primal_index,
    region_inverse,
    coarse_map,
    source_out,
    front_out,
    inverse_out,
    lower_out,
    upper_out,
    pick_out,
    spots_out,
    choose_out,
):
    face = cells * cells
    lower, upper = place_matrices(cells)
    lower_out[...] = lower
    upper_out[...] = upper
    pick_out[...] = pick_matrices(cells)
    where_x, where_y, where_z = positions(cells, cells)
    react = reaction[0]
    for level in range(LEVELS):
        weight = 0.25**level
        diagonal = react + 6.0 * weight
        inverse_out[level] = damping / diagonal
        inverse_out[LEVELS + level] = diagonal
        if level < LEVELS - 1:
            react = pair_mean(react, cells, 2**level, where_x, where_y, where_z)
    faces = [direction[0, d] for d in range(3)]
    row_x = iota((cells, face), 0)
    source = times_choice(jnp.concatenate([spread(faces[1], cells), spread(faces[2], cells)], axis=1), upper)
    own_x = jnp.concatenate(
        [jnp.where(row_x == cells - 1, jnp.broadcast_to(faces[0][c : c + 1], (cells, face)), 0.0) for c in range(3)],
        axis=0,
    )
    source_out[...] = source + own_x
    picked = primal_index[...]
    count = picked.shape[1]
    group_row, _, place_row, _ = decode(picked, cells)
    choose_out[...] = jnp.concatenate(
        [
            one_hot(iota((3 * cells, count), 0) == place_row),
            one_hot(iota((16, count), 0) == group_row),
        ],
        axis=0,
    )
    wide = jnp.broadcast_to(picked.astype(jnp.float32), (count, count))
    diagonal = iota((count, count), 0) == iota((count, count), 1)
    picked_column = jnp.sum(jnp.where(diagonal, wide, 0.0), axis=1, keepdims=True).astype(jnp.int32)
    group, spot, _, lane = decode(picked_column, cells)
    on_spot = iota((count, face), 1) == spot
    on_lane = iota((count, face), 1) == lane
    spots_out[...] = jnp.concatenate([jnp.where(on_lane, 1.0, 0.0), jnp.where(on_spot, 1.0, 0.0)], axis=1)
    nine = jnp.concatenate(faces + [jnp.zeros((7, face), jnp.float32)], axis=0)
    gathered = choice_times(one_hot(iota((count, 16), 1) == group), nine)
    primal = jnp.sum(jnp.where(on_spot, gathered, 0.0), axis=1, keepdims=True)
    share = jnp.sum(primal * coarse_map[0], axis=0, keepdims=True)
    product = jnp.sum(primal * region_inverse[0], axis=0, keepdims=True)
    line = jnp.sum(
        jnp.where(iota((count, LANES), 0) == iota((count, LANES), 1), primal, 0.0), axis=0, keepdims=True
    )
    squares = jnp.sum(residual[0] * residual[0])
    line = jnp.where(iota((1, LANES), 1) == count + 1, squares, line)
    front_out[...] = jnp.zeros_like(front_out)
    width = product.shape[1]
    used = width // LANES
    for i in range(used):
        front_out[i : i + 1, :] = product[:, i * LANES : (i + 1) * LANES]
    front_out[used : used + 1, :] = line
    for i in range(columns // LANES):
        front_out[used + 1 + i : used + 2 + i, :] = share[:, i * LANES : (i + 1) * LANES]


def solve_kernel(
    cells,
    head,
    sizes,
    source_own,
    below_x,
    below_y,
    below_z,
    inverses,
    front,
    lower,
    pick,
    base_out,
    ends_out,
    send_out,
):
    face = cells * cells
    rows = 3 * cells
    n_region, n_sub = sizes
    row_x = iota((cells, face), 0)
    source = source_own[...] - times_choice(
        jnp.concatenate([spread(below_y[...], cells), spread(below_z[...], cells)], axis=1), lower[...]
    )
    source = source - jnp.concatenate(
        [jnp.where(row_x == 0, jnp.broadcast_to(below_x[c : c + 1, :], (cells, face)), 0.0) for c in range(3)],
        axis=0,
    )
    where_x, where_y, where_z = positions(rows, cells)

    def tall(x):
        return jnp.concatenate([x] * 3, axis=0)

    inverse = [tall(inverses[level]) for level in range(LEVELS)]
    diagonal = [tall(inverses[LEVELS + level]) for level in range(LEVELS)]

    def beside(field, level):
        step = 2**level
        last = cells - step
        total = jnp.where(where_x < last, shift(field, -step, 0), 0.0)
        total = total + jnp.where(where_x >= step, shift(field, step, 0), 0.0)
        total = total + jnp.where(where_y < last, shift(field, -step * cells, 1), 0.0)
        total = total + jnp.where(where_y >= step, shift(field, step * cells, 1), 0.0)
        total = total + jnp.where(where_z < last, shift(field, -step, 1), 0.0)
        return total + jnp.where(where_z >= step, shift(field, step, 1), 0.0)

    def relax(field, right, level, sweeps):
        weight = 0.25**level
        for _ in range(sweeps):
            if field is None:
                field = inverse[level] * right
            else:
                field = (1.0 - damping) * field + inverse[level] * (right + weight * beside(field, level))
        return field

    def vcycle(field, right, level):
        if level == LEVELS - 1:
            return relax(field, right, level, COARSE_SWEEPS)
        field = relax(field, right, level, SWEEPS)
        remain = right - diagonal[level] * field + 0.25**level * beside(field, level)
        remain = pair_mean(remain, cells, 2**level, where_x, where_y, where_z)
        field = field + vcycle(None, remain, level + 1)
        return relax(field, right, level, SWEEPS)

    field = None
    for _ in range(VCYCLES):
        field = vcycle(field, source, 0)
    base_out[...] = field
    energy = jnp.sum(source * field)
    ends = times_choice(field, pick[...])
    lower_y, lower_z, upper_y, upper_z = [
        mask_sum(ends[:, i * face : (i + 1) * face], cells) for i in range(4)
    ]
    lower_x = jnp.concatenate([field[c * cells : c * cells + 1] for c in range(3)], axis=0)
    upper_x = jnp.concatenate([field[(c + 1) * cells - 1 : (c + 1) * cells] for c in range(3)], axis=0)
    ends_out[...] = jnp.concatenate([upper_x, upper_y, upper_z, jnp.zeros((7, face), jnp.float32)], axis=0)
    scalar_row, scalar_lane, halo_row = head
    message = front[...]
    at_scalar = (iota(message.shape, 0) == scalar_row) & (iota(message.shape, 1) == scalar_lane)
    message = jnp.where(at_scalar, energy, message)
    for device in range(n_region * n_sub):
        send_out[device] = message
    me_region = lax.axis_index("region")
    me_sub = lax.axis_index("sub")
    to_x = lax.rem(me_region + n_region - 1, n_region) * n_sub + me_sub
    to_y = me_region * n_sub + lax.rem(me_sub + n_sub - DOM_Z, n_sub)
    to_z = me_region * n_sub + lax.rem(me_sub + n_sub - 1, n_sub)
    for target, values in ((to_x, lower_x), (to_y, lower_y), (to_z, lower_z)):
        for i in range(face // LANES):
            send_out[target, halo_row + 3 * i : halo_row + 3 * i + 3, :] = values[:, i * LANES : (i + 1) * LANES]


def after_kernel(
    cells,
    head,
    sizes,
    received,
    base,
    ends,
    upper,
    spots,
    choose,
    direction,
    multipliers,
    residual,
    viscosity,
    region_inverse,
    coarse_map,
    global_inverse,
    multipliers_out,
    residual_out,
    velocity_out,
    pressure_out,
):
    face = cells * cells
    n_region, n_sub = sizes
    scalar_row, count, halo_row = head
    used = scalar_row
    columns = global_inverse.shape[0]
    me_region = lax.axis_index("region")
    me_sub = lax.axis_index("sub")
    region_sums = [jnp.sum(received[r * n_sub : (r + 1) * n_sub], axis=0) for r in range(n_region)]
    everything = functools.reduce(lambda a, b: a + b, region_sums)
    total = jnp.concatenate(
        [everything[used + 1 + i : used + 2 + i] for i in range(columns // LANES)], axis=1
    )
    products = jnp.concatenate(
        [jnp.concatenate([region_sums[r][i : i + 1] for i in range(used)], axis=1) for r in range(n_region)], axis=0
    )
    lines = received[:, scalar_row, :]
    primal = jnp.concatenate(
        [
            jnp.concatenate([lines[r * n_sub + q : r * n_sub + q + 1, :count] for q in range(n_sub)], axis=1)
            for r in range(n_region)
        ],
        axis=0,
    )
    top = jnp.dot(
        jnp.broadcast_to(total, (8, columns)), global_inverse[...], precision=lax.Precision.HIGHEST,
        preferred_element_type=jnp.float32,
    )[:1]
    own_line = everything[scalar_row : scalar_row + 1]
    lane = iota((1, LANES), 1)
    energy = jnp.sum(jnp.where(lane == count, own_line, 0.0), axis=1, keepdims=True)
    squares = jnp.sum(jnp.where(lane == count + 1, own_line, 0.0), axis=1, keepdims=True)
    quadratic = jnp.sum(jnp.sum(products * primal, axis=0, keepdims=True), axis=1, keepdims=True)
    curvature = energy + quadratic + jnp.sum(total * top, axis=1, keepdims=True)
    alpha = squares / curvature
    mine = jnp.sum(
        jnp.where(iota(primal.shape, 0) == me_region, primal, 0.0), axis=0, keepdims=True
    )
    weighed = jnp.sum(region_inverse[0] * mine, axis=1, keepdims=True)
    lifted = weighed + jnp.sum(coarse_map[0] * top, axis=1, keepdims=True)
    added = choice_times(choose[...], lifted * spots[...])
    velocity = base[...] + added[: 3 * cells, :face]
    upper_faces = ends[:9] + added[3 * cells : 3 * cells + 9, face:]
    for c in range(3):
        velocity_out[0, c] = velocity[c * cells : (c + 1) * cells]
    from_x = lax.rem(me_region + 1, n_region) * n_sub + me_sub
    from_y = me_region * n_sub + lax.rem(me_sub + DOM_Z, n_sub)
    from_z = me_region * n_sub + lax.rem(me_sub + 1, n_sub)
    after = [
        jnp.concatenate(
            [received[place, halo_row + 3 * i : halo_row + 3 * i + 3, :] for i in range(face // LANES)], axis=1
        )
        for place in (from_x, from_y, from_z)
    ]
    for d in range(3):
        jump = upper_faces[3 * d : 3 * d + 3] - after[d]
        residual_out[0, d] = residual[0, d] - alpha * jump
        multipliers_out[0, d] = multipliers[0, d] + alpha * direction[0, d]
    ahead = jnp.concatenate(
        [spread(after[1][1:2], cells), spread(after[2][2:3], cells)], axis=1
    )
    ahead = times_choice(ahead, upper[...])
    where_x, where_y, where_z = positions(cells, cells)
    end = cells - 1
    field_x, field_y, field_z = [velocity[c * cells : (c + 1) * cells] for c in range(3)]
    step_x = jnp.where(where_x == end, jnp.broadcast_to(after[0][0:1], (cells, face)), shift(field_x, -1, 0))
    step_y = jnp.where(where_y == end, 0.0, shift(field_y, -cells, 1))
    step_z = jnp.where(where_z == end, 0.0, shift(field_z, -1, 1))
    step = (step_x - field_x) + (step_y - field_y) + (step_z - field_z) + ahead
    pressure_out[0] = -viscosity[0] * step


def body(
    sizes,
    multipliers,
    direction,
    residual,
    reaction,
    viscosity,
    primal_index,
    region_inverse,
    coarse_map,
    global_inverse,
):
    n_region, n_sub = sizes
    devices = n_region * n_sub
    cells = reaction.shape[1]
    face = reaction.shape[2]
    count = primal_index.shape[1]
    columns = coarse_map.shape[2]
    used = region_inverse.shape[2] // LANES
    halo_row = used + 1 + columns // LANES
    height = -(-(halo_row + 3 * face // LANES) // 8) * 8
    head = (used, count, halo_row)
    rows = 3 * cells
    f32 = jnp.float32
    vmem = pl.BlockSpec(memory_space=pltpu.VMEM)

    def call(kernel, out_shape, *operands):
        return pl.pallas_call(
            kernel,
            out_shape=out_shape,
            in_specs=[vmem] * len(operands),
            out_specs=[vmem] * len(out_shape),
            compiler_params=pltpu.CompilerParams(vmem_limit_bytes=32 * 1024 * 1024),
        )(*operands)

    active = direction[0]
    below_x = shifted_2(active[0], "region", 1)
    below_y = shifted_2(active[1], "sub", DOM_Z)
    below_z = shifted_2(active[2], "sub", 1)
    source, front, inverses, lower, upper, pick, spots, choose = call(
        functools.partial(before_kernel, cells, columns),
        [
            jax.ShapeDtypeStruct((rows, face), f32),
            jax.ShapeDtypeStruct((height, LANES), f32),
            jax.ShapeDtypeStruct((2 * LEVELS, cells, face), f32),
            jax.ShapeDtypeStruct((2 * face, face), jnp.bfloat16),
            jax.ShapeDtypeStruct((2 * face, face), jnp.bfloat16),
            jax.ShapeDtypeStruct((face, 4 * face), jnp.bfloat16),
            jax.ShapeDtypeStruct((count, 2 * face), f32),
            jax.ShapeDtypeStruct((rows + 16, count), jnp.bfloat16),
        ],
        direction,
        residual,
        reaction,
        primal_index,
        region_inverse,
        coarse_map,
    )
    base, ends, sent = call(
        functools.partial(solve_kernel, cells, head, sizes),
        [
            jax.ShapeDtypeStruct((rows, face), f32),
            jax.ShapeDtypeStruct((16, face), f32),
            jax.ShapeDtypeStruct((devices, height, LANES), f32),
        ],
        source,
        below_x,
        below_y,
        below_z,
        inverses,
        front,
        lower,
        pick,
    )
    received = lax.all_to_all(sent, ("region", "sub"), 0, 0, tiled=True)
    return tuple(
        call(
            functools.partial(after_kernel, cells, head, sizes),
            [
                jax.ShapeDtypeStruct(multipliers.shape, f32),
                jax.ShapeDtypeStruct(residual.shape, f32),
                jax.ShapeDtypeStruct((1, 3, cells, face), f32),
                jax.ShapeDtypeStruct((1, cells, face), f32),
            ],
            received,
            base,
            ends,
            upper,
            spots,
            choose,
            direction,
            multipliers,
            residual,
            viscosity,
            region_inverse,
            coarse_map,
            global_inverse,
        )
    )


def solution(mesh):
    sizes = (mesh.shape["region"], mesh.shape["sub"])
    whole = P(("region", "sub"))
    in_specs = (whole,) * 6 + (P("region", "sub"), whole, P())
    return jax.shard_map(
        functools.partial(body, sizes), mesh=mesh, in_specs=in_specs, out_specs=(whole,) * 4, check_vma=False
    )
```

```python
import functools

import jax
import jax.numpy as jnp
from jax import lax
from jax.experimental import pallas as pl
from jax.experimental.pallas import tpu as pltpu
from jax.sharding import PartitionSpec as P

DOM_Z = 4
LEVELS = 3
SWEEPS = 1
COARSE_SWEEPS = 8
VCYCLES = 2
LANES = 128

damping = 0.8


def shifted_2(x, axis, by):
    count = lax.axis_size(axis)
    return lax.ppermute(x, axis, [(i, (i + by) % count) for i in range(count)])


def iota(shape, dim):
    return lax.broadcasted_iota(jnp.int32, shape, dim)


def parts_of(x, count=3):
    result = []
    for step in range(count):
        piece = x.astype(jnp.bfloat16)
        result.append(piece)
        if step < count - 1:
            x = x - piece.astype(jnp.float32)
    return result


def times_choice(x, choice):
    rows = x.shape[0]
    stacked = jnp.concatenate(parts_of(x), axis=0)
    y = jnp.dot(stacked, choice, preferred_element_type=jnp.float32)
    return y[:rows] + y[rows : 2 * rows] + y[2 * rows :]


def choice_times(choice, x):
    width = x.shape[1]
    stacked = jnp.concatenate(parts_of(x), axis=1)
    y = jnp.dot(choice, stacked, preferred_element_type=jnp.float32)
    return y[:, :width] + y[:, width : 2 * width] + y[:, 2 * width :]


def one_hot(condition):
    return jnp.where(condition, 1.0, 0.0).astype(jnp.bfloat16)


def decode(picked, cells):
    face = cells * cells
    zero = jnp.zeros_like(picked)
    one = zero + 1
    block = jnp.where(picked >= 3 * face, one, zero) + jnp.where(picked >= 6 * face, one, zero)
    rest = picked - 3 * face * block
    component = jnp.where(rest >= face, one, zero) + jnp.where(rest >= 2 * face, one, zero)
    spot = rest - face * component
    first = lax.div(spot, zero + cells)
    second = spot - first * cells
    end = cells - 1
    x = jnp.where(block == 0, end, first)
    y = jnp.where(block == 0, first, jnp.where(block == 1, end, second))
    z = jnp.where(block == 2, end, second)
    return 3 * block + component, spot, component * cells + x, y * cells + z


def faces_of(rows):
    return [jnp.concatenate([rows[3 * d + c] for c in range(3)], axis=0) for d in range(3)]


def spread(faces, cells):
    face = cells * cells
    here = lax.div(iota((cells, face), 1), jnp.full((cells, face), cells, jnp.int32)) == iota((cells, face), 0)
    rows = [jnp.where(here, jnp.broadcast_to(faces[c : c + 1], (cells, face)), 0.0) for c in range(faces.shape[0])]
    return jnp.concatenate(rows, axis=0)


def mask_sum(x, cells):
    face = cells * cells
    here = lax.div(iota((cells, face), 1), jnp.full((cells, face), cells, jnp.int32)) == iota((cells, face), 0)
    rows = [
        jnp.sum(jnp.where(here, x[c * cells : (c + 1) * cells], 0.0), axis=0, keepdims=True)
        for c in range(x.shape[0] // cells)
    ]
    return jnp.concatenate(rows, axis=0)


def place_matrix(cells, upper):
    face = cells * cells
    row = iota((face, face), 0)
    column = iota((face, face), 1)
    second = row & (cells - 1)
    end = cells - 1 if upper else 0
    return jnp.concatenate(
        [one_hot(column == second + end * cells), one_hot(column == second * cells + end)], axis=0
    )


def pick_matrix(cells, upper):
    face = cells * cells
    row = iota((face, face), 0)
    column = iota((face, face), 1)
    second = column & (cells - 1)
    end = cells - 1 if upper else 0
    return jnp.concatenate(
        [one_hot(row == second + end * cells), one_hot(row == second * cells + end)], axis=1
    )


def face_ends(field, pick, cells, upper):
    face = cells * cells
    at = cells - 1 if upper else 0
    ends = times_choice(field, pick)
    on_x = [field[c * cells + at : c * cells + at + 1] for c in range(3)]
    return jnp.concatenate(on_x, axis=0), mask_sum(ends[:, :face], cells), mask_sum(ends[:, face:], cells)


def column_of(line):
    count = line.shape[1]
    wide = jnp.broadcast_to(line.astype(jnp.float32), (count, count))
    diagonal = iota((count, count), 0) == iota((count, count), 1)
    return jnp.sum(jnp.where(diagonal, wide, 0.0), axis=1, keepdims=True).astype(jnp.int32)


def shift(field, by, dim):
    size = field.shape[dim]
    return pltpu.roll(field, by % size, dim)


def pair_mean(field, cells, step, where_x, where_y, where_z):
    for position, dim, reach in ((where_z, 1, step), (where_y, 1, step * cells), (where_x, 0, step)):
        even = (position & step) == 0
        field = 0.5 * (field + jnp.where(even, shift(field, -reach, dim), shift(field, reach, dim)))
    return field


def positions(rows, cells):
    face = cells * cells
    shape = (rows, face)
    lane = iota(shape, 1)
    row = iota(shape, 0)
    where_x = row & (cells - 1)
    where_z = lane & (cells - 1)
    where_y = lax.shift_right_logical(lane, jnp.full(shape, cells.bit_length() - 1, jnp.int32))
    return where_x, where_y, where_z


def load(pairs, semaphores):
    copies = [pltpu.make_async_copy(a, b, semaphores.at[i]) for i, (a, b) in enumerate(pairs)]
    for copy in copies:
        copy.start()
    return copies


def before_kernel(
    cells,
    sizes,
    direction_in,
    residual_in,
    reaction_in,
    primal_index_in,
    region_inverse_in,
    coarse_map_in,
    direction,
    residual,
    source_out,
    front_out,
    inverse_out,
    lower_out,
    upper_out,
    pick_out,
    reaction,
    primal_index,
    region_inverse,
    coarse_map,
    semaphores,
):
    copies = load(
        [
            (direction_in, direction),
            (reaction_in, reaction),
            (primal_index_in, primal_index),
            (residual_in, residual),
            (coarse_map_in, coarse_map),
            (region_inverse_in, region_inverse),
        ],
        semaphores,
    )
    face = cells * cells
    n_sub = sizes[1]
    lower_out[...] = place_matrix(cells, False)
    upper = place_matrix(cells, True)
    upper_out[...] = upper
    pick_out[...] = pick_matrix(cells, False)
    for copy in copies:
        copy.wait()
    where_x, where_y, where_z = positions(cells, cells)
    react = reaction[0]
    for level in range(LEVELS):
        weight = 0.25**level
        diagonal = react + 6.0 * weight
        inverse_out[level] = damping / diagonal
        inverse_out[LEVELS + level] = diagonal
        if level < LEVELS - 1:
            react = pair_mean(react, cells, 2**level, where_x, where_y, where_z)
    faces = faces_of(direction)
    row_x = iota((cells, face), 0)
    source = times_choice(jnp.concatenate([spread(faces[1], cells), spread(faces[2], cells)], axis=1), upper)
    own_x = jnp.concatenate(
        [jnp.where(row_x == cells - 1, jnp.broadcast_to(faces[0][c : c + 1], (cells, face)), 0.0) for c in range(3)],
        axis=0,
    )
    source_out[...] = source + own_x
    count = primal_index.shape[1]
    group, spot, _, _ = decode(column_of(primal_index[...]), cells)
    nine = jnp.concatenate(faces + [jnp.zeros((7, face), jnp.float32)], axis=0)
    gathered = choice_times(one_hot(iota((count, 16), 1) == group), nine)
    primal = jnp.sum(jnp.where(iota((count, face), 1) == spot, gathered, 0.0), axis=1, keepdims=True)
    share = jnp.sum(primal * coarse_map[0], axis=0, keepdims=True)
    product = jnp.sum(primal * region_inverse[0], axis=0, keepdims=True)
    lane = iota((1, LANES), 1)
    line = jnp.sum(
        jnp.where(iota((count, LANES), 0) == iota((count, LANES), 1), primal, 0.0), axis=0, keepdims=True
    )
    blank = jnp.zeros((1, LANES - count), jnp.float32)
    blocks = jnp.concatenate(
        [jnp.concatenate([product[:, q * count : (q + 1) * count], blank], axis=1) for q in range(n_sub)], axis=0
    )
    me_sub = lax.axis_index("sub")
    own = jnp.sum(jnp.where(iota(blocks.shape, 0) == me_sub, blocks * line, 0.0))
    blocks = pltpu.roll(blocks, n_sub - 1 - me_sub, 0)
    half = n_sub // 2
    twice = jnp.where(iota((half, LANES), 0) == (half - 1 if n_sub % 2 == 0 else half), 1.0, 2.0)
    squares = jnp.sum(residual[...] * residual[...])
    line = jnp.where(lane == count, own, jnp.where(lane == count + 1, squares, line))
    front_out[...] = jnp.zeros_like(front_out)
    front_out[:half, :] = blocks[:half] * twice
    front_out[half : half + 1, :] = line
    for i in range(share.shape[1] // LANES):
        front_out[half + 1 + i : half + 2 + i, :] = share[:, i * LANES : (i + 1) * LANES]


def solve_kernel(
    cells,
    sizes,
    count,
    source_own,
    from_x,
    from_y,
    from_z,
    inverses,
    front,
    lower,
    base_out,
    send_out,
):
    face = cells * cells
    rows = 3 * cells
    below_x, below_y, below_z = [faces_of(ref)[d] for d, ref in enumerate((from_x, from_y, from_z))]
    n_region, n_sub = sizes
    row_x = iota((cells, face), 0)
    source = source_own[...] - times_choice(
        jnp.concatenate([spread(below_y, cells), spread(below_z, cells)], axis=1), lower[...]
    )
    source = source - jnp.concatenate(
        [jnp.where(row_x == 0, jnp.broadcast_to(below_x[c : c + 1], (cells, face)), 0.0) for c in range(3)],
        axis=0,
    )
    where_x, where_y, where_z = positions(rows, cells)

    def tall(x):
        return jnp.concatenate([x] * 3, axis=0)

    inverse = [tall(inverses[level]) for level in range(LEVELS)]
    diagonal = [tall(inverses[LEVELS + level]) for level in range(LEVELS)]

    def beside(field, level):
        step = 2**level
        last = cells - step
        total = jnp.where(where_x < last, shift(field, -step, 0), 0.0)
        total = total + jnp.where(where_x >= step, shift(field, step, 0), 0.0)
        total = total + jnp.where(where_y < last, shift(field, -step * cells, 1), 0.0)
        total = total + jnp.where(where_y >= step, shift(field, step * cells, 1), 0.0)
        total = total + jnp.where(where_z < last, shift(field, -step, 1), 0.0)
        return total + jnp.where(where_z >= step, shift(field, step, 1), 0.0)

    def relax(field, right, level, sweeps):
        weight = 0.25**level
        for _ in range(sweeps):
            if field is None:
                field = inverse[level] * right
            else:
                field = (1.0 - damping) * field + inverse[level] * (right + weight * beside(field, level))
        return field

    def vcycle(field, right, level):
        if level == LEVELS - 1:
            return relax(field, right, level, COARSE_SWEEPS)
        field = relax(field, right, level, SWEEPS)
        remain = right - diagonal[level] * field + 0.25**level * beside(field, level)
        remain = pair_mean(remain, cells, 2**level, where_x, where_y, where_z)
        field = field + vcycle(None, remain, level + 1)
        return relax(field, right, level, SWEEPS)

    field = None
    for _ in range(VCYCLES):
        field = vcycle(field, source, 0)
    base_out[...] = field
    energy = jnp.sum(source * field)
    message = front[...]
    at = (iota(message.shape, 0) == sizes[1] // 2) & (iota(message.shape, 1) == count)
    message = message + jnp.where(at, energy, 0.0)
    for device in range(sizes[0] * sizes[1]):
        send_out[device] = message


def ends_kernel(cells, base, pick, lower_x, lower_y, lower_z):
    lower_x[...], lower_y[...], lower_z[...] = face_ends(base[...], pick[...], cells, False)


def between_kernel(
    cells,
    base,
    primal_index_in,
    region_inverse_in,
    coarse_map_in,
    global_inverse_in,
    multipliers_in,
    viscosity_in,
    multipliers,
    viscosity,
    ends_out,
    region_out,
    through_out,
    global_out,
    spots_out,
    choose_out,
    primal_index,
    region_inverse,
    coarse_map,
    global_inverse,
    semaphores,
):
    copies = load(
        [
            (primal_index_in, primal_index),
            (region_inverse_in, region_inverse),
            (coarse_map_in, coarse_map),
            (global_inverse_in, global_inverse),
            (multipliers_in, multipliers),
            (viscosity_in, viscosity),
        ],
        semaphores,
    )
    face = cells * cells
    on_x, on_y, on_z = face_ends(base[...], pick_matrix(cells, True), cells, True)
    ends_out[...] = jnp.concatenate([on_x, on_y, on_z, jnp.zeros((7, face), jnp.float32)], axis=0)
    for copy in copies:
        copy.wait()
    count = primal_index.shape[1]
    group, _, place, _ = decode(primal_index[...], cells)
    choose_out[...] = jnp.concatenate(
        [one_hot(iota((3 * cells, count), 0) == place), one_hot(iota((16, count), 0) == group)], axis=0
    )
    _, spot, _, lane = decode(column_of(primal_index[...]), cells)
    at = iota((count, face), 1)
    spots_out[...] = jnp.concatenate([jnp.where(at == lane, 1.0, 0.0), jnp.where(at == spot, 1.0, 0.0)], axis=1)
    blank = jnp.zeros((count, LANES - count), jnp.float32)
    for q in range(region_out.shape[0]):
        region_out[q] = jnp.concatenate([region_inverse[0, :, q * count : (q + 1) * count], blank], axis=1)
    through_out[...] = jnp.dot(
        coarse_map[0], global_inverse[...], precision=lax.Precision.HIGHEST, preferred_element_type=jnp.float32
    )
    global_out[...] = jnp.concatenate(parts_of(global_inverse[...], 2), axis=1)


def after_kernel(
    cells,
    sizes,
    count,
    received,
    base,
    ends,
    after_x,
    after_y,
    after_z,
    upper,
    spots,
    choose,
    region_blocks,
    through,
    global_parts,
    direction,
    multipliers,
    residual,
    viscosity,
    multipliers_out,
    residual_out,
    velocity_out,
    pressure_out,
):
    face = cells * cells
    n_region, n_sub = sizes
    half = n_sub // 2
    columns = through.shape[1]
    me_region = lax.axis_index("region")
    everything = jnp.sum(received[...], axis=0)
    totals = [everything[half + 1 + i : half + 2 + i] for i in range(columns // LANES)]
    total = jnp.concatenate(totals, axis=1)
    added = jnp.zeros((count, LANES), jnp.float32)
    for i, part in enumerate(totals):
        added = added + through[:, i * LANES : (i + 1) * LANES] * part
    for q in range(n_sub):
        added = added + region_blocks[q] * received[me_region * n_sub + q, half : half + 1, :]
    lifted = jnp.sum(added, axis=1, keepdims=True)
    added = choice_times(choose[...], lifted * spots[...])
    velocity = base[...] + added[: 3 * cells, :face]
    upper_faces = ends[:9] + added[3 * cells : 3 * cells + 9, face:]
    for c in range(3):
        velocity_out[0, c] = velocity[c * cells : (c + 1) * cells]
    after = [after_x[...], after_y[...], after_z[...]]
    ahead = jnp.concatenate([spread(after[1][1:2], cells), spread(after[2][2:3], cells)], axis=1)
    ahead = times_choice(ahead, upper[...])
    where_x, where_y, where_z = positions(cells, cells)
    end = cells - 1
    field_x, field_y, field_z = [velocity[c * cells : (c + 1) * cells] for c in range(3)]
    step_x = jnp.where(where_x == end, jnp.broadcast_to(after[0][0:1], (cells, face)), shift(field_x, -1, 0))
    step_y = jnp.where(where_y == end, 0.0, shift(field_y, -cells, 1))
    step_z = jnp.where(where_z == end, 0.0, shift(field_z, -1, 1))
    step = (step_x - field_x) + (step_y - field_y) + (step_z - field_z) + ahead
    pressure_out[0] = -viscosity[0] * step
    piece = total.astype(jnp.bfloat16).astype(jnp.float32)
    row = iota((16, columns), 0)
    parts = jnp.where(row == 0, piece, jnp.where(row == 1, total - piece, 0.0)).astype(jnp.bfloat16)
    top = jnp.dot(parts, global_parts[...], preferred_element_type=jnp.float32)
    top = top[0:1, :columns] + top[1:2, :columns] + top[0:1, columns:]
    lines = received[:, half, :].reshape(n_region, n_sub, LANES)
    quadratic = jnp.zeros((n_region, n_sub, LANES), jnp.float32)
    for k in range(half):
        products = received[:, k, :].reshape(n_region, n_sub, LANES)
        quadratic = quadratic + products * pltpu.roll(lines, n_sub - 1 - k, 1)
    own_line = everything[half : half + 1]
    lane = iota((1, LANES), 1)
    quadratic = jnp.sum(quadratic.reshape(n_region * n_sub, LANES), axis=0, keepdims=True)
    curvature = quadratic + jnp.where(lane == count, own_line, 0.0)
    for i in range(columns // LANES):
        curvature = curvature + totals[i] * top[:, i * LANES : (i + 1) * LANES]
    curvature = jnp.sum(curvature, axis=1, keepdims=True)
    squares = jnp.sum(jnp.where(lane == count + 1, own_line, 0.0), axis=1, keepdims=True)
    alpha = squares / curvature
    for d in range(3):
        jump = upper_faces[3 * d : 3 * d + 3] - after[d]
        for c in range(3):
            residual_out[3 * d + c] = residual[3 * d + c] - alpha * jump[c : c + 1]
            multipliers_out[3 * d + c] = multipliers[3 * d + c] + alpha * direction[3 * d + c]


def body(
    sizes,
    multipliers,
    direction,
    residual,
    reaction,
    viscosity,
    primal_index,
    region_inverse,
    coarse_map,
    global_inverse,
):
    n_region, n_sub = sizes
    cells = reaction.shape[1]
    face = reaction.shape[2]
    count = primal_index.shape[1]
    columns = coarse_map.shape[2]
    height = -(-(n_sub // 2 + 1 + columns // LANES) // 8) * 8
    rows = 3 * cells
    shape = direction.shape
    lines = (9, 1, face)
    f32 = jnp.float32
    bf16 = jnp.bfloat16
    vmem = pl.BlockSpec(memory_space=pltpu.VMEM)
    hbm = pl.BlockSpec(memory_space=pltpu.HBM)

    def like(shape, kind=f32):
        return jax.ShapeDtypeStruct(shape, kind)

    def call(kernel, out_shape, operands, in_hbm=(), scratch=()):
        return pl.pallas_call(
            kernel,
            out_shape=out_shape,
            in_specs=[vmem] * len(operands) + [hbm] * len(in_hbm),
            out_specs=[vmem] * len(out_shape),
            scratch_shapes=[pltpu.VMEM(x.shape, x.dtype) for x in scratch]
            + ([pltpu.SemaphoreType.DMA((len(in_hbm),))] if in_hbm else []),
            compiler_params=pltpu.CompilerParams(vmem_limit_bytes=32 * 1024 * 1024),
        )(*operands, *[pltpu.with_memory_space_constraint(x, pltpu.HBM) for x in in_hbm])

    below_x = shifted_2(direction, "region", 1).reshape(lines)
    below_y = shifted_2(direction, "sub", DOM_Z).reshape(lines)
    below_z = shifted_2(direction, "sub", 1).reshape(lines)
    multipliers, direction, residual = [x.reshape(lines) for x in (multipliers, direction, residual)]
    direction, residual, source, front, inverses, lower, upper, pick = call(
        functools.partial(before_kernel, cells, sizes),
        [
            like(lines),
            like(lines),
            like((rows, face)),
            like((height, LANES)),
            like((2 * LEVELS, cells, face)),
            like((2 * face, face), bf16),
            like((2 * face, face), bf16),
            like((face, 2 * face), bf16),
        ],
        [],
        [direction, residual, reaction, primal_index, region_inverse, coarse_map],
        [reaction, primal_index, region_inverse, coarse_map],
    )
    base, sent = call(
        functools.partial(solve_kernel, cells, sizes, count),
        [like((rows, face)), like((n_region * n_sub, height, LANES))],
        [source, below_x, below_y, below_z, inverses, front, lower],
    )
    received = lax.all_to_all(sent, ("region", "sub"), 0, 0, tiled=True)
    lower_x, lower_y, lower_z = call(
        functools.partial(ends_kernel, cells), [like((3, face))] * 3, [base, pick]
    )
    after_x = shifted_2(lower_x, "region", -1)
    after_y = shifted_2(lower_y, "sub", -DOM_Z)
    after_z = shifted_2(lower_z, "sub", -1)
    multipliers, viscosity, ends, region_blocks, through, global_parts, spots, choose = call(
        functools.partial(between_kernel, cells),
        [
            like(lines),
            like(viscosity.shape),
            like((16, face)),
            like((n_sub, count, LANES)),
            like((count, columns)),
            like((columns, 2 * columns), bf16),
            like((count, 2 * face)),
            like((rows + 16, count), bf16),
        ],
        [base],
        [primal_index, region_inverse, coarse_map, global_inverse, multipliers, viscosity],
        [primal_index, region_inverse, coarse_map, global_inverse],
    )
    new_multipliers, new_residual, velocity, pressure = call(
        functools.partial(after_kernel, cells, sizes, count),
        [like(lines), like(lines), like((1, 3, cells, face)), like((1, cells, face))],
        [
            received,
            base,
            ends,
            after_x,
            after_y,
            after_z,
            upper,
            spots,
            choose,
            region_blocks,
            through,
            global_parts,
            direction,
            multipliers,
            residual,
            viscosity,
        ],
    )
    return new_multipliers.reshape(shape), new_residual.reshape(shape), velocity, pressure


def solution(mesh):
    sizes = (mesh.shape["region"], mesh.shape["sub"])
    whole = P(("region", "sub"))
    in_specs = (whole,) * 6 + (P("region", "sub"), whole, P())
    return jax.shard_map(
        functools.partial(body, sizes), mesh=mesh, in_specs=in_specs, out_specs=(whole,) * 4, check_vma=False
    )
```

```python
import functools

import jax
import jax.numpy as jnp
from jax import lax
from jax.experimental import pallas as pl
from jax.experimental.pallas import tpu as pltpu
from jax.sharding import PartitionSpec as P

DOM_Z = 4
LEVELS = 3
SWEEPS = 1
COARSE_SWEEPS = 8
VCYCLES = 2
LANES = 128

damping = 0.8


def shifted_2(x, axis, by):
    count = lax.axis_size(axis)
    return lax.ppermute(x, axis, [(i, (i + by) % count) for i in range(count)])


def iota(shape, dim):
    return lax.broadcasted_iota(jnp.int32, shape, dim)


def parts_of(x, count=3):
    result = []
    for step in range(count):
        piece = x.astype(jnp.bfloat16)
        result.append(piece)
        if step < count - 1:
            x = x - piece.astype(jnp.float32)
    return result


def times_choice(x, choice, count=2):
    rows = x.shape[0]
    stacked = jnp.concatenate(parts_of(x, count), axis=0)
    y = jnp.dot(stacked, choice, preferred_element_type=jnp.float32)
    return functools.reduce(lambda a, b: a + b, [y[i * rows : (i + 1) * rows] for i in range(count)])


def times_parts(x, both):
    rows = x.shape[0]
    width = both.shape[1] // 2
    y = jnp.dot(jnp.concatenate(parts_of(x, 2), axis=0), both, preferred_element_type=jnp.float32)
    return y[:rows, :width] + (y[rows:, :width] + y[:rows, width:])


def both_parts(w):
    return jnp.concatenate(parts_of(w, 2), axis=1)


def choice_times(choice, x, count=2):
    width = x.shape[1]
    stacked = jnp.concatenate(parts_of(x, count), axis=1)
    y = jnp.dot(choice, stacked, preferred_element_type=jnp.float32)
    return functools.reduce(lambda a, b: a + b, [y[:, i * width : (i + 1) * width] for i in range(count)])


def one_hot(condition):
    return jnp.where(condition, 1.0, 0.0).astype(jnp.bfloat16)


def decode(picked, cells):
    face = cells * cells
    zero = jnp.zeros_like(picked)
    one = zero + 1
    block = jnp.where(picked >= 3 * face, one, zero) + jnp.where(picked >= 6 * face, one, zero)
    rest = picked - 3 * face * block
    component = jnp.where(rest >= face, one, zero) + jnp.where(rest >= 2 * face, one, zero)
    spot = rest - face * component
    first = lax.div(spot, zero + cells)
    second = spot - first * cells
    end = cells - 1
    x = jnp.where(block == 0, end, first)
    y = jnp.where(block == 0, first, jnp.where(block == 1, end, second))
    z = jnp.where(block == 2, end, second)
    return 3 * block + component, spot, component * cells + x, y * cells + z


def faces_of(rows):
    return [jnp.concatenate([rows[3 * d + c] for c in range(3)], axis=0) for d in range(3)]


def spread(faces, cells):
    face = cells * cells
    here = lax.div(iota((cells, face), 1), jnp.full((cells, face), cells, jnp.int32)) == iota((cells, face), 0)
    rows = [jnp.where(here, jnp.broadcast_to(faces[c : c + 1], (cells, face)), 0.0) for c in range(faces.shape[0])]
    return jnp.concatenate(rows, axis=0)


def mask_sum(x, cells):
    face = cells * cells
    here = lax.div(iota((cells, face), 1), jnp.full((cells, face), cells, jnp.int32)) == iota((cells, face), 0)
    rows = [
        jnp.sum(jnp.where(here, x[c * cells : (c + 1) * cells], 0.0), axis=0, keepdims=True)
        for c in range(x.shape[0] // cells)
    ]
    return jnp.concatenate(rows, axis=0)


def place_matrix(cells, upper):
    face = cells * cells
    row = iota((face, face), 0)
    column = iota((face, face), 1)
    second = row & (cells - 1)
    end = cells - 1 if upper else 0
    return jnp.concatenate(
        [one_hot(column == second + end * cells), one_hot(column == second * cells + end)], axis=0
    )


def pick_matrix(cells, upper):
    face = cells * cells
    row = iota((face, face), 0)
    column = iota((face, face), 1)
    second = column & (cells - 1)
    end = cells - 1 if upper else 0
    return jnp.concatenate(
        [one_hot(row == second + end * cells), one_hot(row == second * cells + end)], axis=1
    )


def face_ends(field, pick, cells, upper):
    face = cells * cells
    at = cells - 1 if upper else 0
    ends = times_choice(field, pick)
    on_x = [field[c * cells + at : c * cells + at + 1] for c in range(3)]
    return jnp.concatenate(on_x, axis=0), mask_sum(ends[:, :face], cells), mask_sum(ends[:, face:], cells)


def column_of(line):
    count = line.shape[1]
    wide = jnp.broadcast_to(line.astype(jnp.float32), (count, count))
    diagonal = iota((count, count), 0) == iota((count, count), 1)
    return jnp.sum(jnp.where(diagonal, wide, 0.0), axis=1, keepdims=True).astype(jnp.int32)


def shift(field, by, dim):
    size = field.shape[dim]
    return pltpu.roll(field, by % size, dim)


def positions(rows, cells):
    shape = (rows, cells * cells)
    return (iota(shape, 0) & (cells - 1), *split_index(iota(shape, 1), cells, 2))


def bits(cells):
    return cells.bit_length() - 1


def split_index(flat, cells, dims):
    return [(flat >> (bits(cells) * (dims - 1 - i))) & (cells - 1) for i in range(dims)]


def gather_matrix(cells, columns_first):
    face, half = cells * cells, cells // 2
    shape = (half**3, face) if columns_first else (face, half**3)
    y, z = split_index(iota(shape, 1 if columns_first else 0), cells, 2)
    _, half_y, half_z = split_index(iota(shape, 0 if columns_first else 1), half, 3)
    return one_hot(((y >> 1) == half_y) & ((z >> 1) == half_z))


def coarsen_matrix(cells, columns_first):
    half = cells // 2
    shape = (half**3, cells**3) if columns_first else (cells**3, half**3)
    fine = split_index(iota(shape, 1 if columns_first else 0), cells, 3)
    coarse = split_index(iota(shape, 0 if columns_first else 1), half, 3)
    same = [(f >> 1) == c for f, c in zip(fine, coarse)]
    return one_hot(same[0] & same[1] & same[2])


def own_half(cells):
    half = cells // 2
    shape = (cells, half**3)
    return split_index(iota(shape, 1), half, 3)[0] == (iota(shape, 0) >> 1)


def plane_restrict(field, gather, cells, count):
    spread_out = times_choice(field, gather)
    here = own_half(cells)
    rows = [
        jnp.sum(jnp.where(here, spread_out[c * cells : (c + 1) * cells], 0.0), axis=0, keepdims=True)
        for c in range(count)
    ]
    return 0.125 * (rows[0] if count == 1 else jnp.concatenate(rows, axis=0))


def plane_prolong(coarse, scatter, cells, count):
    here = own_half(cells)
    wide = [
        jnp.where(here, jnp.broadcast_to(coarse[c : c + 1], (cells, coarse.shape[1])), 0.0) for c in range(count)
    ]
    return times_choice(jnp.concatenate(wide, axis=0), scatter)


def sweeps_matrix(scale, cells, weight):
    size = cells**3
    shape = (size, size)
    here = split_index(iota(shape, 0), cells, 3)
    there = split_index(iota(shape, 1), cells, 3)
    distance = functools.reduce(lambda a, b: a + b, [jnp.abs(a - b) for a, b in zip(here, there)])
    power = jnp.where(distance == 0, 1.0 - damping, 0.0) + jnp.where(distance == 1, weight * scale, 0.0)
    total = jnp.where(distance == 0, 1.0, 0.0) + power
    done = 2
    while done < COARSE_SWEEPS:
        power = times_parts(power, both_parts(power))
        total = total + times_parts(total, both_parts(power))
        done *= 2
    return total


def load(pairs, semaphores):
    copies = [pltpu.make_async_copy(a, b, semaphores.at[i]) for i, (a, b) in enumerate(pairs)]
    for copy in copies:
        copy.start()
    return copies


def before_kernel(
    cells,
    sizes,
    direction_in,
    residual_in,
    reaction_in,
    primal_index_in,
    region_inverse_in,
    coarse_map_in,
    direction,
    residual,
    source_out,
    front_out,
    inverse_out,
    lower_out,
    upper_out,
    pick_out,
    half_out,
    quarter_out,
    gather_out,
    scatter_out,
    coarsen_out,
    sweeps_out,
    reaction,
    primal_index,
    region_inverse,
    coarse_map,
    semaphores,
):
    copies = load(
        [
            (direction_in, direction),
            (reaction_in, reaction),
            (primal_index_in, primal_index),
            (residual_in, residual),
            (coarse_map_in, coarse_map),
            (region_inverse_in, region_inverse),
        ],
        semaphores,
    )
    face = cells * cells
    n_sub = sizes[1]
    lower_out[...] = place_matrix(cells, False)
    upper = place_matrix(cells, True)
    upper_out[...] = upper
    pick_out[...] = pick_matrix(cells, False)
    half = cells // 2
    gather = gather_matrix(cells, False)
    gather_out[...] = gather
    scatter_out[...] = gather_matrix(cells, True)
    coarsen = coarsen_matrix(half, False)
    coarsen_out[...] = coarsen
    for copy in copies:
        copy.wait()
    react = reaction[0]
    diagonal = react + 6.0
    inverse_out[0] = damping / diagonal
    inverse_out[1] = diagonal
    react = plane_restrict(react, gather, cells, 1)
    diagonal = react + 6.0 * 0.25
    half_out[0:1, :] = damping / diagonal
    half_out[1:2, :] = diagonal
    react = 0.125 * times_choice(jnp.broadcast_to(react, (8, half**3)), coarsen)[:1]
    scale = damping / (react + 6.0 * 0.0625)
    quarter_out[...] = 0.125 * scale
    sweeps = sweeps_matrix(scale, half // 2, 0.0625)
    sweeps_out[...] = both_parts(times_choice(sweeps, coarsen_matrix(half, True)))
    faces = faces_of(direction)
    row_x = iota((cells, face), 0)
    source = times_choice(jnp.concatenate([spread(faces[1], cells), spread(faces[2], cells)], axis=1), upper)
    own_x = jnp.concatenate(
        [jnp.where(row_x == cells - 1, jnp.broadcast_to(faces[0][c : c + 1], (cells, face)), 0.0) for c in range(3)],
        axis=0,
    )
    source_out[...] = source + own_x
    count = primal_index.shape[1]
    group, spot, _, _ = decode(column_of(primal_index[...]), cells)
    nine = jnp.concatenate(faces + [jnp.zeros((7, face), jnp.float32)], axis=0)
    gathered = choice_times(one_hot(iota((count, 16), 1) == group), nine)
    primal = jnp.sum(jnp.where(iota((count, face), 1) == spot, gathered, 0.0), axis=1, keepdims=True)
    share = jnp.sum(primal * coarse_map[0], axis=0, keepdims=True)
    product = jnp.sum(primal * region_inverse[0], axis=0, keepdims=True)
    lane = iota((1, LANES), 1)
    line = jnp.sum(
        jnp.where(iota((count, LANES), 0) == iota((count, LANES), 1), primal, 0.0), axis=0, keepdims=True
    )
    blank = jnp.zeros((1, LANES - count), jnp.float32)
    blocks = jnp.concatenate(
        [jnp.concatenate([product[:, q * count : (q + 1) * count], blank], axis=1) for q in range(n_sub)], axis=0
    )
    me_sub = lax.axis_index("sub")
    own = jnp.sum(jnp.where(iota(blocks.shape, 0) == me_sub, blocks * line, 0.0))
    blocks = pltpu.roll(blocks, n_sub - 1 - me_sub, 0)
    half = n_sub // 2
    twice = jnp.where(iota((half, LANES), 0) == (half - 1 if n_sub % 2 == 0 else half), 1.0, 2.0)
    squares = jnp.sum(residual[...] * residual[...])
    line = jnp.where(lane == count, own, jnp.where(lane == count + 1, squares, line))
    front_out[...] = jnp.zeros_like(front_out)
    front_out[:half, :] = blocks[:half] * twice
    front_out[half : half + 1, :] = line
    for i in range(share.shape[1] // LANES):
        front_out[half + 1 + i : half + 2 + i, :] = share[:, i * LANES : (i + 1) * LANES]


def solve_kernel(
    cells,
    sizes,
    count,
    source_own,
    from_x,
    from_y,
    from_z,
    inverses,
    front,
    lower,
    halves,
    quarter,
    gather,
    scatter,
    coarsen,
    sweeps,
    base_out,
    send_out,
):
    face = cells * cells
    rows = 3 * cells
    below_x, below_y, below_z = [faces_of(ref)[d] for d, ref in enumerate((from_x, from_y, from_z))]
    n_region, n_sub = sizes
    row_x = iota((cells, face), 0)
    source = source_own[...] - times_choice(
        jnp.concatenate([spread(below_y, cells), spread(below_z, cells)], axis=1), lower[...]
    )
    source = source - jnp.concatenate(
        [jnp.where(row_x == 0, jnp.broadcast_to(below_x[c : c + 1], (cells, face)), 0.0) for c in range(3)],
        axis=0,
    )
    where_x, where_y, where_z = positions(rows, cells)
    last = cells - 1

    def tall(x):
        return jnp.concatenate([x] * 3, axis=0)

    inverse = tall(inverses[0])
    diagonal = tall(inverses[1])

    def beside(field):
        total = jnp.where(where_x < last, shift(field, -1, 0), 0.0)
        total = total + jnp.where(where_x > 0, shift(field, 1, 0), 0.0)
        total = total + jnp.where(where_y < last, shift(field, -cells, 1), 0.0)
        total = total + jnp.where(where_y > 0, shift(field, cells, 1), 0.0)
        total = total + jnp.where(where_z < last, shift(field, -1, 1), 0.0)
        return total + jnp.where(where_z > 0, shift(field, 1, 1), 0.0)

    half = cells // 2
    lane = iota((8, half**3), 1)
    half_at = split_index(lane, half, 3)
    half_inverse = halves[0:1, :]
    half_diagonal = halves[1:2, :]

    def half_beside(field):
        total = jnp.zeros_like(field)
        for position, reach in zip(half_at, (half * half, half, 1)):
            total = total + jnp.where(position < half - 1, shift(field, -reach, 1), 0.0)
            total = total + jnp.where(position > 0, shift(field, reach, 1), 0.0)
        return total

    def half_cycle(right):
        field = half_inverse * right
        remain = right - half_diagonal * field + 0.25 * half_beside(field)
        remain = times_choice(remain, coarsen[...])
        field = field + times_parts(remain * quarter[...], sweeps[...])
        return (1.0 - damping) * field + half_inverse * (right + 0.25 * half_beside(field))

    def relax(field, right):
        return (1.0 - damping) * field + inverse * (right + beside(field))

    field = inverse * source
    for cycle in range(VCYCLES):
        if cycle:
            field = relax(field, source)
        remain = source - diagonal * field + beside(field)
        right = plane_restrict(remain, gather[...], cells, 3)
        right = jnp.concatenate([right, jnp.zeros((5, half**3), jnp.float32)], axis=0)
        field = field + plane_prolong(half_cycle(right), scatter[...], cells, 3)
        field = relax(field, source)
    base_out[...] = field
    energy = jnp.sum(jnp.sum(source * field, axis=0, keepdims=True), axis=1, keepdims=True)
    message = front[...]
    at = (iota(message.shape, 0) == sizes[1] // 2) & (iota(message.shape, 1) == count)
    message = message + jnp.where(at, energy, 0.0)
    for device in range(sizes[0] * sizes[1]):
        send_out[device] = message


def ends_kernel(cells, base, pick, lower_x, lower_y, lower_z):
    lower_x[...], lower_y[...], lower_z[...] = face_ends(base[...], pick[...], cells, False)


def between_kernel(
    cells,
    base,
    primal_index,
    region_inverse,
    coarse_map,
    global_inverse,
    ends_out,
    region_out,
    through_out,
    global_out,
    spots_out,
    choose_out,
):
    face = cells * cells
    on_x, on_y, on_z = face_ends(base[...], pick_matrix(cells, True), cells, True)
    ends_out[...] = jnp.concatenate([on_x, on_y, on_z, jnp.zeros((7, face), jnp.float32)], axis=0)
    count = primal_index.shape[1]
    group, _, place, _ = decode(primal_index[...], cells)
    choose_out[...] = jnp.concatenate(
        [one_hot(iota((3 * cells, count), 0) == place), one_hot(iota((16, count), 0) == group)], axis=0
    )
    _, spot, _, lane = decode(column_of(primal_index[...]), cells)
    at = iota((count, face), 1)
    spots_out[...] = jnp.concatenate([jnp.where(at == lane, 1.0, 0.0), jnp.where(at == spot, 1.0, 0.0)], axis=1)
    blank = jnp.zeros((count, LANES - count), jnp.float32)
    for q in range(region_out.shape[0]):
        region_out[q] = jnp.concatenate([region_inverse[0, :, q * count : (q + 1) * count], blank], axis=1)
    both = both_parts(global_inverse[...])
    global_out[...] = both
    through_out[...] = times_parts(coarse_map[0], both)


def after_kernel(
    cells,
    sizes,
    count,
    received,
    base,
    ends,
    after_x,
    after_y,
    after_z,
    upper,
    spots,
    choose,
    region_blocks,
    through,
    global_parts,
    direction,
    multipliers,
    residual,
    viscosity,
    multipliers_out,
    residual_out,
    velocity_out,
    pressure_out,
):
    face = cells * cells
    n_region, n_sub = sizes
    half = n_sub // 2
    columns = through.shape[1]
    me_region = lax.axis_index("region")
    everything = jnp.sum(received[...], axis=0)
    totals = [everything[half + 1 + i : half + 2 + i] for i in range(columns // LANES)]
    total = jnp.concatenate(totals, axis=1)
    added = jnp.zeros((count, LANES), jnp.float32)
    for i, part in enumerate(totals):
        added = added + through[:, i * LANES : (i + 1) * LANES] * part
    for q in range(n_sub):
        added = added + region_blocks[q] * received[me_region * n_sub + q, half : half + 1, :]
    lifted = jnp.sum(added, axis=1, keepdims=True)
    added = choice_times(choose[...], lifted * spots[...])
    velocity = base[...] + added[: 3 * cells, :face]
    upper_faces = ends[:9] + added[3 * cells : 3 * cells + 9, face:]
    for c in range(3):
        velocity_out[0, c] = velocity[c * cells : (c + 1) * cells]
    after = [after_x[...], after_y[...], after_z[...]]
    ahead = jnp.concatenate([spread(after[1][1:2], cells), spread(after[2][2:3], cells)], axis=1)
    ahead = times_choice(ahead, upper[...])
    where_x, where_y, where_z = positions(cells, cells)
    end = cells - 1
    field_x, field_y, field_z = [velocity[c * cells : (c + 1) * cells] for c in range(3)]
    step_x = jnp.where(where_x == end, jnp.broadcast_to(after[0][0:1], (cells, face)), shift(field_x, -1, 0))
    step_y = jnp.where(where_y == end, 0.0, shift(field_y, -cells, 1))
    step_z = jnp.where(where_z == end, 0.0, shift(field_z, -1, 1))
    step = (step_x - field_x) + (step_y - field_y) + (step_z - field_z) + ahead
    pressure_out[0] = -viscosity[0] * step
    piece = total.astype(jnp.bfloat16).astype(jnp.float32)
    row = iota((16, columns), 0)
    parts = jnp.where(row == 0, piece, jnp.where(row == 1, total - piece, 0.0)).astype(jnp.bfloat16)
    top = jnp.dot(parts, global_parts[...], preferred_element_type=jnp.float32)
    top = top[0:1, :columns] + top[1:2, :columns] + top[0:1, columns:]
    lines = received[:, half, :].reshape(n_region, n_sub, LANES)
    quadratic = jnp.zeros((n_region, n_sub, LANES), jnp.float32)
    for k in range(half):
        products = received[:, k, :].reshape(n_region, n_sub, LANES)
        quadratic = quadratic + products * pltpu.roll(lines, n_sub - 1 - k, 1)
    own_line = everything[half : half + 1]
    lane = iota((1, LANES), 1)
    quadratic = jnp.sum(quadratic.reshape(n_region * n_sub, LANES), axis=0, keepdims=True)
    curvature = quadratic + jnp.where(lane == count, own_line, 0.0)
    for i in range(columns // LANES):
        curvature = curvature + totals[i] * top[:, i * LANES : (i + 1) * LANES]
    curvature = jnp.sum(curvature, axis=1, keepdims=True)
    squares = jnp.sum(jnp.where(lane == count + 1, own_line, 0.0), axis=1, keepdims=True)
    alpha = squares / curvature
    for d in range(3):
        jump = upper_faces[3 * d : 3 * d + 3] - after[d]
        for c in range(3):
            residual_out[3 * d + c] = residual[3 * d + c] - alpha * jump[c : c + 1]
            multipliers_out[3 * d + c] = multipliers[3 * d + c] + alpha * direction[3 * d + c]


def body(
    sizes,
    multipliers,
    direction,
    residual,
    reaction,
    viscosity,
    primal_index,
    region_inverse,
    coarse_map,
    global_inverse,
):
    n_region, n_sub = sizes
    cells = reaction.shape[1]
    face = reaction.shape[2]
    count = primal_index.shape[1]
    columns = coarse_map.shape[2]
    height = -(-(n_sub // 2 + 1 + columns // LANES) // 8) * 8
    rows = 3 * cells
    shape = direction.shape
    lines = (9, 1, face)
    f32 = jnp.float32
    bf16 = jnp.bfloat16
    vmem = pl.BlockSpec(memory_space=pltpu.VMEM)
    hbm = pl.BlockSpec(memory_space=pltpu.HBM)

    def like(shape, kind=f32):
        return jax.ShapeDtypeStruct(shape, kind)

    def call(kernel, out_shape, operands, in_hbm=(), scratch=()):
        return pl.pallas_call(
            kernel,
            out_shape=out_shape,
            in_specs=[vmem] * len(operands) + [hbm] * len(in_hbm),
            out_specs=[vmem] * len(out_shape),
            scratch_shapes=[pltpu.VMEM(x.shape, x.dtype) for x in scratch]
            + ([pltpu.SemaphoreType.DMA((len(in_hbm),))] if in_hbm else []),
            compiler_params=pltpu.CompilerParams(vmem_limit_bytes=32 * 1024 * 1024),
        )(*operands, *[pltpu.with_memory_space_constraint(x, pltpu.HBM) for x in in_hbm])

    below_x = shifted_2(direction, "region", 1).reshape(lines)
    below_y = shifted_2(direction, "sub", DOM_Z).reshape(lines)
    below_z = shifted_2(direction, "sub", 1).reshape(lines)
    multipliers, direction, residual = [x.reshape(lines) for x in (multipliers, direction, residual)]
    half_cells = (cells // 2) ** 3
    (
        direction, residual, source, front, inverses, lower, upper, pick, halves, quarter, gather, scatter, coarsen, sweeps
    ) = call(
        functools.partial(before_kernel, cells, sizes),
        [
            like(lines),
            like(lines),
            like((rows, face)),
            like((height, LANES)),
            like((2, cells, face)),
            like((2 * face, face), bf16),
            like((2 * face, face), bf16),
            like((face, 2 * face), bf16),
            like((2, half_cells)),
            like((1, half_cells // 8)),
            like((face, half_cells), bf16),
            like((half_cells, face), bf16),
            like((half_cells, half_cells // 8), bf16),
            like((half_cells // 8, 2 * half_cells), bf16),
        ],
        [],
        [direction, residual, reaction, primal_index, region_inverse, coarse_map],
        [reaction, primal_index, region_inverse, coarse_map],
    )
    base, sent = call(
        functools.partial(solve_kernel, cells, sizes, count),
        [like((rows, face)), like((n_region * n_sub, height, LANES))],
        [source, below_x, below_y, below_z, inverses, front, lower, halves, quarter, gather, scatter, coarsen, sweeps],
    )
    received = lax.all_to_all(sent, ("region", "sub"), 0, 0, tiled=True)
    lower_x, lower_y, lower_z = call(
        functools.partial(ends_kernel, cells), [like((3, face))] * 3, [base, pick]
    )
    after_x = shifted_2(lower_x, "region", -1)
    after_y = shifted_2(lower_y, "sub", -DOM_Z)
    after_z = shifted_2(lower_z, "sub", -1)
    ends, region_blocks, through, global_parts, spots, choose = call(
        functools.partial(between_kernel, cells),
        [
            like((16, face)),
            like((n_sub, count, LANES)),
            like((count, columns)),
            like((columns, 2 * columns), bf16),
            like((count, 2 * face)),
            like((rows + 16, count), bf16),
        ],
        [base, primal_index, region_inverse, coarse_map, global_inverse],
    )
    new_multipliers, new_residual, velocity, pressure = call(
        functools.partial(after_kernel, cells, sizes, count),
        [like(lines), like(lines), like((1, 3, cells, face)), like((1, cells, face))],
        [
            received,
            base,
            ends,
            after_x,
            after_y,
            after_z,
            upper,
            spots,
            choose,
            region_blocks,
            through,
            global_parts,
            direction,
            multipliers,
            residual,
            viscosity,
        ],
    )
    return new_multipliers.reshape(shape), new_residual.reshape(shape), velocity, pressure


def solution(mesh):
    sizes = (mesh.shape["region"], mesh.shape["sub"])
    whole = P(("region", "sub"))
    in_specs = (whole,) * 6 + (P("region", "sub"), whole, P())
    return jax.shard_map(
        functools.partial(body, sizes), mesh=mesh, in_specs=in_specs, out_specs=(whole,) * 4, check_vma=False
    )
```

```python
import functools

import jax
import jax.numpy as jnp
from jax import lax
from jax.experimental import pallas as pl
from jax.experimental.pallas import tpu as pltpu
from jax.sharding import PartitionSpec as P

DOM_Z = 4
LEVELS = 3
SWEEPS = 1
COARSE_SWEEPS = 8
VCYCLES = 2
LANES = 128

damping = 0.8


def shifted_2(x, axis, by):
    count = lax.axis_size(axis)
    return lax.ppermute(x, axis, [(i, (i + by) % count) for i in range(count)])


def iota(shape, dim):
    return lax.broadcasted_iota(jnp.int32, shape, dim)


def parts_of(x, count=3):
    result = []
    for step in range(count):
        piece = x.astype(jnp.bfloat16)
        result.append(piece)
        if step < count - 1:
            x = x - piece.astype(jnp.float32)
    return result


def times_choice(x, choice, count=2):
    rows = x.shape[0]
    stacked = jnp.concatenate(parts_of(x, count), axis=0)
    y = jnp.dot(stacked, choice, preferred_element_type=jnp.float32)
    return functools.reduce(lambda a, b: a + b, [y[i * rows : (i + 1) * rows] for i in range(count)])


def times_parts(x, both):
    rows = x.shape[0]
    width = both.shape[1] // 2
    y = jnp.dot(jnp.concatenate(parts_of(x, 2), axis=0), both, preferred_element_type=jnp.float32)
    return y[:rows, :width] + (y[rows:, :width] + y[:rows, width:])


def both_parts(w):
    return jnp.concatenate(parts_of(w, 2), axis=1)


def choice_times(choice, x, count=2):
    width = x.shape[1]
    stacked = jnp.concatenate(parts_of(x, count), axis=1)
    y = jnp.dot(choice, stacked, preferred_element_type=jnp.float32)
    return functools.reduce(lambda a, b: a + b, [y[:, i * width : (i + 1) * width] for i in range(count)])


def one_hot(condition):
    return jnp.where(condition, 1.0, 0.0).astype(jnp.bfloat16)


def decode(picked, cells):
    face = cells * cells
    zero = jnp.zeros_like(picked)
    one = zero + 1
    block = jnp.where(picked >= 3 * face, one, zero) + jnp.where(picked >= 6 * face, one, zero)
    rest = picked - 3 * face * block
    component = jnp.where(rest >= face, one, zero) + jnp.where(rest >= 2 * face, one, zero)
    spot = rest - face * component
    first = lax.div(spot, zero + cells)
    second = spot - first * cells
    end = cells - 1
    x = jnp.where(block == 0, end, first)
    y = jnp.where(block == 0, first, jnp.where(block == 1, end, second))
    z = jnp.where(block == 2, end, second)
    return 3 * block + component, spot, component * cells + x, y * cells + z


def faces_of(rows):
    return [jnp.concatenate([rows[3 * d + c] for c in range(3)], axis=0) for d in range(3)]


def spread(faces, cells):
    face = cells * cells
    here = lax.div(iota((cells, face), 1), jnp.full((cells, face), cells, jnp.int32)) == iota((cells, face), 0)
    rows = [jnp.where(here, jnp.broadcast_to(faces[c : c + 1], (cells, face)), 0.0) for c in range(faces.shape[0])]
    return jnp.concatenate(rows, axis=0)


def mask_sum(x, cells):
    face = cells * cells
    here = lax.div(iota((cells, face), 1), jnp.full((cells, face), cells, jnp.int32)) == iota((cells, face), 0)
    rows = [
        jnp.sum(jnp.where(here, x[c * cells : (c + 1) * cells], 0.0), axis=0, keepdims=True)
        for c in range(x.shape[0] // cells)
    ]
    return jnp.concatenate(rows, axis=0)


def place_matrix(cells, upper):
    row = iota((cells, cells * cells), 0)
    column = iota((cells, cells * cells), 1)
    end = cells - 1 if upper else 0
    on_y = one_hot(column == row + end * cells)
    on_z = one_hot(column == row * cells + end)
    return jnp.concatenate([on_y] * cells + [on_z] * cells, axis=0)


def pick_matrix(cells, upper):
    face = cells * cells
    row = iota((face, LANES), 0)
    second = iota((face, LANES), 1) & (cells - 1)
    end = cells - 1 if upper else 0
    on_y = one_hot(row == second + end * cells)
    on_z = one_hot(row == second * cells + end)
    return jnp.concatenate([on_y] * (face // LANES) + [on_z] * (face // LANES), axis=1)


def face_ends(field, pick, cells, upper):
    face = cells * cells
    at = cells - 1 if upper else 0
    ends = times_choice(field, pick)
    on_x = [field[c * cells + at : c * cells + at + 1] for c in range(3)]
    return jnp.concatenate(on_x, axis=0), mask_sum(ends[:, :face], cells), mask_sum(ends[:, face:], cells)


def column_of(line):
    count = line.shape[1]
    wide = jnp.broadcast_to(line.astype(jnp.float32), (count, count))
    diagonal = iota((count, count), 0) == iota((count, count), 1)
    return jnp.sum(jnp.where(diagonal, wide, 0.0), axis=1, keepdims=True).astype(jnp.int32)


def shift(field, by, dim):
    size = field.shape[dim]
    return pltpu.roll(field, by % size, dim)


def positions(rows, cells):
    shape = (rows, cells * cells)
    return (iota(shape, 0) & (cells - 1), *split_index(iota(shape, 1), cells, 2))


def bits(cells):
    return cells.bit_length() - 1


def split_index(flat, cells, dims):
    return [(flat >> (bits(cells) * (dims - 1 - i))) & (cells - 1) for i in range(dims)]


def gather_matrix(cells, steps=1):
    size = cells >> steps
    width = min(size**3, LANES)
    shape = (cells * cells, width)
    y, z = split_index(iota(shape, 0), cells, 2)
    _, far_y, far_z = split_index(iota(shape, 1), size, 3)
    return jnp.concatenate([one_hot(((y >> steps) == far_y) & ((z >> steps) == far_z))] * (size**3 // width), axis=1)


def scatter_matrix(cells):
    half = cells // 2
    shape = (half * half, cells * cells)
    y, z = split_index(iota(shape, 1), cells, 2)
    half_y, half_z = split_index(iota(shape, 0), half, 2)
    return jnp.concatenate([one_hot(((y >> 1) == half_y) & ((z >> 1) == half_z))] * half, axis=0)


def block_matrices(cells, blocks_first):
    half = cells // 2
    shape = (half**3, cells**3) if blocks_first else (cells**3, half**3)
    fine = split_index(iota(shape, 1 if blocks_first else 0), cells, 3)
    block = split_index(iota(shape, 0 if blocks_first else 1), half, 3)
    inside = [(f >> 1) == b for f, b in zip(fine, block)]
    nearby = [(f >> 1) + 2 * (f & 1) - 1 == b for f, b in zip(fine, block)]
    same = inside[0] & inside[1] & inside[2]
    near = (
        (nearby[0] & inside[1] & inside[2])
        | (inside[0] & nearby[1] & inside[2])
        | (inside[0] & inside[1] & nearby[2])
    )
    return one_hot(same), jnp.where(same, 3.0, jnp.where(near, 1.0, 0.0)).astype(jnp.bfloat16)


def own_part(cells, steps=1):
    size = cells >> steps
    shape = (cells, size**3)
    return split_index(iota(shape, 1), size, 3)[0] == (iota(shape, 0) >> steps)


def plane_restrict(field, gather, cells, count, steps=1):
    spread_out = times_choice(field, gather)
    here = own_part(cells, steps)
    rows = [
        jnp.sum(jnp.where(here, spread_out[c * cells : (c + 1) * cells], 0.0), axis=0, keepdims=True)
        for c in range(count)
    ]
    return 0.125**steps * (rows[0] if count == 1 else jnp.concatenate(rows, axis=0))


def plane_prolong(coarse, scatter, cells, count):
    here = own_part(cells)
    wide = [
        jnp.where(here, jnp.broadcast_to(coarse[c : c + 1], (cells, coarse.shape[1])), 0.0) for c in range(count)
    ]
    return times_choice(jnp.concatenate(wide, axis=0), scatter)


def sweep_power(scale, cells, weight):
    size = cells**3
    shape = (size, size)
    here = split_index(iota(shape, 0), cells, 3)
    there = split_index(iota(shape, 1), cells, 3)
    distance = functools.reduce(lambda a, b: a + b, [jnp.abs(a - b) for a, b in zip(here, there)])
    one = jnp.where(distance == 0, 1.0, 0.0)
    return (1.0 - damping) * one + jnp.where(distance == 1, weight * scale, 0.0), one


def square(power):
    return times_parts(power, both_parts(power))


def powers_sum(total, power):
    done = 2
    while done < COARSE_SWEEPS:
        total = total + times_parts(total, both_parts(power))
        done *= 2
        if done < COARSE_SWEEPS:
            power = square(power)
    return total


def load(pairs, semaphores):
    copies = [pltpu.make_async_copy(a, b, semaphores.at[i]) for i, (a, b) in enumerate(pairs)]
    for copy in copies:
        copy.start()
    return copies


def before_kernel(
    cells,
    sizes,
    direction_in,
    residual_in,
    reaction_in,
    primal_index_in,
    region_inverse_in,
    coarse_map_in,
    direction,
    residual,
    source_out,
    front_out,
    inverse_out,
    lower_out,
    upper_out,
    pick_out,
    half_out,
    quarter_out,
    gather_out,
    scatter_out,
    coarsen_out,
    sweeps_out,
    reaction,
    primal_index,
    region_inverse,
    coarse_map,
    semaphores,
):
    copies = load(
        [
            (direction_in, direction),
            (reaction_in, reaction),
            (primal_index_in, primal_index),
            (residual_in, residual),
            (coarse_map_in, coarse_map),
            (region_inverse_in, region_inverse),
        ],
        semaphores,
    )
    face = cells * cells
    n_sub = sizes[1]
    lower_out[...] = place_matrix(cells, False)
    upper = place_matrix(cells, True)
    upper_out[...] = upper
    pick_out[...] = pick_matrix(cells, False)
    half = cells // 2
    gather = gather_matrix(cells)
    gather_out[...] = gather
    quarter_gather = gather_matrix(cells, 2)
    scatter_out[...] = scatter_matrix(cells)
    coarsen, coarsen_near = block_matrices(half, False)
    coarsen_out[...] = jnp.concatenate([coarsen, coarsen_near], axis=0)
    refine = jnp.concatenate(block_matrices(half, True), axis=1)
    for copy in copies[:3]:
        copy.wait()
    react = reaction[0]
    scale = damping / (plane_restrict(react, quarter_gather, cells, 1, 2) + 6.0 * 0.0625)
    quarter_out[...] = 0.125 * scale
    power, one = sweep_power(scale, half // 2, 0.0625)
    second_power = square(power)
    diagonal = react + 6.0
    inverse_out[0] = damping / diagonal
    inverse_out[1] = diagonal
    half_scale = damping / (plane_restrict(react, gather, cells, 1) + 6.0 * 0.25)
    half_out[...] = half_scale
    faces = faces_of(direction)
    count = primal_index.shape[1]
    group, spot, _, _ = decode(column_of(primal_index[...]), cells)
    nine = jnp.concatenate(faces + [jnp.zeros((7, face), jnp.float32)], axis=0)
    gathered = choice_times(one_hot(iota((count, 16), 1) == group), nine)
    primal = jnp.sum(jnp.where(iota((count, face), 1) == spot, gathered, 0.0), axis=1, keepdims=True)
    lane = iota((1, LANES), 1)
    line = jnp.sum(
        jnp.where(iota((count, LANES), 0) == iota((count, LANES), 1), primal, 0.0), axis=0, keepdims=True
    )
    for copy in copies[3:]:
        copy.wait()
    refined = times_choice(powers_sum(one + power, second_power), refine)
    sweeps_out[...] = both_parts(
        (1.0 - damping) * refined[:, : half**3] + 0.25 * half_scale * refined[:, half**3 :]
    )
    row_x = iota((cells, face), 0)
    source = times_choice(jnp.concatenate([spread(faces[1], cells), spread(faces[2], cells)], axis=1), upper)
    own_x = jnp.concatenate(
        [jnp.where(row_x == cells - 1, jnp.broadcast_to(faces[0][c : c + 1], (cells, face)), 0.0) for c in range(3)],
        axis=0,
    )
    source_out[...] = source + own_x
    share = jnp.sum(primal * coarse_map[0], axis=0, keepdims=True)
    product = jnp.sum(primal * region_inverse[0], axis=0, keepdims=True)
    blank = jnp.zeros((1, LANES - count), jnp.float32)
    blocks = jnp.concatenate(
        [jnp.concatenate([product[:, q * count : (q + 1) * count], blank], axis=1) for q in range(n_sub)], axis=0
    )
    me_sub = lax.axis_index("sub")
    own = jnp.sum(jnp.where(iota(blocks.shape, 0) == me_sub, blocks, 0.0), axis=0, keepdims=True)
    own = jnp.sum(own * line, axis=1, keepdims=True)
    blocks = pltpu.roll(blocks, n_sub - 1 - me_sub, 0)
    opposite = n_sub // 2
    twice = jnp.where(iota((opposite, LANES), 0) == (opposite - 1 if n_sub % 2 == 0 else opposite), 1.0, 2.0)
    squares = jnp.concatenate([residual[i] for i in range(9)], axis=0)
    squares = jnp.sum(jnp.sum(squares * squares, axis=0, keepdims=True), axis=1, keepdims=True)
    line = jnp.where(lane == count, own, jnp.where(lane == count + 1, squares, line))
    front_out[...] = jnp.zeros_like(front_out)
    front_out[:opposite, :] = blocks[:opposite] * twice
    front_out[opposite : opposite + 1, :] = line
    for i in range(share.shape[1] // LANES):
        front_out[opposite + 1 + i : opposite + 2 + i, :] = share[:, i * LANES : (i + 1) * LANES]


def solve_kernel(
    cells,
    sizes,
    count,
    source_own,
    from_x,
    from_y,
    from_z,
    inverses,
    front,
    lower,
    halves,
    quarter,
    gather,
    scatter,
    coarsen,
    sweeps,
    base_out,
    send_out,
):
    face = cells * cells
    rows = 3 * cells
    below_x, below_y, below_z = [faces_of(ref)[d] for d, ref in enumerate((from_x, from_y, from_z))]
    n_region, n_sub = sizes
    row_x = iota((cells, face), 0)
    source = source_own[...] - times_choice(
        jnp.concatenate([spread(below_y, cells), spread(below_z, cells)], axis=1), lower[...]
    )
    source = source - jnp.concatenate(
        [jnp.where(row_x == 0, jnp.broadcast_to(below_x[c : c + 1], (cells, face)), 0.0) for c in range(3)],
        axis=0,
    )
    where_x, where_y, where_z = positions(rows, cells)
    last = cells - 1

    def tall(x):
        return jnp.concatenate([x] * 3, axis=0)

    inverse = tall(inverses[0])
    diagonal = tall(inverses[1])

    def beside(field):
        total = jnp.where(where_x < last, shift(field, -1, 0), 0.0)
        total = total + jnp.where(where_x > 0, shift(field, 1, 0), 0.0)
        total = total + jnp.where(where_y < last, shift(field, -cells, 1), 0.0)
        total = total + jnp.where(where_y > 0, shift(field, cells, 1), 0.0)
        total = total + jnp.where(where_z < last, shift(field, -1, 1), 0.0)
        return total + jnp.where(where_z > 0, shift(field, 1, 1), 0.0)

    half = cells // 2
    lane = iota((8, half**3), 1)
    half_at = split_index(lane, half, 3)
    half_scale = halves[...]

    def half_beside(field):
        total = jnp.zeros_like(field)
        for position, reach in zip(half_at, (half * half, half, 1)):
            total = total + jnp.where(position < half - 1, shift(field, -reach, 1), 0.0)
            total = total + jnp.where(position > 0, shift(field, reach, 1), 0.0)
        return total

    def half_cycle(right):
        swept = half_scale * right
        remain = times_choice(jnp.concatenate([(1.0 - damping) * right, 0.25 * swept], axis=1), coarsen[...])
        local = (2.0 - damping) * swept + 0.25 * half_scale * half_beside(swept)
        return local + times_parts(remain * quarter[...], sweeps[...])

    def relax(field, right):
        return (1.0 - damping) * field + inverse * (right + beside(field))

    field = inverse * source
    for cycle in range(VCYCLES):
        if cycle:
            field = relax(field, source)
        remain = source - diagonal * field + beside(field)
        right = plane_restrict(remain, gather[...], cells, 3)
        right = jnp.concatenate([right, jnp.zeros((5, half**3), jnp.float32)], axis=0)
        field = field + plane_prolong(half_cycle(right), scatter[...], cells, 3)
        field = relax(field, source)
    base_out[...] = field
    energy = jnp.sum(jnp.sum(source * field, axis=0, keepdims=True), axis=1, keepdims=True)
    message = front[...]
    at = (iota(message.shape, 0) == sizes[1] // 2) & (iota(message.shape, 1) == count)
    message = message + jnp.where(at, energy, 0.0)
    for device in range(sizes[0] * sizes[1]):
        send_out[device] = message


def ends_kernel(cells, base, pick, lower_x, lower_y, lower_z):
    lower_x[...], lower_y[...], lower_z[...] = face_ends(base[...], pick[...], cells, False)


def between_kernel(
    cells,
    base,
    primal_index,
    region_inverse,
    coarse_map,
    global_inverse,
    ends_out,
    region_out,
    through_out,
    global_out,
    spots_out,
    choose_out,
):
    face = cells * cells
    on_x, on_y, on_z = face_ends(base[...], pick_matrix(cells, True), cells, True)
    ends_out[...] = jnp.concatenate([on_x, on_y, on_z, jnp.zeros((7, face), jnp.float32)], axis=0)
    count = primal_index.shape[1]
    group, _, place, _ = decode(primal_index[...], cells)
    choose_out[...] = jnp.concatenate(
        [one_hot(iota((3 * cells, count), 0) == place), one_hot(iota((16, count), 0) == group)], axis=0
    )
    _, spot, _, lane = decode(column_of(primal_index[...]), cells)
    at = iota((count, face), 1)
    spots_out[...] = jnp.concatenate([jnp.where(at == lane, 1.0, 0.0), jnp.where(at == spot, 1.0, 0.0)], axis=1)
    blank = jnp.zeros((count, LANES - count), jnp.float32)
    for q in range(region_out.shape[0]):
        region_out[q] = jnp.concatenate([region_inverse[0, :, q * count : (q + 1) * count], blank], axis=1)
    both = both_parts(global_inverse[...])
    global_out[...] = both
    through_out[...] = times_parts(coarse_map[0], both)


def after_kernel(
    cells,
    sizes,
    count,
    received,
    base,
    ends,
    after_x,
    after_y,
    after_z,
    upper,
    spots,
    choose,
    region_blocks,
    through,
    global_parts,
    direction,
    multipliers,
    residual,
    viscosity,
    multipliers_out,
    residual_out,
    velocity_out,
    pressure_out,
):
    face = cells * cells
    n_region, n_sub = sizes
    half = n_sub // 2
    columns = through.shape[1]
    me_region = lax.axis_index("region")
    everything = jnp.sum(received[...], axis=0)
    totals = [everything[half + 1 + i : half + 2 + i] for i in range(columns // LANES)]
    total = jnp.concatenate(totals, axis=1)
    added = jnp.zeros((count, LANES), jnp.float32)
    for i, part in enumerate(totals):
        added = added + through[:, i * LANES : (i + 1) * LANES] * part
    for q in range(n_sub):
        added = added + region_blocks[q] * received[me_region * n_sub + q, half : half + 1, :]
    lifted = jnp.sum(added, axis=1, keepdims=True)
    added = choice_times(choose[...], lifted * spots[...])
    velocity = base[...] + added[: 3 * cells, :face]
    upper_faces = ends[:9] + added[3 * cells : 3 * cells + 9, face:]
    for c in range(3):
        velocity_out[0, c] = velocity[c * cells : (c + 1) * cells]
    after = [after_x[...], after_y[...], after_z[...]]
    ahead = jnp.concatenate([spread(after[1][1:2], cells), spread(after[2][2:3], cells)], axis=1)
    ahead = times_choice(ahead, upper[...])
    where_x, where_y, where_z = positions(cells, cells)
    end = cells - 1
    field_x, field_y, field_z = [velocity[c * cells : (c + 1) * cells] for c in range(3)]
    step_x = jnp.where(where_x == end, jnp.broadcast_to(after[0][0:1], (cells, face)), shift(field_x, -1, 0))
    step_y = jnp.where(where_y == end, 0.0, shift(field_y, -cells, 1))
    step_z = jnp.where(where_z == end, 0.0, shift(field_z, -1, 1))
    step = (step_x - field_x) + (step_y - field_y) + (step_z - field_z) + ahead
    pressure_out[0] = -viscosity[0] * step
    piece = total.astype(jnp.bfloat16).astype(jnp.float32)
    row = iota((16, columns), 0)
    parts = jnp.where(row == 0, piece, jnp.where(row == 1, total - piece, 0.0)).astype(jnp.bfloat16)
    top = jnp.dot(parts, global_parts[...], preferred_element_type=jnp.float32)
    top = top[0:1, :columns] + top[1:2, :columns] + top[0:1, columns:]
    lines = received[:, half, :].reshape(n_region, n_sub, LANES)
    quadratic = jnp.zeros((n_region, n_sub, LANES), jnp.float32)
    for k in range(half):
        products = received[:, k, :].reshape(n_region, n_sub, LANES)
        quadratic = quadratic + products * pltpu.roll(lines, n_sub - 1 - k, 1)
    own_line = everything[half : half + 1]
    lane = iota((1, LANES), 1)
    quadratic = jnp.sum(quadratic.reshape(n_region * n_sub, LANES), axis=0, keepdims=True)
    curvature = quadratic + jnp.where(lane == count, own_line, 0.0)
    for i in range(columns // LANES):
        curvature = curvature + totals[i] * top[:, i * LANES : (i + 1) * LANES]
    curvature = jnp.sum(curvature, axis=1, keepdims=True)
    squares = jnp.sum(jnp.where(lane == count + 1, own_line, 0.0), axis=1, keepdims=True)
    alpha = squares / curvature
    for d in range(3):
        jump = upper_faces[3 * d : 3 * d + 3] - after[d]
        for c in range(3):
            residual_out[3 * d + c] = residual[3 * d + c] - alpha * jump[c : c + 1]
            multipliers_out[3 * d + c] = multipliers[3 * d + c] + alpha * direction[3 * d + c]


def body(
    sizes,
    multipliers,
    direction,
    residual,
    reaction,
    viscosity,
    primal_index,
    region_inverse,
    coarse_map,
    global_inverse,
):
    n_region, n_sub = sizes
    cells = reaction.shape[1]
    face = reaction.shape[2]
    count = primal_index.shape[1]
    columns = coarse_map.shape[2]
    height = -(-(n_sub // 2 + 1 + columns // LANES) // 8) * 8
    rows = 3 * cells
    shape = direction.shape
    lines = (9, 1, face)
    f32 = jnp.float32
    bf16 = jnp.bfloat16
    vmem = pl.BlockSpec(memory_space=pltpu.VMEM)
    hbm = pl.BlockSpec(memory_space=pltpu.HBM)

    def like(shape, kind=f32):
        return jax.ShapeDtypeStruct(shape, kind)

    def call(kernel, out_shape, operands, in_hbm=(), scratch=()):
        return pl.pallas_call(
            kernel,
            out_shape=out_shape,
            in_specs=[vmem] * len(operands) + [hbm] * len(in_hbm),
            out_specs=[vmem] * len(out_shape),
            scratch_shapes=[pltpu.VMEM(x.shape, x.dtype) for x in scratch]
            + ([pltpu.SemaphoreType.DMA((len(in_hbm),))] if in_hbm else []),
            compiler_params=pltpu.CompilerParams(vmem_limit_bytes=32 * 1024 * 1024),
        )(*operands, *[pltpu.with_memory_space_constraint(x, pltpu.HBM) for x in in_hbm])

    below_x = shifted_2(direction, "region", 1).reshape(lines)
    below_y = shifted_2(direction, "sub", DOM_Z).reshape(lines)
    below_z = shifted_2(direction, "sub", 1).reshape(lines)
    multipliers, direction, residual = [x.reshape(lines) for x in (multipliers, direction, residual)]
    half_cells = (cells // 2) ** 3
    (
        direction, residual, source, front, inverses, lower, upper, pick, halves, quarter, gather, scatter, coarsen, sweeps
    ) = call(
        functools.partial(before_kernel, cells, sizes),
        [
            like(lines),
            like(lines),
            like((rows, face)),
            like((height, LANES)),
            like((2, cells, face)),
            like((2 * face, face), bf16),
            like((2 * face, face), bf16),
            like((face, 2 * face), bf16),
            like((1, half_cells)),
            like((1, half_cells // 8)),
            like((face, half_cells), bf16),
            like((half_cells, face), bf16),
            like((2 * half_cells, half_cells // 8), bf16),
            like((half_cells // 8, 2 * half_cells), bf16),
        ],
        [],
        [direction, residual, reaction, primal_index, region_inverse, coarse_map],
        [reaction, primal_index, region_inverse, coarse_map],
    )
    base, sent = call(
        functools.partial(solve_kernel, cells, sizes, count),
        [like((rows, face)), like((n_region * n_sub, height, LANES))],
        [source, below_x, below_y, below_z, inverses, front, lower, halves, quarter, gather, scatter, coarsen, sweeps],
    )
    received = lax.all_to_all(sent, ("region", "sub"), 0, 0, tiled=True)
    lower_x, lower_y, lower_z = call(
        functools.partial(ends_kernel, cells), [like((3, face))] * 3, [base, pick]
    )
    after_x = shifted_2(lower_x, "region", -1)
    after_y = shifted_2(lower_y, "sub", -DOM_Z)
    after_z = shifted_2(lower_z, "sub", -1)
    ends, region_blocks, through, global_parts, spots, choose = call(
        functools.partial(between_kernel, cells),
        [
            like((16, face)),
            like((n_sub, count, LANES)),
            like((count, columns)),
            like((columns, 2 * columns), bf16),
            like((count, 2 * face)),
            like((rows + 16, count), bf16),
        ],
        [base, primal_index, region_inverse, coarse_map, global_inverse],
    )
    new_multipliers, new_residual, velocity, pressure = call(
        functools.partial(after_kernel, cells, sizes, count),
        [like(lines), like(lines), like((1, 3, cells, face)), like((1, cells, face))],
        [
            received,
            base,
            ends,
            after_x,
            after_y,
            after_z,
            upper,
            spots,
            choose,
            region_blocks,
            through,
            global_parts,
            direction,
            multipliers,
            residual,
            viscosity,
        ],
    )
    return new_multipliers.reshape(shape), new_residual.reshape(shape), velocity, pressure


def solution(mesh):
    sizes = (mesh.shape["region"], mesh.shape["sub"])
    whole = P(("region", "sub"))
    in_specs = (whole,) * 6 + (P("region", "sub"), whole, P())
    return jax.shard_map(
        functools.partial(body, sizes), mesh=mesh, in_specs=in_specs, out_specs=(whole,) * 4, check_vma=False
    )
```

```python
import functools

import jax
import jax.numpy as jnp
from jax import lax
from jax.experimental import pallas as pl
from jax.experimental.pallas import tpu as pltpu
from jax.sharding import PartitionSpec as P

DOM_Z = 4
LEVELS = 3
SWEEPS = 1
COARSE_SWEEPS = 8
VCYCLES = 2
LANES = 128

damping = 0.8


def shifted_2(x, axis, by):
    count = lax.axis_size(axis)
    return lax.ppermute(x, axis, [(i, (i + by) % count) for i in range(count)])


def iota(shape, dim):
    return lax.broadcasted_iota(jnp.int32, shape, dim)


def parts_of(x, count=3):
    result = []
    for step in range(count):
        piece = x.astype(jnp.bfloat16)
        result.append(piece)
        if step < count - 1:
            x = x - piece.astype(jnp.float32)
    return result


def times_choice(x, choice, count=2):
    rows = x.shape[0]
    stacked = jnp.concatenate(parts_of(x, count), axis=0)
    y = jnp.dot(stacked, choice, preferred_element_type=jnp.float32)
    return functools.reduce(lambda a, b: a + b, [y[i * rows : (i + 1) * rows] for i in range(count)])


def times_parts(x, both):
    rows = x.shape[0]
    width = both.shape[1] // 2
    y = jnp.dot(jnp.concatenate(parts_of(x, 2), axis=0), both, preferred_element_type=jnp.float32)
    return y[:rows, :width] + (y[rows:, :width] + y[:rows, width:])


def both_parts(w):
    return jnp.concatenate(parts_of(w, 2), axis=1)


def choice_times(choice, x, count=2):
    width = x.shape[1]
    stacked = jnp.concatenate(parts_of(x, count), axis=1)
    y = jnp.dot(choice, stacked, preferred_element_type=jnp.float32)
    return functools.reduce(lambda a, b: a + b, [y[:, i * width : (i + 1) * width] for i in range(count)])


def one_hot(condition):
    return jnp.where(condition, 1.0, 0.0).astype(jnp.bfloat16)


def decode(picked, cells):
    face = cells * cells
    zero = jnp.zeros_like(picked)
    one = zero + 1
    block = jnp.where(picked >= 3 * face, one, zero) + jnp.where(picked >= 6 * face, one, zero)
    rest = picked - 3 * face * block
    component = jnp.where(rest >= face, one, zero) + jnp.where(rest >= 2 * face, one, zero)
    spot = rest - face * component
    first = lax.div(spot, zero + cells)
    second = spot - first * cells
    end = cells - 1
    x = jnp.where(block == 0, end, first)
    y = jnp.where(block == 0, first, jnp.where(block == 1, end, second))
    z = jnp.where(block == 2, end, second)
    return 3 * block + component, spot, component * cells + x, y * cells + z


def faces_of(rows):
    return [jnp.concatenate([rows[3 * d + c] for c in range(3)], axis=0) for d in range(3)]


def spread(faces, cells):
    face = cells * cells
    here = lax.div(iota((cells, face), 1), jnp.full((cells, face), cells, jnp.int32)) == iota((cells, face), 0)
    rows = [jnp.where(here, jnp.broadcast_to(faces[c : c + 1], (cells, face)), 0.0) for c in range(faces.shape[0])]
    return jnp.concatenate(rows, axis=0)


def mask_sum(x, cells):
    face = cells * cells
    here = lax.div(iota((cells, face), 1), jnp.full((cells, face), cells, jnp.int32)) == iota((cells, face), 0)
    rows = [
        jnp.sum(jnp.where(here, x[c * cells : (c + 1) * cells], 0.0), axis=0, keepdims=True)
        for c in range(x.shape[0] // cells)
    ]
    return jnp.concatenate(rows, axis=0)


def place_matrix(cells, upper):
    row = iota((cells, cells * cells), 0)
    column = iota((cells, cells * cells), 1)
    end = cells - 1 if upper else 0
    on_y = one_hot(column == row + end * cells)
    on_z = one_hot(column == row * cells + end)
    return jnp.concatenate([on_y] * cells + [on_z] * cells, axis=0)


def pick_matrix(cells, upper):
    face = cells * cells
    row = iota((face, LANES), 0)
    second = iota((face, LANES), 1) & (cells - 1)
    end = cells - 1 if upper else 0
    on_y = one_hot(row == second + end * cells)
    on_z = one_hot(row == second * cells + end)
    return jnp.concatenate([on_y] * (face // LANES) + [on_z] * (face // LANES), axis=1)


def face_ends(field, pick, cells, upper):
    face = cells * cells
    at = cells - 1 if upper else 0
    ends = times_choice(field, pick)
    on_x = [field[c * cells + at : c * cells + at + 1] for c in range(3)]
    return jnp.concatenate(on_x, axis=0), mask_sum(ends[:, :face], cells), mask_sum(ends[:, face:], cells)


def column_of(line):
    count = line.shape[1]
    wide = jnp.broadcast_to(line.astype(jnp.float32), (count, count))
    diagonal = iota((count, count), 0) == iota((count, count), 1)
    return jnp.sum(jnp.where(diagonal, wide, 0.0), axis=1, keepdims=True).astype(jnp.int32)


def shift(field, by, dim):
    size = field.shape[dim]
    return pltpu.roll(field, by % size, dim)


def positions(rows, cells):
    shape = (rows, cells * cells)
    return (iota(shape, 0) & (cells - 1), *split_index(iota(shape, 1), cells, 2))


def bits(cells):
    return cells.bit_length() - 1


def split_index(flat, cells, dims):
    return [(flat >> (bits(cells) * (dims - 1 - i))) & (cells - 1) for i in range(dims)]


def plane_blocks(y, z, far_y, far_z, steps=1):
    inside = [(y >> steps) == far_y, (z >> steps) == far_z]
    nearby = [(f >> 1) + 2 * (f & 1) - 1 == b for f, b in ((y, far_y), (z, far_z))]
    same = inside[0] & inside[1]
    near = (nearby[0] & inside[1]) | (inside[0] & nearby[1])
    return one_hot(same), jnp.where(same, 2.0, jnp.where(near, 1.0, 0.0)).astype(jnp.bfloat16)


def gather_matrix(cells, steps=1):
    size = cells >> steps
    width = min(size**3, LANES)
    shape = (cells * cells, width)
    y, z = split_index(iota(shape, 0), cells, 2)
    _, far_y, far_z = split_index(iota(shape, 1), size, 3)
    return [
        jnp.concatenate([x] * (size**3 // width), axis=1) for x in plane_blocks(y, z, far_y, far_z, steps)
    ]


def scatter_matrix(cells):
    half = cells // 2
    shape = (half * half, cells * cells)
    y, z = split_index(iota(shape, 1), cells, 2)
    half_y, half_z = split_index(iota(shape, 0), half, 2)
    return jnp.concatenate([jnp.concatenate(plane_blocks(y, z, half_y, half_z), axis=1)] * half, axis=0)


def block_matrices(cells, blocks_first):
    half = cells // 2
    shape = (half**3, cells**3) if blocks_first else (cells**3, half**3)
    fine = split_index(iota(shape, 1 if blocks_first else 0), cells, 3)
    block = split_index(iota(shape, 0 if blocks_first else 1), half, 3)
    inside = [(f >> 1) == b for f, b in zip(fine, block)]
    nearby = [(f >> 1) + 2 * (f & 1) - 1 == b for f, b in zip(fine, block)]
    same = inside[0] & inside[1] & inside[2]
    near = (
        (nearby[0] & inside[1] & inside[2])
        | (inside[0] & nearby[1] & inside[2])
        | (inside[0] & inside[1] & nearby[2])
    )
    return one_hot(same), jnp.where(same, 3.0, jnp.where(near, 1.0, 0.0)).astype(jnp.bfloat16)


def own_part(cells, steps=1):
    size = cells >> steps
    shape = (cells, size**3)
    return split_index(iota(shape, 1), size, 3)[0] == (iota(shape, 0) >> steps)


def plane_restrict(field, gather, cells, count, steps=1):
    spread_out = times_choice(field, gather)
    here = own_part(cells, steps)
    rows = [
        jnp.sum(jnp.where(here, spread_out[c * cells : (c + 1) * cells], 0.0), axis=0, keepdims=True)
        for c in range(count)
    ]
    return 0.125**steps * (rows[0] if count == 1 else jnp.concatenate(rows, axis=0))


def plane_prolong(coarse, scatter, cells, count):
    here = own_part(cells)
    wide = [
        jnp.where(here, jnp.broadcast_to(coarse[c : c + 1], (cells, coarse.shape[1])), 0.0) for c in range(count)
    ]
    fine = times_choice(jnp.concatenate(wide, axis=0), scatter)
    face = cells * cells
    return fine[:, :face], fine[:, face:]


def sweep_power(scale, cells, weight):
    size = cells**3
    shape = (size, size)
    here = split_index(iota(shape, 0), cells, 3)
    there = split_index(iota(shape, 1), cells, 3)
    distance = functools.reduce(lambda a, b: a + b, [jnp.abs(a - b) for a, b in zip(here, there)])
    one = jnp.where(distance == 0, 1.0, 0.0)
    return (1.0 - damping) * one + jnp.where(distance == 1, weight * scale, 0.0), one


def square(power):
    return times_parts(power, both_parts(power))


def powers_sum(total, power):
    done = 2
    while done < COARSE_SWEEPS:
        total = total + times_parts(total, both_parts(power))
        done *= 2
        if done < COARSE_SWEEPS:
            power = square(power)
    return total


def load(pairs, semaphores):
    copies = [pltpu.make_async_copy(a, b, semaphores.at[i]) for i, (a, b) in enumerate(pairs)]
    for copy in copies:
        copy.start()
    return copies


def before_kernel(
    cells,
    sizes,
    direction_in,
    residual_in,
    reaction_in,
    primal_index_in,
    region_inverse_in,
    coarse_map_in,
    direction,
    residual,
    source_out,
    front_out,
    inverse_out,
    lower_out,
    upper_out,
    pick_out,
    half_out,
    quarter_out,
    gather_out,
    scatter_out,
    coarsen_out,
    sweeps_out,
    reaction,
    primal_index,
    region_inverse,
    coarse_map,
    semaphores,
):
    copies = load(
        [
            (direction_in, direction),
            (reaction_in, reaction),
            (primal_index_in, primal_index),
            (residual_in, residual),
            (coarse_map_in, coarse_map),
            (region_inverse_in, region_inverse),
        ],
        semaphores,
    )
    face = cells * cells
    n_sub = sizes[1]
    lower_out[...] = place_matrix(cells, False)
    upper = place_matrix(cells, True)
    upper_out[...] = upper
    pick_out[...] = pick_matrix(cells, False)
    half = cells // 2
    gather, gather_near = gather_matrix(cells)
    gather_out[...] = jnp.concatenate([gather, gather_near], axis=0)
    quarter_gather = gather_matrix(cells, 2)[0]
    scatter_out[...] = scatter_matrix(cells)
    coarsen, coarsen_near = block_matrices(half, False)
    coarsen_out[...] = jnp.concatenate([coarsen, coarsen_near], axis=0)
    refine = jnp.concatenate(block_matrices(half, True), axis=1)
    for copy in copies[:3]:
        copy.wait()
    react = reaction[0]
    scale = damping / (plane_restrict(react, quarter_gather, cells, 1, 2) + 6.0 * 0.0625)
    quarter_out[...] = 0.125 * scale
    power, one = sweep_power(scale, half // 2, 0.0625)
    second_power = square(power)
    diagonal = react + 6.0
    inverse_out[0] = damping / diagonal
    inverse_out[1] = diagonal
    half_scale = damping / (plane_restrict(react, gather, cells, 1) + 6.0 * 0.25)
    half_out[...] = half_scale
    faces = faces_of(direction)
    count = primal_index.shape[1]
    group, spot, _, _ = decode(column_of(primal_index[...]), cells)
    nine = jnp.concatenate(faces + [jnp.zeros((7, face), jnp.float32)], axis=0)
    gathered = choice_times(one_hot(iota((count, 16), 1) == group), nine)
    primal = jnp.sum(jnp.where(iota((count, face), 1) == spot, gathered, 0.0), axis=1, keepdims=True)
    lane = iota((1, LANES), 1)
    line = jnp.sum(
        jnp.where(iota((count, LANES), 0) == iota((count, LANES), 1), primal, 0.0), axis=0, keepdims=True
    )
    for copy in copies[3:]:
        copy.wait()
    refined = times_choice(powers_sum(one + power, second_power), refine)
    sweeps_out[...] = both_parts(
        (1.0 - damping) * refined[:, : half**3] + 0.25 * half_scale * refined[:, half**3 :]
    )
    row_x = iota((cells, face), 0)
    source = times_choice(jnp.concatenate([spread(faces[1], cells), spread(faces[2], cells)], axis=1), upper)
    own_x = jnp.concatenate(
        [jnp.where(row_x == cells - 1, jnp.broadcast_to(faces[0][c : c + 1], (cells, face)), 0.0) for c in range(3)],
        axis=0,
    )
    source_out[...] = source + own_x
    share = jnp.sum(primal * coarse_map[0], axis=0, keepdims=True)
    product = jnp.sum(primal * region_inverse[0], axis=0, keepdims=True)
    blank = jnp.zeros((1, LANES - count), jnp.float32)
    blocks = jnp.concatenate(
        [jnp.concatenate([product[:, q * count : (q + 1) * count], blank], axis=1) for q in range(n_sub)], axis=0
    )
    me_sub = lax.axis_index("sub")
    own = jnp.sum(jnp.where(iota(blocks.shape, 0) == me_sub, blocks, 0.0), axis=0, keepdims=True)
    own = jnp.sum(own * line, axis=1, keepdims=True)
    blocks = pltpu.roll(blocks, n_sub - 1 - me_sub, 0)
    opposite = n_sub // 2
    twice = jnp.where(iota((opposite, LANES), 0) == (opposite - 1 if n_sub % 2 == 0 else opposite), 1.0, 2.0)
    squares = jnp.concatenate([residual[i] for i in range(9)], axis=0)
    squares = jnp.sum(jnp.sum(squares * squares, axis=0, keepdims=True), axis=1, keepdims=True)
    line = jnp.where(lane == count, own, jnp.where(lane == count + 1, squares, line))
    front_out[...] = jnp.zeros_like(front_out)
    front_out[:opposite, :] = blocks[:opposite] * twice
    front_out[opposite : opposite + 1, :] = line
    for i in range(share.shape[1] // LANES):
        front_out[opposite + 1 + i : opposite + 2 + i, :] = share[:, i * LANES : (i + 1) * LANES]


def solve_kernel(
    cells,
    sizes,
    count,
    source_own,
    from_x,
    from_y,
    from_z,
    inverses,
    front,
    lower,
    halves,
    quarter,
    gather,
    scatter,
    coarsen,
    sweeps,
    base_out,
    send_out,
    buffer,
    semaphores,
):
    face = cells * cells
    rows = 3 * cells
    below_x, below_y, below_z = [faces_of(ref)[d] for d, ref in enumerate((from_x, from_y, from_z))]
    n_region, n_sub = sizes
    row_x = iota((cells, face), 0)
    source = source_own[...] - times_choice(
        jnp.concatenate([spread(below_y, cells), spread(below_z, cells)], axis=1), lower[...]
    )
    source = source - jnp.concatenate(
        [jnp.where(row_x == 0, jnp.broadcast_to(below_x[c : c + 1], (cells, face)), 0.0) for c in range(3)],
        axis=0,
    )
    where_x, where_y, where_z = positions(rows, cells)
    last = cells - 1

    def tall(x):
        return jnp.concatenate([x] * 3, axis=0)

    inverse = tall(inverses[0])
    diagonal = tall(inverses[1])

    def beside_x(field):
        total = jnp.where(where_x < last, shift(field, -1, 0), 0.0)
        return total + jnp.where(where_x > 0, shift(field, 1, 0), 0.0)

    def beside(field):
        total = jnp.where(where_y < last, shift(field, -cells, 1), 0.0)
        total = total + jnp.where(where_y > 0, shift(field, cells, 1), 0.0)
        total = total + jnp.where(where_z < last, shift(field, -1, 1), 0.0)
        total = total + jnp.where(where_z > 0, shift(field, 1, 1), 0.0)
        return beside_x(field) + total

    half = cells // 2
    lane = iota((8, half**3), 1)
    half_at = split_index(lane, half, 3)
    half_scale = halves[...]

    def half_beside(field):
        total = jnp.zeros_like(field)
        for position, reach in zip(half_at, (half * half, half, 1)):
            total = total + jnp.where(position < half - 1, shift(field, -reach, 1), 0.0)
            total = total + jnp.where(position > 0, shift(field, reach, 1), 0.0)
        return total

    def half_cycle(right):
        swept = half_scale * right
        remain = times_choice(jnp.concatenate([(1.0 - damping) * right, 0.25 * swept], axis=1), coarsen[...])
        local = (2.0 - damping) * swept + 0.25 * half_scale * half_beside(swept)
        return local + times_parts(remain * quarter[...], sweeps[...])

    scaled = inverse * source

    def relax(field, neighbours):
        return (1.0 - damping) * field + scaled + inverse * neighbours

    def restrict(field):
        remain = jnp.concatenate([source - diagonal * field + beside_x(field), field], axis=1)
        remain = plane_restrict(remain, gather[...], cells, 3)
        return jnp.concatenate([remain, jnp.zeros((5, half**3), jnp.float32)], axis=0)

    field = scaled
    first = None
    for cycle in range(VCYCLES):
        if cycle:
            field = relax(field, beside(field))
        neighbours = beside(field)
        right = restrict(field)
        if first is None:
            first = right
            residual = (1.0 - damping) * source + neighbours
        coarse = half_cycle(right)
        if cycle == VCYCLES - 1:
            energy = jnp.sum(source * scaled + residual * field, axis=0, keepdims=True)
            coarse_energy = 8.0 * jnp.sum(first * coarse, axis=0, keepdims=True)
            pieces = [energy[:, i * LANES : (i + 1) * LANES] for i in range(face // LANES)]
            pieces += [coarse_energy[:, i * LANES : (i + 1) * LANES] for i in range(half**3 // LANES)]
            energy = jnp.sum(functools.reduce(lambda a, b: a + b, pieces), axis=1, keepdims=True)
            message = front[...]
            at = (iota(message.shape, 0) == sizes[1] // 2) & (iota(message.shape, 1) == count)
            message = message + jnp.where(at, energy, 0.0)
            for device in range(sizes[0] * sizes[1]):
                buffer[device] = message
            (copy,) = load([(buffer, send_out)], semaphores)
        correction, nearby = plane_prolong(coarse, scatter[...], cells, 3)
        field = relax(field + correction, neighbours + beside_x(correction) + nearby)
    base_out[...] = field
    copy.wait()


def ends_kernel(cells, base, pick, lower_x, lower_y, lower_z):
    lower_x[...], lower_y[...], lower_z[...] = face_ends(base[...], pick[...], cells, False)


def between_kernel(
    cells,
    base,
    primal_index,
    region_inverse,
    coarse_map,
    global_inverse,
    ends_out,
    region_out,
    through_out,
    global_out,
    spots_out,
    choose_out,
):
    face = cells * cells
    on_x, on_y, on_z = face_ends(base[...], pick_matrix(cells, True), cells, True)
    ends_out[...] = jnp.concatenate([on_x, on_y, on_z, jnp.zeros((7, face), jnp.float32)], axis=0)
    count = primal_index.shape[1]
    group, _, place, _ = decode(primal_index[...], cells)
    choose_out[...] = jnp.concatenate(
        [one_hot(iota((3 * cells, count), 0) == place), one_hot(iota((16, count), 0) == group)], axis=0
    )
    _, spot, _, lane = decode(column_of(primal_index[...]), cells)
    at = iota((count, face), 1)
    spots_out[...] = jnp.concatenate([jnp.where(at == lane, 1.0, 0.0), jnp.where(at == spot, 1.0, 0.0)], axis=1)
    blank = jnp.zeros((count, LANES - count), jnp.float32)
    for q in range(region_out.shape[0]):
        region_out[q] = jnp.concatenate([region_inverse[0, :, q * count : (q + 1) * count], blank], axis=1)
    both = both_parts(global_inverse[...])
    global_out[...] = both
    through_out[...] = times_parts(coarse_map[0], both)


def after_kernel(
    cells,
    sizes,
    count,
    received,
    base,
    ends,
    after_x,
    after_y,
    after_z,
    upper,
    spots,
    choose,
    region_blocks,
    through,
    global_parts,
    direction,
    multipliers,
    residual,
    viscosity,
    multipliers_out,
    residual_out,
    velocity_out,
    pressure_out,
):
    face = cells * cells
    n_region, n_sub = sizes
    half = n_sub // 2
    columns = through.shape[1]
    me_region = lax.axis_index("region")
    everything = jnp.sum(received[...], axis=0)
    totals = [everything[half + 1 + i : half + 2 + i] for i in range(columns // LANES)]
    total = jnp.concatenate(totals, axis=1)
    added = jnp.zeros((count, LANES), jnp.float32)
    for i, part in enumerate(totals):
        added = added + through[:, i * LANES : (i + 1) * LANES] * part
    for q in range(n_sub):
        added = added + region_blocks[q] * received[me_region * n_sub + q, half : half + 1, :]
    lifted = jnp.sum(added, axis=1, keepdims=True)
    added = choice_times(choose[...], lifted * spots[...])
    velocity = base[...] + added[: 3 * cells, :face]
    upper_faces = ends[:9] + added[3 * cells : 3 * cells + 9, face:]
    for c in range(3):
        velocity_out[0, c] = velocity[c * cells : (c + 1) * cells]
    after = [after_x[...], after_y[...], after_z[...]]
    ahead = jnp.concatenate([spread(after[1][1:2], cells), spread(after[2][2:3], cells)], axis=1)
    ahead = times_choice(ahead, upper[...])
    where_x, where_y, where_z = positions(cells, cells)
    end = cells - 1
    field_x, field_y, field_z = [velocity[c * cells : (c + 1) * cells] for c in range(3)]
    step_x = jnp.where(where_x == end, jnp.broadcast_to(after[0][0:1], (cells, face)), shift(field_x, -1, 0))
    step_y = jnp.where(where_y == end, 0.0, shift(field_y, -cells, 1))
    step_z = jnp.where(where_z == end, 0.0, shift(field_z, -1, 1))
    step = (step_x - field_x) + (step_y - field_y) + (step_z - field_z) + ahead
    pressure_out[0] = -viscosity[0] * step
    piece = total.astype(jnp.bfloat16).astype(jnp.float32)
    row = iota((16, columns), 0)
    parts = jnp.where(row == 0, piece, jnp.where(row == 1, total - piece, 0.0)).astype(jnp.bfloat16)
    top = jnp.dot(parts, global_parts[...], preferred_element_type=jnp.float32)
    top = top[0:1, :columns] + top[1:2, :columns] + top[0:1, columns:]
    lines = received[:, half, :].reshape(n_region, n_sub, LANES)
    quadratic = jnp.zeros((n_region, n_sub, LANES), jnp.float32)
    for k in range(half):
        products = received[:, k, :].reshape(n_region, n_sub, LANES)
        quadratic = quadratic + products * pltpu.roll(lines, n_sub - 1 - k, 1)
    own_line = everything[half : half + 1]
    lane = iota((1, LANES), 1)
    quadratic = jnp.sum(quadratic.reshape(n_region * n_sub, LANES), axis=0, keepdims=True)
    curvature = quadratic + jnp.where(lane == count, own_line, 0.0)
    for i in range(columns // LANES):
        curvature = curvature + totals[i] * top[:, i * LANES : (i + 1) * LANES]
    curvature = jnp.sum(curvature, axis=1, keepdims=True)
    squares = jnp.sum(jnp.where(lane == count + 1, own_line, 0.0), axis=1, keepdims=True)
    alpha = squares / curvature
    for d in range(3):
        jump = upper_faces[3 * d : 3 * d + 3] - after[d]
        for c in range(3):
            residual_out[3 * d + c] = residual[3 * d + c] - alpha * jump[c : c + 1]
            multipliers_out[3 * d + c] = multipliers[3 * d + c] + alpha * direction[3 * d + c]


def body(
    sizes,
    multipliers,
    direction,
    residual,
    reaction,
    viscosity,
    primal_index,
    region_inverse,
    coarse_map,
    global_inverse,
):
    n_region, n_sub = sizes
    cells = reaction.shape[1]
    face = reaction.shape[2]
    count = primal_index.shape[1]
    columns = coarse_map.shape[2]
    height = -(-(n_sub // 2 + 1 + columns // LANES) // 8) * 8
    rows = 3 * cells
    shape = direction.shape
    lines = (9, 1, face)
    f32 = jnp.float32
    bf16 = jnp.bfloat16
    vmem = pl.BlockSpec(memory_space=pltpu.VMEM)
    hbm = pl.BlockSpec(memory_space=pltpu.HBM)

    def like(shape, kind=f32):
        return jax.ShapeDtypeStruct(shape, kind)

    def call(kernel, out_shape, operands, in_hbm=(), scratch=(), out_hbm=0):
        return pl.pallas_call(
            kernel,
            out_shape=out_shape,
            in_specs=[vmem] * len(operands) + [hbm] * len(in_hbm),
            out_specs=[vmem] * (len(out_shape) - out_hbm) + [hbm] * out_hbm,
            scratch_shapes=[pltpu.VMEM(x.shape, x.dtype) for x in scratch]
            + ([pltpu.SemaphoreType.DMA((len(in_hbm) + out_hbm,))] if in_hbm or out_hbm else []),
            compiler_params=pltpu.CompilerParams(vmem_limit_bytes=32 * 1024 * 1024),
        )(*operands, *[pltpu.with_memory_space_constraint(x, pltpu.HBM) for x in in_hbm])

    below_x = shifted_2(direction, "region", 1).reshape(lines)
    below_y = shifted_2(direction, "sub", DOM_Z).reshape(lines)
    below_z = shifted_2(direction, "sub", 1).reshape(lines)
    multipliers, direction, residual = [x.reshape(lines) for x in (multipliers, direction, residual)]
    half_cells = (cells // 2) ** 3
    (
        direction, residual, source, front, inverses, lower, upper, pick, halves, quarter, gather, scatter, coarsen, sweeps
    ) = call(
        functools.partial(before_kernel, cells, sizes),
        [
            like(lines),
            like(lines),
            like((rows, face)),
            like((height, LANES)),
            like((2, cells, face)),
            like((2 * face, face), bf16),
            like((2 * face, face), bf16),
            like((face, 2 * face), bf16),
            like((1, half_cells)),
            like((1, half_cells // 8)),
            like((2 * face, half_cells), bf16),
            like((half_cells, 2 * face), bf16),
            like((2 * half_cells, half_cells // 8), bf16),
            like((half_cells // 8, 2 * half_cells), bf16),
        ],
        [],
        [direction, residual, reaction, primal_index, region_inverse, coarse_map],
        [reaction, primal_index, region_inverse, coarse_map],
    )
    base, sent = call(
        functools.partial(solve_kernel, cells, sizes, count),
        [like((rows, face)), like((n_region * n_sub, height, LANES))],
        [source, below_x, below_y, below_z, inverses, front, lower, halves, quarter, gather, scatter, coarsen, sweeps],
        scratch=[like((n_region * n_sub, height, LANES))],
        out_hbm=1,
    )
    received = lax.all_to_all(sent, ("region", "sub"), 0, 0, tiled=True)
    lower_x, lower_y, lower_z = call(
        functools.partial(ends_kernel, cells), [like((3, face))] * 3, [base, pick]
    )
    after_x = shifted_2(lower_x, "region", -1)
    after_y = shifted_2(lower_y, "sub", -DOM_Z)
    after_z = shifted_2(lower_z, "sub", -1)
    ends, region_blocks, through, global_parts, spots, choose = call(
        functools.partial(between_kernel, cells),
        [
            like((16, face)),
            like((n_sub, count, LANES)),
            like((count, columns)),
            like((columns, 2 * columns), bf16),
            like((count, 2 * face)),
            like((rows + 16, count), bf16),
        ],
        [base, primal_index, region_inverse, coarse_map, global_inverse],
    )
    new_multipliers, new_residual, velocity, pressure = call(
        functools.partial(after_kernel, cells, sizes, count),
        [like(lines), like(lines), like((1, 3, cells, face)), like((1, cells, face))],
        [
            received,
            base,
            ends,
            after_x,
            after_y,
            after_z,
            upper,
            spots,
            choose,
            region_blocks,
            through,
            global_parts,
            direction,
            multipliers,
            residual,
            viscosity,
        ],
    )
    return new_multipliers.reshape(shape), new_residual.reshape(shape), velocity, pressure


def solution(mesh):
    sizes = (mesh.shape["region"], mesh.shape["sub"])
    whole = P(("region", "sub"))
    in_specs = (whole,) * 6 + (P("region", "sub"), whole, P())
    return jax.shard_map(
        functools.partial(body, sizes), mesh=mesh, in_specs=in_specs, out_specs=(whole,) * 4, check_vma=False
    )
```

```python
import functools

import jax
import jax.numpy as jnp
from jax import lax
from jax.experimental import pallas as pl
from jax.experimental.pallas import tpu as pltpu
from jax.sharding import PartitionSpec as P

DOM_Z = 4
COARSE_SWEEPS = 8
LANES = 128

damping = 0.8


def shifted_2(x, axis, by):
    count = lax.axis_size(axis)
    return lax.ppermute(x, axis, [(i, (i + by) % count) for i in range(count)])


def iota(shape, dim):
    return lax.broadcasted_iota(jnp.int32, shape, dim)


def parts_of(x, count=3):
    result = []
    for step in range(count):
        piece = x.astype(jnp.bfloat16)
        result.append(piece)
        if step < count - 1:
            x = x - piece.astype(jnp.float32)
    return result


def times_choice(x, choice, count=2):
    rows = x.shape[0]
    stacked = jnp.concatenate(parts_of(x, count), axis=0)
    y = jnp.dot(stacked, choice, preferred_element_type=jnp.float32)
    return functools.reduce(lambda a, b: a + b, [y[i * rows : (i + 1) * rows] for i in range(count)])


def times_parts(x, both):
    rows = x.shape[0]
    width = both.shape[1] // 2
    y = jnp.dot(jnp.concatenate(parts_of(x, 2), axis=0), both, preferred_element_type=jnp.float32)
    return y[:rows, :width] + (y[rows:, :width] + y[:rows, width:])


def both_parts(w):
    return jnp.concatenate(parts_of(w, 2), axis=1)


def choice_times(choice, x, count=2):
    width = x.shape[1]
    stacked = jnp.concatenate(parts_of(x, count), axis=1)
    y = jnp.dot(choice, stacked, preferred_element_type=jnp.float32)
    return functools.reduce(lambda a, b: a + b, [y[:, i * width : (i + 1) * width] for i in range(count)])


def one_hot(condition):
    return jnp.where(condition, 1.0, 0.0).astype(jnp.bfloat16)


def decode(picked, cells):
    face = cells * cells
    zero = jnp.zeros_like(picked)
    one = zero + 1
    block = jnp.where(picked >= 3 * face, one, zero) + jnp.where(picked >= 6 * face, one, zero)
    rest = picked - 3 * face * block
    component = jnp.where(rest >= face, one, zero) + jnp.where(rest >= 2 * face, one, zero)
    spot = rest - face * component
    first = lax.div(spot, zero + cells)
    second = spot - first * cells
    end = cells - 1
    x = jnp.where(block == 0, end, first)
    y = jnp.where(block == 0, first, jnp.where(block == 1, end, second))
    z = jnp.where(block == 2, end, second)
    return 3 * block + component, spot, component * cells + x, y * cells + z


def faces_of(rows):
    return [jnp.concatenate([rows[3 * d + c] for c in range(3)], axis=0) for d in range(3)]


def lane_gather(x, lanes):
    return jnp.take_along_axis(x, lanes, axis=1, mode="promise_in_bounds")


def grid(cells, count, tile):
    shape = (count * cells, LANES)
    y, z = split_index(iota(shape, 1) + tile * LANES, cells, 2)
    return iota(shape, 0) & (cells - 1), y, z


def rows_of_tiles(x, rows):
    count, width = x.shape
    tiles = width // LANES
    return jnp.concatenate(
        [
            jnp.broadcast_to(x[c : c + 1, i * LANES : (i + 1) * LANES], (rows // tiles, LANES))
            for c in range(count)
            for i in range(tiles)
        ],
        axis=0,
    )


def unfold(on_y, on_z, cells, upper):
    count, face = on_y.shape
    end = cells - 1 if upper else 0
    wide_y = rows_of_tiles(on_y, cells)
    wide_z = rows_of_tiles(on_z, cells)
    tiles = []
    for tile in range(face // LANES):
        x, y, z = grid(cells, count, tile)
        start = (x * cells) & (LANES - 1)
        field = jnp.where(z == end, lane_gather(wide_z, start + y), 0.0)
        if end * cells // LANES == tile:
            field = field + jnp.where(y == end, lane_gather(wide_y, start + z), 0.0)
        tiles.append(field)
    return jnp.concatenate(tiles, axis=1)


def fold(field, cells, upper):
    face = cells * cells
    end = cells - 1 if upper else 0
    rows = LANES // cells
    tiles = [field[:, i * LANES : (i + 1) * LANES] for i in range(face // LANES)]
    x, first, second = grid(cells, 3, 0)
    on_y = lane_gather(tiles[end * cells // LANES], ((end * cells) & (LANES - 1)) + second)
    on_z = jnp.zeros_like(on_y)
    for i, tile in enumerate(tiles):
        values = lane_gather(tile, ((second * cells) & (LANES - 1)) + end)
        on_z = jnp.where(second // rows == i, values, on_z)
    here = first == (x & (rows - 1))
    faces = [jnp.concatenate([field[c * cells + end : c * cells + end + 1] for c in range(3)], axis=0)]
    for values in (on_y, on_z):
        values = jnp.where(here, values, 0.0)
        sums = [jnp.sum(values[i * rows : (i + 1) * rows], axis=0, keepdims=True) for i in range(3 * cells // rows)]
        per = face // LANES
        faces.append(
            jnp.concatenate([jnp.concatenate(sums[c * per : (c + 1) * per], axis=1) for c in range(3)], axis=0)
        )
    return faces


def column_of(line):
    count = line.shape[1]
    wide = jnp.broadcast_to(line.astype(jnp.float32), (count, count))
    diagonal = iota((count, count), 0) == iota((count, count), 1)
    return jnp.sum(jnp.where(diagonal, wide, 0.0), axis=1, keepdims=True).astype(jnp.int32)


def shift(field, by, dim):
    size = field.shape[dim]
    return pltpu.roll(field, by % size, dim)


def positions(rows, cells):
    shape = (rows, cells * cells)
    return (iota(shape, 0) & (cells - 1), *split_index(iota(shape, 1), cells, 2))


def bits(cells):
    return cells.bit_length() - 1


def split_index(flat, cells, dims):
    return [(flat >> (bits(cells) * (dims - 1 - i))) & (cells - 1) for i in range(dims)]


def plane_blocks(y, z, far_y, far_z, steps=1):
    inside = [(y >> steps) == far_y, (z >> steps) == far_z]
    nearby = [(f >> 1) + 2 * (f & 1) - 1 == b for f, b in ((y, far_y), (z, far_z))]
    same = inside[0] & inside[1]
    near = (nearby[0] & inside[1]) | (inside[0] & nearby[1])
    return one_hot(same), jnp.where(same, 2.0, jnp.where(near, 1.0, 0.0)).astype(jnp.bfloat16)


def gather_matrix(cells, steps=1):
    size = cells >> steps
    shape = (cells * cells, min(size**3, LANES))
    y, z = split_index(iota(shape, 0), cells, 2)
    _, far_y, far_z = split_index(iota(shape, 1), size, 3)
    return plane_blocks(y, z, far_y, far_z, steps)


def block_matrices(cells, blocks_first):
    half = cells // 2
    shape = (half**3, cells**3) if blocks_first else (cells**3, half**3)
    fine = split_index(iota(shape, 1 if blocks_first else 0), cells, 3)
    block = split_index(iota(shape, 0 if blocks_first else 1), half, 3)
    inside = [(f >> 1) == b for f, b in zip(fine, block)]
    nearby = [(f >> 1) + 2 * (f & 1) - 1 == b for f, b in zip(fine, block)]
    same = inside[0] & inside[1] & inside[2]
    near = (
        (nearby[0] & inside[1] & inside[2])
        | (inside[0] & nearby[1] & inside[2])
        | (inside[0] & inside[1] & nearby[2])
    )
    return one_hot(same), jnp.where(same, 3.0, jnp.where(near, 1.0, 0.0)).astype(jnp.bfloat16)


def plane_restrict(field, gather, cells, count, steps=1):
    size = cells >> steps
    width = gather.shape[1]
    per = width // (size * size) << steps
    spread_out = times_choice(field, gather)
    shape = (cells, width)
    own = split_index(iota(shape, 1), size, 3)[0] == ((iota(shape, 0) & (per - 1)) >> steps)
    group = iota(shape, 0) // per
    rows = []
    for c in range(count):
        values = jnp.where(own, spread_out[c * cells : (c + 1) * cells], 0.0)
        tiles = [
            jnp.sum(jnp.where(group == i, values, 0.0), axis=0, keepdims=True) for i in range(cells // per)
        ]
        rows.append(tiles[0] if len(tiles) == 1 else jnp.concatenate(tiles, axis=1))
    return 0.125**steps * (rows[0] if count == 1 else jnp.concatenate(rows, axis=0))


def plane_prolong(coarse, cells, count):
    half = cells // 2
    wide = rows_of_tiles(coarse[:count], cells)
    fine, nearby = [], []
    for tile in range(cells * cells // LANES):
        x, y, z = grid(cells, count, tile)
        start = ((x >> 1) * half * half) & (LANES - 1)
        half_y, half_z = y >> 1, z >> 1
        other_y, other_z = half_y + 2 * (y & 1) - 1, half_z + 2 * (z & 1) - 1
        inside_y, inside_z = (other_y & (half - 1)) == other_y, (other_z & (half - 1)) == other_z
        values = lane_gather(wide, start + half_y * half + half_z)
        beside_y = lane_gather(wide, start + (other_y & (half - 1)) * half + half_z)
        beside_z = lane_gather(wide, start + half_y * half + (other_z & (half - 1)))
        fine.append(values)
        nearby.append(2.0 * values + jnp.where(inside_y, beside_y, 0.0) + jnp.where(inside_z, beside_z, 0.0))
    return jnp.concatenate(fine, axis=1), jnp.concatenate(nearby, axis=1)


def sweep_power(scale, cells, weight):
    size = cells**3
    shape = (size, size)
    here = split_index(iota(shape, 0), cells, 3)
    there = split_index(iota(shape, 1), cells, 3)
    distance = functools.reduce(lambda a, b: a + b, [jnp.abs(a - b) for a, b in zip(here, there)])
    one = jnp.where(distance == 0, 1.0, 0.0)
    return (1.0 - damping) * one + jnp.where(distance == 1, weight * scale, 0.0), one


def square(power):
    return times_parts(power, both_parts(power))


def powers_sum(total, power):
    done = 2
    while done < COARSE_SWEEPS:
        total = total + times_parts(total, both_parts(power))
        done *= 2
        if done < COARSE_SWEEPS:
            power = square(power)
    return total


def load(pairs, semaphores):
    copies = [pltpu.make_async_copy(a, b, semaphores.at[i]) for i, (a, b) in enumerate(pairs)]
    for copy in copies:
        copy.start()
    return copies


def before_kernel(
    cells,
    sizes,
    direction_in,
    residual_in,
    reaction_in,
    primal_index_in,
    region_inverse_in,
    coarse_map_in,
    direction,
    residual,
    source_out,
    front_out,
    inverse_out,
    half_out,
    quarter_out,
    gather_out,
    coarsen_out,
    sweeps_out,
    reaction,
    primal_index,
    region_inverse,
    coarse_map,
    semaphores,
):
    copies = load(
        [
            (direction_in, direction),
            (reaction_in, reaction),
            (primal_index_in, primal_index),
            (residual_in, residual),
            (coarse_map_in, coarse_map),
            (region_inverse_in, region_inverse),
        ],
        semaphores,
    )
    face = cells * cells
    n_sub = sizes[1]
    half = cells // 2
    gather, gather_near = gather_matrix(cells)
    gather_out[...] = jnp.concatenate([gather, gather_near], axis=0)
    quarter_gather = gather_matrix(cells, 2)[0]
    coarsen, coarsen_near = block_matrices(half, False)
    coarsen_out[...] = jnp.concatenate([coarsen, coarsen_near], axis=0)
    refine = jnp.concatenate(block_matrices(half, True), axis=1)
    for copy in copies[:3]:
        copy.wait()
    react = reaction[0]
    scale = damping / (plane_restrict(react, quarter_gather, cells, 1, 2) + 6.0 * 0.0625)
    quarter_out[...] = 0.125 * scale
    power, one = sweep_power(scale, half // 2, 0.0625)
    second_power = square(power)
    diagonal = react + 6.0
    inverse_out[0] = damping / diagonal
    inverse_out[1] = diagonal
    half_scale = damping / (plane_restrict(react, gather, cells, 1) + 6.0 * 0.25)
    half_out[...] = half_scale
    faces = faces_of(direction)
    count = primal_index.shape[1]
    group, spot, _, _ = decode(column_of(primal_index[...]), cells)
    nine = jnp.concatenate(faces + [jnp.zeros((7, face), jnp.float32)], axis=0)
    gathered = choice_times(one_hot(iota((count, 16), 1) == group), nine)
    primal = jnp.sum(jnp.where(iota((count, face), 1) == spot, gathered, 0.0), axis=1, keepdims=True)
    lane = iota((1, LANES), 1)
    line = jnp.sum(
        jnp.where(iota((count, LANES), 0) == iota((count, LANES), 1), primal, 0.0), axis=0, keepdims=True
    )
    for copy in copies[3:]:
        copy.wait()
    refined = times_choice(powers_sum(one + power, second_power), refine)
    sweeps_out[...] = both_parts(
        (1.0 - damping) * refined[:, : half**3] + 0.25 * half_scale * refined[:, half**3 :]
    )
    row_x = iota((cells, face), 0)
    source = unfold(faces[1], faces[2], cells, True)
    own_x = jnp.concatenate(
        [jnp.where(row_x == cells - 1, jnp.broadcast_to(faces[0][c : c + 1], (cells, face)), 0.0) for c in range(3)],
        axis=0,
    )
    source_out[...] = source + own_x
    share = jnp.sum(primal * coarse_map[0], axis=0, keepdims=True)
    product = jnp.sum(primal * region_inverse[0], axis=0, keepdims=True)
    blank = jnp.zeros((1, LANES - count), jnp.float32)
    blocks = jnp.concatenate(
        [jnp.concatenate([product[:, q * count : (q + 1) * count], blank], axis=1) for q in range(n_sub)], axis=0
    )
    me_sub = lax.axis_index("sub")
    own = jnp.sum(jnp.where(iota(blocks.shape, 0) == me_sub, blocks, 0.0), axis=0, keepdims=True)
    own = jnp.sum(own * line, axis=1, keepdims=True)
    blocks = pltpu.roll(blocks, n_sub - 1 - me_sub, 0)
    opposite = n_sub // 2
    twice = jnp.where(iota((opposite, LANES), 0) == (opposite - 1 if n_sub % 2 == 0 else opposite), 1.0, 2.0)
    squares = jnp.concatenate([residual[i] for i in range(9)], axis=0)
    squares = jnp.sum(jnp.sum(squares * squares, axis=0, keepdims=True), axis=1, keepdims=True)
    line = jnp.where(lane == count, own, jnp.where(lane == count + 1, squares, line))
    front_out[...] = jnp.zeros_like(front_out)
    front_out[:opposite, :] = blocks[:opposite] * twice
    front_out[opposite : opposite + 1, :] = line
    for i in range(share.shape[1] // LANES):
        front_out[opposite + 1 + i : opposite + 2 + i, :] = share[:, i * LANES : (i + 1) * LANES]


def solve_kernel(
    cells,
    sizes,
    count,
    source_own,
    from_x,
    from_y,
    from_z,
    inverses,
    front,
    halves,
    quarter,
    gather,
    coarsen,
    sweeps,
    base_out,
    send_out,
    buffer,
    semaphores,
):
    face = cells * cells
    rows = 3 * cells
    below_x, below_y, below_z = [faces_of(ref)[d] for d, ref in enumerate((from_x, from_y, from_z))]
    n_region, n_sub = sizes
    row_x = iota((cells, face), 0)
    source = source_own[...] - unfold(below_y, below_z, cells, False)
    source = source - jnp.concatenate(
        [jnp.where(row_x == 0, jnp.broadcast_to(below_x[c : c + 1], (cells, face)), 0.0) for c in range(3)],
        axis=0,
    )
    where_x, where_y, where_z = positions(rows, cells)
    last = cells - 1

    def tall(x):
        return jnp.concatenate([x] * 3, axis=0)

    inverse = tall(inverses[0])
    diagonal = tall(inverses[1])

    def beside_x(field):
        total = jnp.where(where_x < last, shift(field, -1, 0), 0.0)
        return total + jnp.where(where_x > 0, shift(field, 1, 0), 0.0)

    def beside(field):
        total = jnp.where(where_y < last, shift(field, -cells, 1), 0.0)
        total = total + jnp.where(where_y > 0, shift(field, cells, 1), 0.0)
        total = total + jnp.where(where_z < last, shift(field, -1, 1), 0.0)
        total = total + jnp.where(where_z > 0, shift(field, 1, 1), 0.0)
        return beside_x(field) + total

    half = cells // 2
    lane = iota((8, half**3), 1)
    half_at = split_index(lane, half, 3)
    half_scale = halves[...]

    def half_beside(field):
        total = jnp.zeros_like(field)
        for position, reach in zip(half_at, (half * half, half, 1)):
            total = total + jnp.where(position < half - 1, shift(field, -reach, 1), 0.0)
            total = total + jnp.where(position > 0, shift(field, reach, 1), 0.0)
        return total

    def half_cycle(right):
        swept = half_scale * right
        remain = times_choice(jnp.concatenate([(1.0 - damping) * right, 0.25 * swept], axis=1), coarsen[...])
        local = (2.0 - damping) * swept + 0.25 * half_scale * half_beside(swept)
        return local + times_parts(remain * quarter[...], sweeps[...])

    def correct(residual):
        swept = inverse * residual
        remain = (1.0 - damping) * residual
        right = plane_restrict(
            jnp.concatenate([remain + beside_x(swept), swept], axis=1), gather[...], cells, 3
        )
        right = jnp.concatenate([right, jnp.zeros((5, half**3), jnp.float32)], axis=0)
        remain = remain + beside(swept)
        correction, nearby = plane_prolong(half_cycle(right), cells, 3)
        return swept + correction, remain - diagonal * correction + beside_x(correction) + nearby

    field, residual = correct(source)
    swept = inverse * residual
    then = (1.0 - damping) * residual + beside(swept)
    energy = jnp.sum((source + residual) * field + swept * (residual + then), axis=0, keepdims=True)
    energy = functools.reduce(lambda a, b: a + b, [energy[:, i * LANES : (i + 1) * LANES] for i in range(face // LANES)])
    energy = jnp.sum(energy, axis=1, keepdims=True)
    message = front[...]
    at = (iota(message.shape, 0) == sizes[1] // 2) & (iota(message.shape, 1) == count)
    message = message + jnp.where(at, energy, 0.0)
    for device in range(sizes[0] * sizes[1]):
        buffer[device] = message
    (copy,) = load([(buffer, send_out)], semaphores)
    field = field + swept
    more, residual = correct(then)
    base_out[...] = field + more + inverse * residual
    copy.wait()


def ends_kernel(cells, base, lower_x, lower_y, lower_z):
    lower_x[...], lower_y[...], lower_z[...] = fold(base[...], cells, False)


def between_kernel(
    cells,
    base,
    primal_index,
    region_inverse,
    coarse_map,
    global_inverse,
    ends_out,
    region_out,
    through_out,
    global_out,
    spots_out,
    choose_out,
):
    face = cells * cells
    ends_out[...] = jnp.concatenate(fold(base[...], cells, True) + [jnp.zeros((7, face), jnp.float32)], axis=0)
    count = primal_index.shape[1]
    group, _, place, _ = decode(primal_index[...], cells)
    choose_out[...] = jnp.concatenate(
        [one_hot(iota((3 * cells, count), 0) == place), one_hot(iota((16, count), 0) == group)], axis=0
    )
    _, spot, _, lane = decode(column_of(primal_index[...]), cells)
    at = iota((count, face), 1)
    spots_out[...] = jnp.concatenate([jnp.where(at == lane, 1.0, 0.0), jnp.where(at == spot, 1.0, 0.0)], axis=1)
    blank = jnp.zeros((count, LANES - count), jnp.float32)
    for q in range(region_out.shape[0]):
        region_out[q] = jnp.concatenate([region_inverse[0, :, q * count : (q + 1) * count], blank], axis=1)
    both = both_parts(global_inverse[...])
    global_out[...] = both
    through_out[...] = times_parts(coarse_map[0], both)


def after_kernel(
    cells,
    sizes,
    count,
    received,
    base,
    ends,
    after_x,
    after_y,
    after_z,
    spots,
    choose,
    region_blocks,
    through,
    global_parts,
    direction,
    multipliers,
    residual,
    viscosity,
    multipliers_out,
    residual_out,
    velocity_out,
    pressure_out,
):
    face = cells * cells
    n_region, n_sub = sizes
    half = n_sub // 2
    columns = through.shape[1]
    me_region = lax.axis_index("region")
    everything = jnp.sum(received[...], axis=0)
    totals = [everything[half + 1 + i : half + 2 + i] for i in range(columns // LANES)]
    total = jnp.concatenate(totals, axis=1)
    added = jnp.zeros((count, LANES), jnp.float32)
    for i, part in enumerate(totals):
        added = added + through[:, i * LANES : (i + 1) * LANES] * part
    for q in range(n_sub):
        added = added + region_blocks[q] * received[me_region * n_sub + q, half : half + 1, :]
    lifted = jnp.sum(added, axis=1, keepdims=True)
    added = choice_times(choose[...], lifted * spots[...])
    velocity = base[...] + added[: 3 * cells, :face]
    upper_faces = ends[:9] + added[3 * cells : 3 * cells + 9, face:]
    for c in range(3):
        velocity_out[0, c] = velocity[c * cells : (c + 1) * cells]
    after = [after_x[...], after_y[...], after_z[...]]
    ahead = unfold(after[1][1:2], after[2][2:3], cells, True)
    where_x, where_y, where_z = positions(cells, cells)
    end = cells - 1
    field_x, field_y, field_z = [velocity[c * cells : (c + 1) * cells] for c in range(3)]
    step_x = jnp.where(where_x == end, jnp.broadcast_to(after[0][0:1], (cells, face)), shift(field_x, -1, 0))
    step_y = jnp.where(where_y == end, 0.0, shift(field_y, -cells, 1))
    step_z = jnp.where(where_z == end, 0.0, shift(field_z, -1, 1))
    step = (step_x - field_x) + (step_y - field_y) + (step_z - field_z) + ahead
    pressure_out[0] = -viscosity[0] * step
    piece = total.astype(jnp.bfloat16).astype(jnp.float32)
    row = iota((16, columns), 0)
    parts = jnp.where(row == 0, piece, jnp.where(row == 1, total - piece, 0.0)).astype(jnp.bfloat16)
    top = jnp.dot(parts, global_parts[...], preferred_element_type=jnp.float32)
    top = top[0:1, :columns] + top[1:2, :columns] + top[0:1, columns:]
    lines = received[:, half, :].reshape(n_region, n_sub, LANES)
    quadratic = jnp.zeros((n_region, n_sub, LANES), jnp.float32)
    for k in range(half):
        products = received[:, k, :].reshape(n_region, n_sub, LANES)
        quadratic = quadratic + products * pltpu.roll(lines, n_sub - 1 - k, 1)
    own_line = everything[half : half + 1]
    lane = iota((1, LANES), 1)
    quadratic = jnp.sum(quadratic.reshape(n_region * n_sub, LANES), axis=0, keepdims=True)
    curvature = quadratic + jnp.where(lane == count, own_line, 0.0)
    for i in range(columns // LANES):
        curvature = curvature + totals[i] * top[:, i * LANES : (i + 1) * LANES]
    curvature = jnp.sum(curvature, axis=1, keepdims=True)
    squares = jnp.sum(jnp.where(lane == count + 1, own_line, 0.0), axis=1, keepdims=True)
    alpha = squares / curvature
    for d in range(3):
        jump = upper_faces[3 * d : 3 * d + 3] - after[d]
        for c in range(3):
            residual_out[3 * d + c] = residual[3 * d + c] - alpha * jump[c : c + 1]
            multipliers_out[3 * d + c] = multipliers[3 * d + c] + alpha * direction[3 * d + c]


def body(
    sizes,
    multipliers,
    direction,
    residual,
    reaction,
    viscosity,
    primal_index,
    region_inverse,
    coarse_map,
    global_inverse,
):
    n_region, n_sub = sizes
    cells = reaction.shape[1]
    face = reaction.shape[2]
    count = primal_index.shape[1]
    columns = coarse_map.shape[2]
    height = -(-(n_sub // 2 + 1 + columns // LANES) // 8) * 8
    rows = 3 * cells
    shape = direction.shape
    lines = (9, 1, face)
    f32 = jnp.float32
    bf16 = jnp.bfloat16
    vmem = pl.BlockSpec(memory_space=pltpu.VMEM)
    hbm = pl.BlockSpec(memory_space=pltpu.HBM)

    def like(shape, kind=f32):
        return jax.ShapeDtypeStruct(shape, kind)

    def call(kernel, out_shape, operands, in_hbm=(), scratch=(), out_hbm=0):
        return pl.pallas_call(
            kernel,
            out_shape=out_shape,
            in_specs=[vmem] * len(operands) + [hbm] * len(in_hbm),
            out_specs=[vmem] * (len(out_shape) - out_hbm) + [hbm] * out_hbm,
            scratch_shapes=[pltpu.VMEM(x.shape, x.dtype) for x in scratch]
            + ([pltpu.SemaphoreType.DMA((len(in_hbm) + out_hbm,))] if in_hbm or out_hbm else []),
            compiler_params=pltpu.CompilerParams(vmem_limit_bytes=32 * 1024 * 1024),
        )(*operands, *[pltpu.with_memory_space_constraint(x, pltpu.HBM) for x in in_hbm])

    below_x = shifted_2(direction, "region", 1).reshape(lines)
    below_y = shifted_2(direction, "sub", DOM_Z).reshape(lines)
    below_z = shifted_2(direction, "sub", 1).reshape(lines)
    multipliers, direction, residual = [x.reshape(lines) for x in (multipliers, direction, residual)]
    half_cells = (cells // 2) ** 3
    direction, residual, source, front, inverses, halves, quarter, gather, coarsen, sweeps = call(
        functools.partial(before_kernel, cells, sizes),
        [
            like(lines),
            like(lines),
            like((rows, face)),
            like((height, LANES)),
            like((2, cells, face)),
            like((1, half_cells)),
            like((1, half_cells // 8)),
            like((2 * face, min(half_cells, LANES)), bf16),
            like((2 * half_cells, half_cells // 8), bf16),
            like((half_cells // 8, 2 * half_cells), bf16),
        ],
        [],
        [direction, residual, reaction, primal_index, region_inverse, coarse_map],
        [reaction, primal_index, region_inverse, coarse_map],
    )
    base, sent = call(
        functools.partial(solve_kernel, cells, sizes, count),
        [like((rows, face)), like((n_region * n_sub, height, LANES))],
        [source, below_x, below_y, below_z, inverses, front, halves, quarter, gather, coarsen, sweeps],
        scratch=[like((n_region * n_sub, height, LANES))],
        out_hbm=1,
    )
    received = lax.all_to_all(sent, ("region", "sub"), 0, 0, tiled=True)
    lower_x, lower_y, lower_z = call(
        functools.partial(ends_kernel, cells), [like((3, face))] * 3, [base]
    )
    after_x = shifted_2(lower_x, "region", -1)
    after_y = shifted_2(lower_y, "sub", -DOM_Z)
    after_z = shifted_2(lower_z, "sub", -1)
    ends, region_blocks, through, global_parts, spots, choose = call(
        functools.partial(between_kernel, cells),
        [
            like((16, face)),
            like((n_sub, count, LANES)),
            like((count, columns)),
            like((columns, 2 * columns), bf16),
            like((count, 2 * face)),
            like((rows + 16, count), bf16),
        ],
        [base, primal_index, region_inverse, coarse_map, global_inverse],
    )
    new_multipliers, new_residual, velocity, pressure = call(
        functools.partial(after_kernel, cells, sizes, count),
        [like(lines), like(lines), like((1, 3, cells, face)), like((1, cells, face))],
        [
            received,
            base,
            ends,
            after_x,
            after_y,
            after_z,
            spots,
            choose,
            region_blocks,
            through,
            global_parts,
            direction,
            multipliers,
            residual,
            viscosity,
        ],
    )
    return new_multipliers.reshape(shape), new_residual.reshape(shape), velocity, pressure


def solution(mesh):
    sizes = (mesh.shape["region"], mesh.shape["sub"])
    whole = P(("region", "sub"))
    in_specs = (whole,) * 6 + (P("region", "sub"), whole, P())
    return jax.shard_map(
        functools.partial(body, sizes), mesh=mesh, in_specs=in_specs, out_specs=(whole,) * 4, check_vma=False
    )
```

```python
import functools

import jax
import jax.numpy as jnp
from jax import lax
from jax.experimental import pallas as pl
from jax.experimental.pallas import tpu as pltpu
from jax.sharding import PartitionSpec as P

DOM_Z = 4
COARSE_SWEEPS = 8
LANES = 128

damping = 0.8


def shifted_2(x, axis, by):
    count = lax.axis_size(axis)
    return lax.ppermute(x, axis, [(i, (i + by) % count) for i in range(count)])


def iota(shape, dim):
    return lax.broadcasted_iota(jnp.int32, shape, dim)


def parts_of(x, count=3):
    result = []
    for step in range(count):
        piece = x.astype(jnp.bfloat16)
        result.append(piece)
        if step < count - 1:
            x = x - piece.astype(jnp.float32)
    return result


def times_choice(x, choice, count=2):
    rows = x.shape[0]
    stacked = jnp.concatenate(parts_of(x, count), axis=0)
    y = jnp.dot(stacked, choice, preferred_element_type=jnp.float32)
    return functools.reduce(lambda a, b: a + b, [y[i * rows : (i + 1) * rows] for i in range(count)])


def times_parts(x, both):
    rows = x.shape[0]
    width = both.shape[1] // 2
    y = jnp.dot(jnp.concatenate(parts_of(x, 2), axis=0), both, preferred_element_type=jnp.float32)
    return y[:rows, :width] + (y[rows:, :width] + y[:rows, width:])


def both_parts(w):
    return jnp.concatenate(parts_of(w, 2), axis=1)


def choice_times(choice, x, count=2):
    width = x.shape[1]
    stacked = jnp.concatenate(parts_of(x, count), axis=1)
    y = jnp.dot(choice, stacked, preferred_element_type=jnp.float32)
    return functools.reduce(lambda a, b: a + b, [y[:, i * width : (i + 1) * width] for i in range(count)])


def one_hot(condition):
    return jnp.where(condition, 1.0, 0.0).astype(jnp.bfloat16)


def decode(picked, cells):
    face = cells * cells
    zero = jnp.zeros_like(picked)
    one = zero + 1
    block = jnp.where(picked >= 3 * face, one, zero) + jnp.where(picked >= 6 * face, one, zero)
    rest = picked - 3 * face * block
    component = jnp.where(rest >= face, one, zero) + jnp.where(rest >= 2 * face, one, zero)
    spot = rest - face * component
    first = lax.div(spot, zero + cells)
    second = spot - first * cells
    end = cells - 1
    x = jnp.where(block == 0, end, first)
    y = jnp.where(block == 0, first, jnp.where(block == 1, end, second))
    z = jnp.where(block == 2, end, second)
    return 3 * block + component, spot, component * cells + x, y * cells + z


def faces_of(rows):
    return [jnp.concatenate([rows[3 * d + c] for c in range(3)], axis=0) for d in range(3)]


def lane_gather(x, lanes):
    return jnp.take_along_axis(x, lanes, axis=1, mode="promise_in_bounds")


def grid(cells, count, tile):
    shape = (count * cells, LANES)
    y, z = split_index(iota(shape, 1) + tile * LANES, cells, 2)
    return iota(shape, 0) & (cells - 1), y, z


def rows_of_tiles(x, rows):
    count, width = x.shape
    tiles = width // LANES
    return jnp.concatenate(
        [
            jnp.broadcast_to(x[c : c + 1, i * LANES : (i + 1) * LANES], (rows // tiles, LANES))
            for c in range(count)
            for i in range(tiles)
        ],
        axis=0,
    )


def unfold(on_y, on_z, cells, upper):
    count, face = on_y.shape
    end = cells - 1 if upper else 0
    wide_y = rows_of_tiles(on_y, cells)
    wide_z = rows_of_tiles(on_z, cells)
    tiles = []
    for tile in range(face // LANES):
        x, y, z = grid(cells, count, tile)
        start = (x * cells) & (LANES - 1)
        field = jnp.where(z == end, lane_gather(wide_z, start + y), 0.0)
        if end * cells // LANES == tile:
            field = field + jnp.where(y == end, lane_gather(wide_y, start + z), 0.0)
        tiles.append(field)
    return jnp.concatenate(tiles, axis=1)


def fold(field, cells, upper):
    face = cells * cells
    end = cells - 1 if upper else 0
    rows = LANES // cells
    tiles = [field[:, i * LANES : (i + 1) * LANES] for i in range(face // LANES)]
    x, first, second = grid(cells, 3, 0)
    on_y = lane_gather(tiles[end * cells // LANES], ((end * cells) & (LANES - 1)) + second)
    on_z = jnp.zeros_like(on_y)
    for i, tile in enumerate(tiles):
        values = lane_gather(tile, ((second * cells) & (LANES - 1)) + end)
        on_z = jnp.where(second // rows == i, values, on_z)
    here = first == (x & (rows - 1))
    faces = [jnp.concatenate([field[c * cells + end : c * cells + end + 1] for c in range(3)], axis=0)]
    for values in (on_y, on_z):
        values = jnp.where(here, values, 0.0)
        sums = [jnp.sum(values[i * rows : (i + 1) * rows], axis=0, keepdims=True) for i in range(3 * cells // rows)]
        per = face // LANES
        faces.append(
            jnp.concatenate([jnp.concatenate(sums[c * per : (c + 1) * per], axis=1) for c in range(3)], axis=0)
        )
    return faces


def column_of(line):
    count = line.shape[1]
    wide = jnp.broadcast_to(line.astype(jnp.float32), (count, count))
    diagonal = iota((count, count), 0) == iota((count, count), 1)
    return jnp.sum(jnp.where(diagonal, wide, 0.0), axis=1, keepdims=True).astype(jnp.int32)


def shift(field, by, dim):
    size = field.shape[dim]
    return pltpu.roll(field, by % size, dim)


def positions(rows, cells):
    shape = (rows, cells * cells)
    return (iota(shape, 0) & (cells - 1), *split_index(iota(shape, 1), cells, 2))


def bits(cells):
    return cells.bit_length() - 1


def split_index(flat, cells, dims):
    return [(flat >> (bits(cells) * (dims - 1 - i))) & (cells - 1) for i in range(dims)]


def plane_blocks(y, z, far_y, far_z, steps=1):
    inside = [(y >> steps) == far_y, (z >> steps) == far_z]
    nearby = [(f >> 1) + 2 * (f & 1) - 1 == b for f, b in ((y, far_y), (z, far_z))]
    same = inside[0] & inside[1]
    near = (nearby[0] & inside[1]) | (inside[0] & nearby[1])
    return one_hot(same), jnp.where(same, 2.0, jnp.where(near, 1.0, 0.0)).astype(jnp.bfloat16)


def gather_matrix(cells, steps=1):
    size = cells >> steps
    shape = (cells * cells, min(size**3, LANES))
    y, z = split_index(iota(shape, 0), cells, 2)
    _, far_y, far_z = split_index(iota(shape, 1), size, 3)
    return plane_blocks(y, z, far_y, far_z, steps)


def block_matrices(cells, blocks_first):
    half = cells // 2
    shape = (half**3, cells**3) if blocks_first else (cells**3, half**3)
    fine = split_index(iota(shape, 1 if blocks_first else 0), cells, 3)
    block = split_index(iota(shape, 0 if blocks_first else 1), half, 3)
    inside = [(f >> 1) == b for f, b in zip(fine, block)]
    nearby = [(f >> 1) + 2 * (f & 1) - 1 == b for f, b in zip(fine, block)]
    same = inside[0] & inside[1] & inside[2]
    near = (
        (nearby[0] & inside[1] & inside[2])
        | (inside[0] & nearby[1] & inside[2])
        | (inside[0] & inside[1] & nearby[2])
    )
    return one_hot(same), jnp.where(same, 3.0, jnp.where(near, 1.0, 0.0)).astype(jnp.bfloat16)


def plane_restrict(field, gather, cells, count, steps=1):
    size = cells >> steps
    width = gather.shape[1]
    per = width // (size * size) << steps
    spread_out = times_choice(field, gather)
    shape = (cells, width)
    own = split_index(iota(shape, 1), size, 3)[0] == ((iota(shape, 0) & (per - 1)) >> steps)
    group = iota(shape, 0) // per
    rows = []
    for c in range(count):
        values = jnp.where(own, spread_out[c * cells : (c + 1) * cells], 0.0)
        tiles = [
            jnp.sum(jnp.where(group == i, values, 0.0), axis=0, keepdims=True) for i in range(cells // per)
        ]
        rows.append(tiles[0] if len(tiles) == 1 else jnp.concatenate(tiles, axis=1))
    return 0.125**steps * (rows[0] if count == 1 else jnp.concatenate(rows, axis=0))


def plane_prolong(coarse, cells, count):
    half = cells // 2
    wide = rows_of_tiles(coarse[:count], cells)
    fine, nearby = [], []
    for tile in range(cells * cells // LANES):
        x, y, z = grid(cells, count, tile)
        start = ((x >> 1) * half * half) & (LANES - 1)
        half_y, half_z = y >> 1, z >> 1
        other_y, other_z = half_y + 2 * (y & 1) - 1, half_z + 2 * (z & 1) - 1
        inside_y, inside_z = (other_y & (half - 1)) == other_y, (other_z & (half - 1)) == other_z
        values = lane_gather(wide, start + half_y * half + half_z)
        beside_y = lane_gather(wide, start + (other_y & (half - 1)) * half + half_z)
        beside_z = lane_gather(wide, start + half_y * half + (other_z & (half - 1)))
        fine.append(values)
        nearby.append(2.0 * values + jnp.where(inside_y, beside_y, 0.0) + jnp.where(inside_z, beside_z, 0.0))
    return jnp.concatenate(fine, axis=1), jnp.concatenate(nearby, axis=1)


def sweep_power(scale, cells, weight):
    size = cells**3
    shape = (size, size)
    here = split_index(iota(shape, 0), cells, 3)
    there = split_index(iota(shape, 1), cells, 3)
    distance = functools.reduce(lambda a, b: a + b, [jnp.abs(a - b) for a, b in zip(here, there)])
    one = jnp.where(distance == 0, 1.0, 0.0)
    return (1.0 - damping) * one + jnp.where(distance == 1, weight * scale, 0.0), one


def square(power):
    return times_parts(power, both_parts(power))


def powers_sum(total, power):
    done = 2
    while done < COARSE_SWEEPS:
        total = total + times_parts(total, both_parts(power))
        done *= 2
        if done < COARSE_SWEEPS:
            power = square(power)
    return total


def load(pairs, semaphores):
    copies = [pltpu.make_async_copy(a, b, semaphores.at[i]) for i, (a, b) in enumerate(pairs)]
    for copy in copies:
        copy.start()
    return copies


def before_kernel(
    cells,
    sizes,
    direction_in,
    residual_in,
    reaction_in,
    primal_index_in,
    region_inverse_in,
    coarse_map_in,
    direction,
    residual,
    source_out,
    front_out,
    inverse_out,
    half_out,
    quarter_out,
    gather_out,
    coarsen_out,
    sweeps_out,
    reaction,
    primal_index,
    region_inverse,
    coarse_map,
    semaphores,
):
    copies = load(
        [
            (direction_in, direction),
            (reaction_in, reaction),
            (primal_index_in, primal_index),
            (residual_in, residual),
            (coarse_map_in, coarse_map),
            (region_inverse_in, region_inverse),
        ],
        semaphores,
    )
    face = cells * cells
    n_sub = sizes[1]
    half = cells // 2
    gather, gather_near = gather_matrix(cells)
    gather_out[...] = jnp.concatenate([gather, gather_near], axis=0)
    quarter_gather = gather_matrix(cells, 2)[0]
    coarsen, coarsen_near = block_matrices(half, False)
    coarsen_out[...] = jnp.concatenate([coarsen, coarsen_near], axis=0)
    refine = jnp.concatenate(block_matrices(half, True), axis=1)
    for copy in copies[:3]:
        copy.wait()
    react = reaction[0]
    scale = damping / (plane_restrict(react, quarter_gather, cells, 1, 2) + 6.0 * 0.0625)
    quarter_out[...] = 0.125 * scale
    power, one = sweep_power(scale, half // 2, 0.0625)
    second_power = square(power)
    diagonal = react + 6.0
    inverse_out[0] = damping / diagonal
    inverse_out[1] = diagonal
    half_scale = damping / (plane_restrict(react, gather, cells, 1) + 6.0 * 0.25)
    half_out[...] = half_scale
    faces = faces_of(direction)
    count = primal_index.shape[1]
    group, spot, _, _ = decode(column_of(primal_index[...]), cells)
    nine = jnp.concatenate(faces + [jnp.zeros((7, face), jnp.float32)], axis=0)
    gathered = choice_times(one_hot(iota((count, 16), 1) == group), nine)
    primal = jnp.sum(jnp.where(iota((count, face), 1) == spot, gathered, 0.0), axis=1, keepdims=True)
    lane = iota((1, LANES), 1)
    line = jnp.sum(
        jnp.where(iota((count, LANES), 0) == iota((count, LANES), 1), primal, 0.0), axis=0, keepdims=True
    )
    for copy in copies[3:]:
        copy.wait()
    refined = times_choice(powers_sum(one + power, second_power), refine)
    sweeps_out[...] = both_parts(
        (1.0 - damping) * refined[:, : half**3] + 0.25 * half_scale * refined[:, half**3 :]
    )
    row_x = iota((cells, face), 0)
    source = unfold(faces[1], faces[2], cells, True)
    own_x = jnp.concatenate(
        [jnp.where(row_x == cells - 1, jnp.broadcast_to(faces[0][c : c + 1], (cells, face)), 0.0) for c in range(3)],
        axis=0,
    )
    source_out[...] = source + own_x
    share = jnp.sum(primal * coarse_map[0], axis=0, keepdims=True)
    product = jnp.sum(primal * region_inverse[0], axis=0, keepdims=True)
    blank = jnp.zeros((1, LANES - count), jnp.float32)
    blocks = jnp.concatenate(
        [jnp.concatenate([product[:, q * count : (q + 1) * count], blank], axis=1) for q in range(n_sub)], axis=0
    )
    me_sub = lax.axis_index("sub")
    own = jnp.sum(jnp.where(iota(blocks.shape, 0) == me_sub, blocks, 0.0), axis=0, keepdims=True)
    own = jnp.sum(own * line, axis=1, keepdims=True)
    blocks = pltpu.roll(blocks, n_sub - 1 - me_sub, 0)
    opposite = n_sub // 2
    twice = jnp.where(iota((opposite, LANES), 0) == (opposite - 1 if n_sub % 2 == 0 else opposite), 1.0, 2.0)
    squares = jnp.concatenate([residual[i] for i in range(9)], axis=0)
    squares = jnp.sum(jnp.sum(squares * squares, axis=0, keepdims=True), axis=1, keepdims=True)
    line = jnp.where(lane == count, own, jnp.where(lane == count + 1, squares, line))
    front_out[...] = jnp.zeros_like(front_out)
    front_out[:opposite, :] = blocks[:opposite] * twice
    front_out[opposite : opposite + 1, :] = line
    for i in range(share.shape[1] // LANES):
        front_out[opposite + 1 + i : opposite + 2 + i, :] = share[:, i * LANES : (i + 1) * LANES]


def solve_kernel(
    cells,
    sizes,
    count,
    source_own,
    from_x,
    from_y,
    from_z,
    inverses,
    front,
    halves,
    quarter,
    gather,
    coarsen,
    sweeps,
    base_out,
    send_out,
    buffer,
    semaphores,
):
    face = cells * cells
    rows = 3 * cells
    below_x, below_y, below_z = [faces_of(ref)[d] for d, ref in enumerate((from_x, from_y, from_z))]
    n_region, n_sub = sizes
    row_x = iota((cells, face), 0)
    source = source_own[...] - unfold(below_y, below_z, cells, False)
    source = source - jnp.concatenate(
        [jnp.where(row_x == 0, jnp.broadcast_to(below_x[c : c + 1], (cells, face)), 0.0) for c in range(3)],
        axis=0,
    )
    where_x, where_y, where_z = positions(rows, cells)
    last = cells - 1

    def tall(x):
        return jnp.concatenate([x] * 3, axis=0)

    inverse = tall(inverses[0])
    diagonal = tall(inverses[1])

    def beside_x(field):
        total = jnp.where(where_x < last, shift(field, -1, 0), 0.0)
        return total + jnp.where(where_x > 0, shift(field, 1, 0), 0.0)

    def beside(field):
        total = jnp.where(where_y < last, shift(field, -cells, 1), 0.0)
        total = total + jnp.where(where_y > 0, shift(field, cells, 1), 0.0)
        total = total + jnp.where(where_z < last, shift(field, -1, 1), 0.0)
        total = total + jnp.where(where_z > 0, shift(field, 1, 1), 0.0)
        return beside_x(field) + total

    half = cells // 2
    lane = iota((8, half**3), 1)
    half_at = split_index(lane, half, 3)
    half_scale = halves[...]

    def half_beside(field):
        total = jnp.zeros_like(field)
        for position, reach in zip(half_at, (half * half, half, 1)):
            total = total + jnp.where(position < half - 1, shift(field, -reach, 1), 0.0)
            total = total + jnp.where(position > 0, shift(field, reach, 1), 0.0)
        return total

    def half_cycle(right):
        swept = half_scale * right
        remain = times_choice(jnp.concatenate([(1.0 - damping) * right, 0.25 * swept], axis=1), coarsen[...])
        local = (2.0 - damping) * swept + 0.25 * half_scale * half_beside(swept)
        return local + times_parts(remain * quarter[...], sweeps[...])

    def correct(residual):
        swept = inverse * residual
        remain = (1.0 - damping) * residual
        right = plane_restrict(
            jnp.concatenate([remain + beside_x(swept), swept], axis=1), gather[...], cells, 3
        )
        right = jnp.concatenate([right, jnp.zeros((5, half**3), jnp.float32)], axis=0)
        remain = remain + beside(swept)
        correction, nearby = plane_prolong(half_cycle(right), cells, 3)
        return swept + correction, remain - diagonal * correction + beside_x(correction) + nearby

    field, residual = correct(source)
    swept = inverse * residual
    then = (1.0 - damping) * residual + beside(swept)
    energy = jnp.sum((source + residual) * field + swept * (residual + then), axis=0, keepdims=True)
    energy = functools.reduce(lambda a, b: a + b, [energy[:, i * LANES : (i + 1) * LANES] for i in range(face // LANES)])
    energy = jnp.sum(energy, axis=1, keepdims=True)
    message = front[...]
    at = (iota(message.shape, 0) == sizes[1] // 2) & (iota(message.shape, 1) == count)
    message = message + jnp.where(at, energy, 0.0)
    for device in range(sizes[0] * sizes[1]):
        buffer[device] = message
    (copy,) = load([(buffer, send_out)], semaphores)
    field = field + swept
    more, residual = correct(then)
    base_out[...] = field + more + inverse * residual
    copy.wait()


def ends_kernel(cells, base, lower_x, lower_y, lower_z):
    lower_x[...], lower_y[...], lower_z[...] = fold(base[...], cells, False)


def between_kernel(
    cells,
    base,
    primal_index,
    region_inverse,
    coarse_map,
    global_inverse,
    ends_out,
    region_out,
    through_out,
    global_out,
    field_map_out,
    face_map_out,
    ahead_map_out,
):
    face = cells * cells
    ends_out[...] = jnp.concatenate(fold(base[...], cells, True) + [jnp.zeros((7, face), jnp.float32)], axis=0)
    count = primal_index.shape[1]
    group, _, place, _ = decode(primal_index[...], cells)
    choose = jnp.concatenate(
        [one_hot(iota((3 * cells, count), 0) == place), one_hot(iota((16, count), 0) == group)], axis=0
    )
    _, spot, _, lane = decode(column_of(primal_index[...]), cells)
    at = iota((count, face), 1)
    number = iota((count, 2 * face), 0) + 1
    spots = jnp.where(jnp.concatenate([at == lane, at == spot], axis=1), number, 0).astype(jnp.float32)
    maps = choice_times(choose, spots).astype(jnp.int32)
    maps = jnp.where(maps > 0, maps - 1, LANES - 1)
    field_map = maps[: 3 * cells, :face]
    field_map_out[...] = field_map
    face_map_out[...] = maps[3 * cells :, face:]
    _, where_y, where_z = positions(cells, cells)
    end = cells - 1
    ahead_map_out[...] = jnp.concatenate(
        [
            jnp.where(where_y == end, LANES - 1, shift(field_map[cells : 2 * cells], -cells, 1)),
            jnp.where(where_z == end, LANES - 1, shift(field_map[2 * cells :], -1, 1)),
        ],
        axis=0,
    )
    blank = jnp.zeros((count, LANES - count), jnp.float32)
    for q in range(region_out.shape[0]):
        region_out[q] = jnp.concatenate([region_inverse[0, :, q * count : (q + 1) * count], blank], axis=1)
    both = both_parts(global_inverse[...])
    global_out[...] = both
    through_out[...] = times_parts(coarse_map[0], both)


def after_kernel(
    cells,
    sizes,
    count,
    received,
    base,
    ends,
    after_x,
    after_y,
    after_z,
    field_map,
    face_map,
    ahead_map,
    region_blocks,
    through,
    global_parts,
    direction,
    multipliers,
    residual,
    viscosity,
    multipliers_out,
    residual_out,
    velocity_out,
    pressure_out,
):
    face = cells * cells
    n_region, n_sub = sizes
    half = n_sub // 2
    columns = through.shape[1]
    me_region = lax.axis_index("region")
    everything = jnp.sum(received[...], axis=0)
    totals = [everything[half + 1 + i : half + 2 + i] for i in range(columns // LANES)]
    after = [after_x[...], after_y[...], after_z[...]]
    field = base[...]
    field_x, field_y, field_z = [field[c * cells : (c + 1) * cells] for c in range(3)]
    where_x, where_y, where_z = positions(cells, cells)
    end = cells - 1
    step = jnp.where(where_x == end, jnp.broadcast_to(after[0][0:1], (cells, face)), shift(field_x, -1, 0)) - field_x
    step = step + jnp.where(where_y == end, 0.0, shift(field_y, -cells, 1)) - field_y
    step = step + jnp.where(where_z == end, 0.0, shift(field_z, -1, 1)) - field_z
    step = step + unfold(after[1][1:2], after[2][2:3], cells, True)
    jump = ends[:9] - jnp.concatenate(after, axis=0)
    added = jnp.zeros((count, LANES), jnp.float32)
    for i, part in enumerate(totals):
        added = added + through[:, i * LANES : (i + 1) * LANES] * part
    for q in range(n_sub):
        added = added + region_blocks[q] * received[me_region * n_sub + q, half : half + 1, :]
    lifted = jnp.sum(added, axis=1, keepdims=True)
    own_lane = iota((count, LANES), 0) == iota((count, LANES), 1)
    lifted = jnp.sum(jnp.where(own_lane, lifted, 0.0), axis=0, keepdims=True)

    def placed(numbers):
        wide = jnp.broadcast_to(lifted, (numbers.shape[0], LANES))
        return jnp.concatenate(
            [lane_gather(wide, numbers[:, i * LANES : (i + 1) * LANES]) for i in range(face // LANES)], axis=1
        )

    added = placed(field_map)
    ahead = placed(ahead_map)
    velocity = field + added
    for c in range(3):
        velocity_out[0, c] = velocity[c * cells : (c + 1) * cells]
    added_x = added[:cells]
    step = step + jnp.where(where_x == end, 0.0, shift(added_x, -1, 0)) - added_x
    step = step + ahead[:cells] - added[cells : 2 * cells] + ahead[cells:] - added[2 * cells :]
    pressure_out[0] = -viscosity[0] * step
    jump = jump + placed(face_map)[:9]
    total = jnp.concatenate(totals, axis=1)
    piece = total.astype(jnp.bfloat16).astype(jnp.float32)
    row = iota((16, columns), 0)
    parts = jnp.where(row == 0, piece, jnp.where(row == 1, total - piece, 0.0)).astype(jnp.bfloat16)
    top = jnp.dot(parts, global_parts[...], preferred_element_type=jnp.float32)
    top = top[0:1, :columns] + top[1:2, :columns] + top[0:1, columns:]
    lines = received[:, half, :].reshape(n_region, n_sub, LANES)
    quadratic = jnp.zeros((n_region, n_sub, LANES), jnp.float32)
    for k in range(half):
        products = received[:, k, :].reshape(n_region, n_sub, LANES)
        quadratic = quadratic + products * pltpu.roll(lines, n_sub - 1 - k, 1)
    own_line = everything[half : half + 1]
    lane = iota((1, LANES), 1)
    quadratic = jnp.sum(quadratic.reshape(n_region * n_sub, LANES), axis=0, keepdims=True)
    curvature = quadratic + jnp.where(lane == count, own_line, 0.0)
    for i in range(columns // LANES):
        curvature = curvature + totals[i] * top[:, i * LANES : (i + 1) * LANES]
    curvature = jnp.sum(curvature, axis=1, keepdims=True)
    squares = jnp.sum(jnp.where(lane == count + 1, own_line, 0.0), axis=1, keepdims=True)
    alpha = squares / curvature
    for i in range(9):
        residual_out[i] = residual[i] - alpha * jump[i : i + 1]
        multipliers_out[i] = multipliers[i] + alpha * direction[i]


def body(
    sizes,
    multipliers,
    direction,
    residual,
    reaction,
    viscosity,
    primal_index,
    region_inverse,
    coarse_map,
    global_inverse,
):
    n_region, n_sub = sizes
    cells = reaction.shape[1]
    face = reaction.shape[2]
    count = primal_index.shape[1]
    columns = coarse_map.shape[2]
    height = -(-(n_sub // 2 + 1 + columns // LANES) // 8) * 8
    rows = 3 * cells
    shape = direction.shape
    lines = (9, 1, face)
    f32 = jnp.float32
    bf16 = jnp.bfloat16
    vmem = pl.BlockSpec(memory_space=pltpu.VMEM)
    hbm = pl.BlockSpec(memory_space=pltpu.HBM)

    def like(shape, kind=f32):
        return jax.ShapeDtypeStruct(shape, kind)

    def call(kernel, out_shape, operands, in_hbm=(), scratch=(), out_hbm=0):
        return pl.pallas_call(
            kernel,
            out_shape=out_shape,
            in_specs=[vmem] * len(operands) + [hbm] * len(in_hbm),
            out_specs=[vmem] * (len(out_shape) - out_hbm) + [hbm] * out_hbm,
            scratch_shapes=[pltpu.VMEM(x.shape, x.dtype) for x in scratch]
            + ([pltpu.SemaphoreType.DMA((len(in_hbm) + out_hbm,))] if in_hbm or out_hbm else []),
            compiler_params=pltpu.CompilerParams(vmem_limit_bytes=32 * 1024 * 1024),
        )(*operands, *[pltpu.with_memory_space_constraint(x, pltpu.HBM) for x in in_hbm])

    below_x = shifted_2(direction, "region", 1).reshape(lines)
    below_y = shifted_2(direction, "sub", DOM_Z).reshape(lines)
    below_z = shifted_2(direction, "sub", 1).reshape(lines)
    multipliers, direction, residual = [x.reshape(lines) for x in (multipliers, direction, residual)]
    half_cells = (cells // 2) ** 3
    direction, residual, source, front, inverses, halves, quarter, gather, coarsen, sweeps = call(
        functools.partial(before_kernel, cells, sizes),
        [
            like(lines),
            like(lines),
            like((rows, face)),
            like((height, LANES)),
            like((2, cells, face)),
            like((1, half_cells)),
            like((1, half_cells // 8)),
            like((2 * face, min(half_cells, LANES)), bf16),
            like((2 * half_cells, half_cells // 8), bf16),
            like((half_cells // 8, 2 * half_cells), bf16),
        ],
        [],
        [direction, residual, reaction, primal_index, region_inverse, coarse_map],
        [reaction, primal_index, region_inverse, coarse_map],
    )
    base, sent = call(
        functools.partial(solve_kernel, cells, sizes, count),
        [like((rows, face)), like((n_region * n_sub, height, LANES))],
        [source, below_x, below_y, below_z, inverses, front, halves, quarter, gather, coarsen, sweeps],
        scratch=[like((n_region * n_sub, height, LANES))],
        out_hbm=1,
    )
    received = lax.all_to_all(sent, ("region", "sub"), 0, 0, tiled=True)
    lower_x, lower_y, lower_z = call(
        functools.partial(ends_kernel, cells), [like((3, face))] * 3, [base]
    )
    after_x = shifted_2(lower_x, "region", -1)
    after_y = shifted_2(lower_y, "sub", -DOM_Z)
    after_z = shifted_2(lower_z, "sub", -1)
    ends, region_blocks, through, global_parts, field_map, face_map, ahead_map = call(
        functools.partial(between_kernel, cells),
        [
            like((16, face)),
            like((n_sub, count, LANES)),
            like((count, columns)),
            like((columns, 2 * columns), bf16),
            like((rows, face), jnp.int32),
            like((16, face), jnp.int32),
            like((2 * cells, face), jnp.int32),
        ],
        [base, primal_index, region_inverse, coarse_map, global_inverse],
    )
    new_multipliers, new_residual, velocity, pressure = call(
        functools.partial(after_kernel, cells, sizes, count),
        [like(lines), like(lines), like((1, 3, cells, face)), like((1, cells, face))],
        [
            received,
            base,
            ends,
            after_x,
            after_y,
            after_z,
            field_map,
            face_map,
            ahead_map,
            region_blocks,
            through,
            global_parts,
            direction,
            multipliers,
            residual,
            viscosity,
        ],
    )
    return new_multipliers.reshape(shape), new_residual.reshape(shape), velocity, pressure


def solution(mesh):
    sizes = (mesh.shape["region"], mesh.shape["sub"])
    whole = P(("region", "sub"))
    in_specs = (whole,) * 6 + (P("region", "sub"), whole, P())
    return jax.shard_map(
        functools.partial(body, sizes), mesh=mesh, in_specs=in_specs, out_specs=(whole,) * 4, check_vma=False
    )
```

```python
import functools

import jax
import jax.numpy as jnp
from jax import lax
from jax.experimental import pallas as pl
from jax.experimental.pallas import tpu as pltpu
from jax.sharding import PartitionSpec as P

DOM_Z = 4
COARSE_SWEEPS = 8
LANES = 128

damping = 0.8


def shifted_2(x, axis, by):
    count = lax.axis_size(axis)
    return lax.ppermute(x, axis, [(i, (i + by) % count) for i in range(count)])


def iota(shape, dim):
    return lax.broadcasted_iota(jnp.int32, shape, dim)


def parts_of(x, count=3):
    result = []
    for step in range(count):
        piece = x.astype(jnp.bfloat16)
        result.append(piece)
        if step < count - 1:
            x = x - piece.astype(jnp.float32)
    return result


def times_choice(x, choice, count=2):
    rows = x.shape[0]
    stacked = jnp.concatenate(parts_of(x, count), axis=0)
    y = jnp.dot(stacked, choice, preferred_element_type=jnp.float32)
    return functools.reduce(lambda a, b: a + b, [y[i * rows : (i + 1) * rows] for i in range(count)])


def times_parts(x, both):
    rows = x.shape[0]
    width = both.shape[1] // 2
    y = jnp.dot(jnp.concatenate(parts_of(x, 2), axis=0), both, preferred_element_type=jnp.float32)
    return y[:rows, :width] + (y[rows:, :width] + y[:rows, width:])


def stacked_parts(w):
    first, second = parts_of(w, 2)
    return jnp.concatenate([first, first, second, jnp.zeros_like(first)], axis=0)


def times_stacked(x, stacked):
    first, second = parts_of(x, 2)
    left = iota(x.shape, 1) < x.shape[1] // 2
    zero = jnp.zeros_like(x)
    pair = jnp.where(left, first.astype(jnp.float32), second.astype(jnp.float32))
    other = jnp.where(left, first.astype(jnp.float32), zero)
    pair = jnp.concatenate([pair, other], axis=1).astype(jnp.bfloat16)
    return jnp.dot(pair, stacked, preferred_element_type=jnp.float32)


def both_parts(w):
    return jnp.concatenate(parts_of(w, 2), axis=1)


def choice_times(choice, x, count=2):
    width = x.shape[1]
    stacked = jnp.concatenate(parts_of(x, count), axis=1)
    y = jnp.dot(choice, stacked, preferred_element_type=jnp.float32)
    return functools.reduce(lambda a, b: a + b, [y[:, i * width : (i + 1) * width] for i in range(count)])


def one_hot(condition):
    return jnp.where(condition, 1.0, 0.0).astype(jnp.bfloat16)


def decode(picked, cells):
    face = cells * cells
    zero = jnp.zeros_like(picked)
    one = zero + 1
    block = jnp.where(picked >= 3 * face, one, zero) + jnp.where(picked >= 6 * face, one, zero)
    rest = picked - 3 * face * block
    component = jnp.where(rest >= face, one, zero) + jnp.where(rest >= 2 * face, one, zero)
    spot = rest - face * component
    first = lax.div(spot, zero + cells)
    second = spot - first * cells
    end = cells - 1
    x = jnp.where(block == 0, end, first)
    y = jnp.where(block == 0, first, jnp.where(block == 1, end, second))
    z = jnp.where(block == 2, end, second)
    return 3 * block + component, spot, component * cells + x, y * cells + z


def faces_of(rows):
    return [jnp.concatenate([rows[3 * d + c] for c in range(3)], axis=0) for d in range(3)]


def lane_gather(x, lanes):
    return jnp.take_along_axis(x, lanes, axis=1, mode="promise_in_bounds")


def grid(cells, count, tile):
    shape = (count * cells, LANES)
    y, z = split_index(iota(shape, 1) + tile * LANES, cells, 2)
    return iota(shape, 0) & (cells - 1), y, z


def rows_of_tiles(x, rows):
    count, width = x.shape
    tiles = width // LANES
    return jnp.concatenate(
        [
            jnp.broadcast_to(x[c : c + 1, i * LANES : (i + 1) * LANES], (rows // tiles, LANES))
            for c in range(count)
            for i in range(tiles)
        ],
        axis=0,
    )


def unfold(on_y, on_z, cells, upper):
    count, face = on_y.shape
    end = cells - 1 if upper else 0
    wide_y = rows_of_tiles(on_y, cells)
    wide_z = rows_of_tiles(on_z, cells)
    tiles = []
    for tile in range(face // LANES):
        x, y, z = grid(cells, count, tile)
        start = (x * cells) & (LANES - 1)
        field = jnp.where(z == end, lane_gather(wide_z, start + y), 0.0)
        if end * cells // LANES == tile:
            field = field + jnp.where(y == end, lane_gather(wide_y, start + z), 0.0)
        tiles.append(field)
    return jnp.concatenate(tiles, axis=1)


def fold(field, cells, upper):
    face = cells * cells
    end = cells - 1 if upper else 0
    rows = LANES // cells
    tiles = [field[:, i * LANES : (i + 1) * LANES] for i in range(face // LANES)]
    x, first, second = grid(cells, 3, 0)
    on_y = lane_gather(tiles[end * cells // LANES], ((end * cells) & (LANES - 1)) + second)
    on_z = jnp.zeros_like(on_y)
    for i, tile in enumerate(tiles):
        values = lane_gather(tile, ((second * cells) & (LANES - 1)) + end)
        on_z = jnp.where(second // rows == i, values, on_z)
    here = first == (x & (rows - 1))
    faces = [jnp.concatenate([field[c * cells + end : c * cells + end + 1] for c in range(3)], axis=0)]
    for values in (on_y, on_z):
        values = jnp.where(here, values, 0.0)
        sums = [jnp.sum(values[i * rows : (i + 1) * rows], axis=0, keepdims=True) for i in range(3 * cells // rows)]
        per = face // LANES
        faces.append(
            jnp.concatenate([jnp.concatenate(sums[c * per : (c + 1) * per], axis=1) for c in range(3)], axis=0)
        )
    return faces


def column_of(line):
    count = line.shape[1]
    wide = jnp.broadcast_to(line.astype(jnp.float32), (count, count))
    diagonal = iota((count, count), 0) == iota((count, count), 1)
    return jnp.sum(jnp.where(diagonal, wide, 0.0), axis=1, keepdims=True).astype(jnp.int32)


def shift(field, by, dim):
    size = field.shape[dim]
    return pltpu.roll(field, by % size, dim)


def positions(rows, cells):
    shape = (rows, cells * cells)
    return (iota(shape, 0) & (cells - 1), *split_index(iota(shape, 1), cells, 2))


def bits(cells):
    return cells.bit_length() - 1


def split_index(flat, cells, dims):
    return [(flat >> (bits(cells) * (dims - 1 - i))) & (cells - 1) for i in range(dims)]


def plane_blocks(y, z, far_y, far_z, steps=1):
    inside = [(y >> steps) == far_y, (z >> steps) == far_z]
    nearby = [(f >> 1) + 2 * (f & 1) - 1 == b for f, b in ((y, far_y), (z, far_z))]
    same = inside[0] & inside[1]
    near = (nearby[0] & inside[1]) | (inside[0] & nearby[1])
    return one_hot(same), jnp.where(same, 2.0, jnp.where(near, 1.0, 0.0)).astype(jnp.bfloat16)


def gather_matrix(cells, steps=1):
    size = cells >> steps
    shape = (cells * cells, min(size**3, LANES))
    y, z = split_index(iota(shape, 0), cells, 2)
    _, far_y, far_z = split_index(iota(shape, 1), size, 3)
    return plane_blocks(y, z, far_y, far_z, steps)


def block_matrices(cells, blocks_first):
    half = cells // 2
    shape = (half**3, cells**3) if blocks_first else (cells**3, half**3)
    fine = split_index(iota(shape, 1 if blocks_first else 0), cells, 3)
    block = split_index(iota(shape, 0 if blocks_first else 1), half, 3)
    inside = [(f >> 1) == b for f, b in zip(fine, block)]
    nearby = [(f >> 1) + 2 * (f & 1) - 1 == b for f, b in zip(fine, block)]
    same = inside[0] & inside[1] & inside[2]
    near = (
        (nearby[0] & inside[1] & inside[2])
        | (inside[0] & nearby[1] & inside[2])
        | (inside[0] & inside[1] & nearby[2])
    )
    return one_hot(same), jnp.where(same, 3.0, jnp.where(near, 1.0, 0.0)).astype(jnp.bfloat16)


def plane_restrict(field, gather, cells, count, steps=1):
    size = cells >> steps
    width = gather.shape[1]
    per = width // (size * size) << steps
    spread_out = times_choice(field, gather)
    shape = (cells, width)
    own = split_index(iota(shape, 1), size, 3)[0] == ((iota(shape, 0) & (per - 1)) >> steps)
    group = iota(shape, 0) // per
    rows = []
    for c in range(count):
        values = jnp.where(own, spread_out[c * cells : (c + 1) * cells], 0.0)
        tiles = [
            jnp.sum(jnp.where(group == i, values, 0.0), axis=0, keepdims=True) for i in range(cells // per)
        ]
        rows.append(tiles[0] if len(tiles) == 1 else jnp.concatenate(tiles, axis=1))
    return 0.125**steps * (rows[0] if count == 1 else jnp.concatenate(rows, axis=0))


def plane_prolong(coarse, cells, count):
    half = cells // 2
    wide = rows_of_tiles(coarse[:count], cells)
    fine, nearby = [], []
    for tile in range(cells * cells // LANES):
        x, y, z = grid(cells, count, tile)
        start = ((x >> 1) * half * half) & (LANES - 1)
        half_y, half_z = y >> 1, z >> 1
        other_y, other_z = half_y + 2 * (y & 1) - 1, half_z + 2 * (z & 1) - 1
        inside_y, inside_z = (other_y & (half - 1)) == other_y, (other_z & (half - 1)) == other_z
        values = lane_gather(wide, start + half_y * half + half_z)
        beside_y = lane_gather(wide, start + (other_y & (half - 1)) * half + half_z)
        beside_z = lane_gather(wide, start + half_y * half + (other_z & (half - 1)))
        fine.append(values)
        nearby.append(2.0 * values + jnp.where(inside_y, beside_y, 0.0) + jnp.where(inside_z, beside_z, 0.0))
    return jnp.concatenate(fine, axis=1), jnp.concatenate(nearby, axis=1)


def sweep_power(scale, cells, weight):
    size = cells**3
    shape = (size, size)
    here = split_index(iota(shape, 0), cells, 3)
    there = split_index(iota(shape, 1), cells, 3)
    distance = functools.reduce(lambda a, b: a + b, [jnp.abs(a - b) for a, b in zip(here, there)])
    one = jnp.where(distance == 0, 1.0, 0.0)
    return (1.0 - damping) * one + jnp.where(distance == 1, weight * scale, 0.0), one


def square(power):
    return times_parts(power, both_parts(power))


def powers_sum(total, power):
    done = 2
    while done < COARSE_SWEEPS:
        total = total + times_parts(total, both_parts(power))
        done *= 2
        if done < COARSE_SWEEPS:
            power = square(power)
    return total


def load(pairs, semaphores):
    copies = [pltpu.make_async_copy(a, b, semaphores.at[i]) for i, (a, b) in enumerate(pairs)]
    for copy in copies:
        copy.start()
    return copies


def before_kernel(
    cells,
    sizes,
    direction_in,
    residual_in,
    reaction_in,
    primal_index_in,
    region_inverse_in,
    coarse_map_in,
    direction,
    residual,
    source_out,
    front_out,
    inverse_out,
    half_out,
    quarter_out,
    gather_out,
    coarsen_out,
    sweeps_out,
    reaction,
    primal_index,
    region_inverse,
    coarse_map,
    semaphores,
):
    copies = load(
        [
            (direction_in, direction),
            (reaction_in, reaction),
            (primal_index_in, primal_index),
            (residual_in, residual),
            (coarse_map_in, coarse_map),
            (region_inverse_in, region_inverse),
        ],
        semaphores,
    )
    face = cells * cells
    n_sub = sizes[1]
    half = cells // 2
    gather, gather_near = gather_matrix(cells)
    gather_out[...] = jnp.concatenate([gather, gather_near], axis=0)
    quarter_gather = gather_matrix(cells, 2)[0]
    coarsen, coarsen_near = block_matrices(half, False)
    coarsen_out[...] = jnp.concatenate([jnp.concatenate([x, x], axis=1) for x in (coarsen, coarsen_near)], axis=0)
    refine = jnp.concatenate(block_matrices(half, True), axis=1)
    for copy in copies[:3]:
        copy.wait()
    react = reaction[0]
    scale = damping / (plane_restrict(react, quarter_gather, cells, 1, 2) + 6.0 * 0.0625)
    quarter_out[...] = 0.125 * jnp.concatenate([scale, scale], axis=1)
    power, one = sweep_power(scale, half // 2, 0.0625)
    second_power = square(power)
    diagonal = react + 6.0
    inverse_out[0] = damping / diagonal
    inverse_out[1] = diagonal
    half_scale = damping / (plane_restrict(react, gather, cells, 1) + 6.0 * 0.25)
    half_out[...] = half_scale
    faces = faces_of(direction)
    count = primal_index.shape[1]
    group, spot, _, _ = decode(column_of(primal_index[...]), cells)
    nine = jnp.concatenate(faces + [jnp.zeros((7, face), jnp.float32)], axis=0)
    gathered = choice_times(one_hot(iota((count, 16), 1) == group), nine)
    primal = jnp.sum(jnp.where(iota((count, face), 1) == spot, gathered, 0.0), axis=1, keepdims=True)
    lane = iota((1, LANES), 1)
    line = jnp.sum(
        jnp.where(iota((count, LANES), 0) == iota((count, LANES), 1), primal, 0.0), axis=0, keepdims=True
    )
    for copy in copies[3:]:
        copy.wait()
    refined = times_choice(powers_sum(one + power, second_power), refine)
    sweeps_out[...] = stacked_parts(
        (1.0 - damping) * refined[:, : half**3] + 0.25 * half_scale * refined[:, half**3 :]
    )
    row_x = iota((cells, face), 0)
    source = unfold(faces[1], faces[2], cells, True)
    own_x = jnp.concatenate(
        [jnp.where(row_x == cells - 1, jnp.broadcast_to(faces[0][c : c + 1], (cells, face)), 0.0) for c in range(3)],
        axis=0,
    )
    source_out[...] = source + own_x
    share = jnp.sum(primal * coarse_map[0], axis=0, keepdims=True)
    product = jnp.sum(primal * region_inverse[0], axis=0, keepdims=True)
    blank = jnp.zeros((1, LANES - count), jnp.float32)
    blocks = jnp.concatenate(
        [jnp.concatenate([product[:, q * count : (q + 1) * count], blank], axis=1) for q in range(n_sub)], axis=0
    )
    me_sub = lax.axis_index("sub")
    own = jnp.sum(jnp.where(iota(blocks.shape, 0) == me_sub, blocks, 0.0), axis=0, keepdims=True)
    own = jnp.sum(own * line, axis=1, keepdims=True)
    blocks = pltpu.roll(blocks, n_sub - 1 - me_sub, 0)
    opposite = n_sub // 2
    twice = jnp.where(iota((opposite, LANES), 0) == (opposite - 1 if n_sub % 2 == 0 else opposite), 1.0, 2.0)
    squares = jnp.concatenate([residual[i] for i in range(9)], axis=0)
    squares = jnp.sum(jnp.sum(squares * squares, axis=0, keepdims=True), axis=1, keepdims=True)
    line = jnp.where(lane == count, own, jnp.where(lane == count + 1, squares, line))
    front_out[...] = jnp.zeros_like(front_out)
    front_out[:opposite, :] = blocks[:opposite] * twice
    front_out[opposite : opposite + 1, :] = line
    for i in range(share.shape[1] // LANES):
        front_out[opposite + 1 + i : opposite + 2 + i, :] = share[:, i * LANES : (i + 1) * LANES]


def solve_kernel(
    cells,
    sizes,
    count,
    source_own,
    from_x,
    from_y,
    from_z,
    inverses,
    front,
    halves,
    quarter,
    gather,
    coarsen,
    sweeps,
    base_out,
    send_out,
    buffer,
    semaphores,
):
    face = cells * cells
    rows = 3 * cells
    below_x, below_y, below_z = [faces_of(ref)[d] for d, ref in enumerate((from_x, from_y, from_z))]
    n_region, n_sub = sizes
    row_x = iota((cells, face), 0)
    source = source_own[...] - unfold(below_y, below_z, cells, False)
    source = source - jnp.concatenate(
        [jnp.where(row_x == 0, jnp.broadcast_to(below_x[c : c + 1], (cells, face)), 0.0) for c in range(3)],
        axis=0,
    )
    where_x, where_y, where_z = positions(rows, cells)
    last = cells - 1

    def tall(x):
        return jnp.concatenate([x] * 3, axis=0)

    inverse = tall(inverses[0])
    diagonal = tall(inverses[1])

    def beside_x(field):
        total = jnp.where(where_x < last, shift(field, -1, 0), 0.0)
        return total + jnp.where(where_x > 0, shift(field, 1, 0), 0.0)

    def beside(field):
        total = jnp.where(where_y < last, shift(field, -cells, 1), 0.0)
        total = total + jnp.where(where_y > 0, shift(field, cells, 1), 0.0)
        total = total + jnp.where(where_z < last, shift(field, -1, 1), 0.0)
        total = total + jnp.where(where_z > 0, shift(field, 1, 1), 0.0)
        return beside_x(field) + total

    half = cells // 2
    lane = iota((8, half**3), 1)
    half_at = split_index(lane, half, 3)
    half_scale = halves[...]

    def half_beside(field):
        total = jnp.zeros_like(field)
        for position, reach in zip(half_at, (half * half, half, 1)):
            total = total + jnp.where(position < half - 1, shift(field, -reach, 1), 0.0)
            total = total + jnp.where(position > 0, shift(field, reach, 1), 0.0)
        return total

    def half_cycle(right):
        swept = half_scale * right
        remain = times_choice(jnp.concatenate([(1.0 - damping) * right, 0.25 * swept], axis=1), coarsen[...])
        local = (2.0 - damping) * swept + 0.25 * half_scale * half_beside(swept)
        return local + times_stacked(remain * quarter[...], sweeps[...])

    def correct(residual):
        swept = inverse * residual
        remain = (1.0 - damping) * residual
        right = plane_restrict(
            jnp.concatenate([remain + beside_x(swept), swept], axis=1), gather[...], cells, 3
        )
        right = jnp.concatenate([right, jnp.zeros((5, half**3), jnp.float32)], axis=0)
        remain = remain + beside(swept)
        correction, nearby = plane_prolong(half_cycle(right), cells, 3)
        return swept + correction, remain - diagonal * correction + beside_x(correction) + nearby

    field, residual = correct(source)
    swept = inverse * residual
    ahead = jnp.where(where_x < last, shift(swept, -1, 0), 0.0)
    ahead = ahead + jnp.where(where_y < last, shift(swept, -cells, 1), 0.0)
    ahead = ahead + jnp.where(where_z < last, shift(swept, -1, 1), 0.0)
    energy = (source + residual) * field + swept * (2.0 * residual - diagonal * swept + 2.0 * ahead)
    energy = jnp.sum(energy, axis=0, keepdims=True)
    energy = functools.reduce(lambda a, b: a + b, [energy[:, i * LANES : (i + 1) * LANES] for i in range(face // LANES)])
    energy = jnp.sum(energy, axis=1, keepdims=True)
    message = front[...]
    at = (iota(message.shape, 0) == sizes[1] // 2) & (iota(message.shape, 1) == count)
    message = message + jnp.where(at, energy, 0.0)
    for device in range(sizes[0] * sizes[1]):
        buffer[device] = message
    (copy,) = load([(buffer, send_out)], semaphores)
    then = (1.0 - damping) * residual + beside(swept)
    field = field + swept
    more, residual = correct(then)
    base_out[...] = field + more + inverse * residual
    copy.wait()


def ends_kernel(cells, base, lower_x, lower_y, lower_z):
    lower_x[...], lower_y[...], lower_z[...] = fold(base[...], cells, False)


def between_kernel(
    cells,
    base,
    primal_index,
    region_inverse,
    coarse_map,
    global_inverse,
    ends_out,
    region_out,
    through_out,
    global_out,
    field_map_out,
    face_map_out,
    ahead_map_out,
):
    face = cells * cells
    ends_out[...] = jnp.concatenate(fold(base[...], cells, True) + [jnp.zeros((7, face), jnp.float32)], axis=0)
    count = primal_index.shape[1]
    group, _, place, _ = decode(primal_index[...], cells)
    choose = jnp.concatenate(
        [one_hot(iota((3 * cells, count), 0) == place), one_hot(iota((16, count), 0) == group)], axis=0
    )
    _, spot, _, lane = decode(column_of(primal_index[...]), cells)
    at = iota((count, face), 1)
    number = iota((count, 2 * face), 0) + 1
    spots = jnp.where(jnp.concatenate([at == lane, at == spot], axis=1), number, 0).astype(jnp.float32)
    maps = choice_times(choose, spots).astype(jnp.int32)
    maps = jnp.where(maps > 0, maps - 1, LANES - 1)
    field_map = maps[: 3 * cells, :face]
    field_map_out[...] = field_map
    face_map_out[...] = maps[3 * cells :, face:]
    _, where_y, where_z = positions(cells, cells)
    end = cells - 1
    ahead_map_out[...] = jnp.concatenate(
        [
            jnp.where(where_y == end, LANES - 1, shift(field_map[cells : 2 * cells], -cells, 1)),
            jnp.where(where_z == end, LANES - 1, shift(field_map[2 * cells :], -1, 1)),
        ],
        axis=0,
    )
    blank = jnp.zeros((count, LANES - count), jnp.float32)
    for q in range(region_out.shape[0]):
        region_out[q] = jnp.concatenate([region_inverse[0, :, q * count : (q + 1) * count], blank], axis=1)
    both = both_parts(global_inverse[...])
    global_out[...] = both
    through_out[...] = times_parts(coarse_map[0], both)


def after_kernel(
    cells,
    sizes,
    count,
    received,
    base,
    ends,
    after_x,
    after_y,
    after_z,
    field_map,
    face_map,
    ahead_map,
    region_blocks,
    through,
    global_parts,
    direction,
    multipliers,
    residual,
    viscosity,
    multipliers_out,
    residual_out,
    velocity_out,
    pressure_out,
):
    face = cells * cells
    n_region, n_sub = sizes
    half = n_sub // 2
    columns = through.shape[1]
    me_region = lax.axis_index("region")
    everything = jnp.sum(received[...], axis=0)
    totals = [everything[half + 1 + i : half + 2 + i] for i in range(columns // LANES)]
    after = [after_x[...], after_y[...], after_z[...]]
    field = base[...]
    field_x, field_y, field_z = [field[c * cells : (c + 1) * cells] for c in range(3)]
    where_x, where_y, where_z = positions(cells, cells)
    end = cells - 1
    step = jnp.where(where_x == end, jnp.broadcast_to(after[0][0:1], (cells, face)), shift(field_x, -1, 0)) - field_x
    step = step + jnp.where(where_y == end, 0.0, shift(field_y, -cells, 1)) - field_y
    step = step + jnp.where(where_z == end, 0.0, shift(field_z, -1, 1)) - field_z
    step = step + unfold(after[1][1:2], after[2][2:3], cells, True)
    jump = ends[:9] - jnp.concatenate(after, axis=0)
    added = jnp.zeros((count, LANES), jnp.float32)
    for i, part in enumerate(totals):
        added = added + through[:, i * LANES : (i + 1) * LANES] * part
    for q in range(n_sub):
        added = added + region_blocks[q] * received[me_region * n_sub + q, half : half + 1, :]
    lifted = jnp.sum(added, axis=1, keepdims=True)
    own_lane = iota((count, LANES), 0) == iota((count, LANES), 1)
    lifted = jnp.sum(jnp.where(own_lane, lifted, 0.0), axis=0, keepdims=True)

    def placed(numbers):
        wide = jnp.broadcast_to(lifted, (numbers.shape[0], LANES))
        return jnp.concatenate(
            [lane_gather(wide, numbers[:, i * LANES : (i + 1) * LANES]) for i in range(face // LANES)], axis=1
        )

    added = placed(field_map)
    ahead = placed(ahead_map)
    velocity = field + added
    for c in range(3):
        velocity_out[0, c] = velocity[c * cells : (c + 1) * cells]
    added_x = added[:cells]
    step = step + jnp.where(where_x == end, 0.0, shift(added_x, -1, 0)) - added_x
    step = step + ahead[:cells] - added[cells : 2 * cells] + ahead[cells:] - added[2 * cells :]
    pressure_out[0] = -viscosity[0] * step
    jump = jump + placed(face_map)[:9]
    total = jnp.concatenate(totals, axis=1)
    piece = total.astype(jnp.bfloat16).astype(jnp.float32)
    row = iota((16, columns), 0)
    parts = jnp.where(row == 0, piece, jnp.where(row == 1, total - piece, 0.0)).astype(jnp.bfloat16)
    top = jnp.dot(parts, global_parts[...], preferred_element_type=jnp.float32)
    top = top[0:1, :columns] + top[1:2, :columns] + top[0:1, columns:]
    lines = received[:, half, :].reshape(n_region, n_sub, LANES)
    quadratic = jnp.zeros((n_region, n_sub, LANES), jnp.float32)
    for k in range(half):
        products = received[:, k, :].reshape(n_region, n_sub, LANES)
        quadratic = quadratic + products * pltpu.roll(lines, n_sub - 1 - k, 1)
    own_line = everything[half : half + 1]
    lane = iota((1, LANES), 1)
    quadratic = jnp.sum(quadratic.reshape(n_region * n_sub, LANES), axis=0, keepdims=True)
    curvature = quadratic + jnp.where(lane == count, own_line, 0.0)
    for i in range(columns // LANES):
        curvature = curvature + totals[i] * top[:, i * LANES : (i + 1) * LANES]
    curvature = jnp.sum(curvature, axis=1, keepdims=True)
    squares = jnp.sum(jnp.where(lane == count + 1, own_line, 0.0), axis=1, keepdims=True)
    alpha = squares / curvature
    for i in range(9):
        residual_out[i] = residual[i] - alpha * jump[i : i + 1]
        multipliers_out[i] = multipliers[i] + alpha * direction[i]


def body(
    sizes,
    multipliers,
    direction,
    residual,
    reaction,
    viscosity,
    primal_index,
    region_inverse,
    coarse_map,
    global_inverse,
):
    n_region, n_sub = sizes
    cells = reaction.shape[1]
    face = reaction.shape[2]
    count = primal_index.shape[1]
    columns = coarse_map.shape[2]
    height = -(-(n_sub // 2 + 1 + columns // LANES) // 8) * 8
    rows = 3 * cells
    shape = direction.shape
    lines = (9, 1, face)
    f32 = jnp.float32
    bf16 = jnp.bfloat16
    vmem = pl.BlockSpec(memory_space=pltpu.VMEM)
    hbm = pl.BlockSpec(memory_space=pltpu.HBM)

    def like(shape, kind=f32):
        return jax.ShapeDtypeStruct(shape, kind)

    def call(kernel, out_shape, operands, in_hbm=(), scratch=(), out_hbm=0):
        return pl.pallas_call(
            kernel,
            out_shape=out_shape,
            in_specs=[vmem] * len(operands) + [hbm] * len(in_hbm),
            out_specs=[vmem] * (len(out_shape) - out_hbm) + [hbm] * out_hbm,
            scratch_shapes=[pltpu.VMEM(x.shape, x.dtype) for x in scratch]
            + ([pltpu.SemaphoreType.DMA((len(in_hbm) + out_hbm,))] if in_hbm or out_hbm else []),
            compiler_params=pltpu.CompilerParams(vmem_limit_bytes=32 * 1024 * 1024),
        )(*operands, *[pltpu.with_memory_space_constraint(x, pltpu.HBM) for x in in_hbm])

    below_x = shifted_2(direction, "region", 1).reshape(lines)
    below_y = shifted_2(direction, "sub", DOM_Z).reshape(lines)
    below_z = shifted_2(direction, "sub", 1).reshape(lines)
    multipliers, direction, residual = [x.reshape(lines) for x in (multipliers, direction, residual)]
    half_cells = (cells // 2) ** 3
    direction, residual, source, front, inverses, halves, quarter, gather, coarsen, sweeps = call(
        functools.partial(before_kernel, cells, sizes),
        [
            like(lines),
            like(lines),
            like((rows, face)),
            like((height, LANES)),
            like((2, cells, face)),
            like((1, half_cells)),
            like((1, half_cells // 4)),
            like((2 * face, min(half_cells, LANES)), bf16),
            like((2 * half_cells, half_cells // 4), bf16),
            like((half_cells // 2, half_cells), bf16),
        ],
        [],
        [direction, residual, reaction, primal_index, region_inverse, coarse_map],
        [reaction, primal_index, region_inverse, coarse_map],
    )
    base, sent = call(
        functools.partial(solve_kernel, cells, sizes, count),
        [like((rows, face)), like((n_region * n_sub, height, LANES))],
        [source, below_x, below_y, below_z, inverses, front, halves, quarter, gather, coarsen, sweeps],
        scratch=[like((n_region * n_sub, height, LANES))],
        out_hbm=1,
    )
    received = lax.all_to_all(sent, ("region", "sub"), 0, 0, tiled=True)
    lower_x, lower_y, lower_z = call(
        functools.partial(ends_kernel, cells), [like((3, face))] * 3, [base]
    )
    after_x = shifted_2(lower_x, "region", -1)
    after_y = shifted_2(lower_y, "sub", -DOM_Z)
    after_z = shifted_2(lower_z, "sub", -1)
    ends, region_blocks, through, global_parts, field_map, face_map, ahead_map = call(
        functools.partial(between_kernel, cells),
        [
            like((16, face)),
            like((n_sub, count, LANES)),
            like((count, columns)),
            like((columns, 2 * columns), bf16),
            like((rows, face), jnp.int32),
            like((16, face), jnp.int32),
            like((2 * cells, face), jnp.int32),
        ],
        [base, primal_index, region_inverse, coarse_map, global_inverse],
    )
    new_multipliers, new_residual, velocity, pressure = call(
        functools.partial(after_kernel, cells, sizes, count),
        [like(lines), like(lines), like((1, 3, cells, face)), like((1, cells, face))],
        [
            received,
            base,
            ends,
            after_x,
            after_y,
            after_z,
            field_map,
            face_map,
            ahead_map,
            region_blocks,
            through,
            global_parts,
            direction,
            multipliers,
            residual,
            viscosity,
        ],
    )
    return new_multipliers.reshape(shape), new_residual.reshape(shape), velocity, pressure


def solution(mesh):
    sizes = (mesh.shape["region"], mesh.shape["sub"])
    whole = P(("region", "sub"))
    in_specs = (whole,) * 6 + (P("region", "sub"), whole, P())
    return jax.shard_map(
        functools.partial(body, sizes), mesh=mesh, in_specs=in_specs, out_specs=(whole,) * 4, check_vma=False
    )
```

```python
import functools

import jax
import jax.numpy as jnp
from jax import lax
from jax.experimental import pallas as pl
from jax.experimental.pallas import tpu as pltpu
from jax.sharding import PartitionSpec as P

DOM_Z = 4
COARSE_SWEEPS = 8
LANES = 128

damping = 0.8


def shifted_2(x, axis, by):
    count = lax.axis_size(axis)
    return lax.ppermute(x, axis, [(i, (i + by) % count) for i in range(count)])


def iota(shape, dim):
    return lax.broadcasted_iota(jnp.int32, shape, dim)


def parts_of(x, count=3):
    result = []
    for step in range(count):
        piece = x.astype(jnp.bfloat16)
        result.append(piece)
        if step < count - 1:
            x = x - piece.astype(jnp.float32)
    return result


def times_choice(x, choice, count=2):
    rows = x.shape[0]
    stacked = jnp.concatenate(parts_of(x, count), axis=0)
    y = jnp.dot(stacked, choice, preferred_element_type=jnp.float32)
    return functools.reduce(lambda a, b: a + b, [y[i * rows : (i + 1) * rows] for i in range(count)])


def times_parts(x, both):
    rows = x.shape[0]
    width = both.shape[1] // 2
    y = jnp.dot(jnp.concatenate(parts_of(x, 2), axis=0), both, preferred_element_type=jnp.float32)
    return y[:rows, :width] + (y[rows:, :width] + y[:rows, width:])


def stacked_parts(w):
    first, second = parts_of(w, 2)
    return jnp.concatenate([first, first, second, jnp.zeros_like(first)], axis=0)


def times_stacked(x, stacked):
    first, second = parts_of(x, 2)
    left = iota(x.shape, 1) < x.shape[1] // 2
    zero = jnp.zeros_like(x)
    pair = jnp.where(left, first.astype(jnp.float32), second.astype(jnp.float32))
    other = jnp.where(left, first.astype(jnp.float32), zero)
    pair = jnp.concatenate([pair, other], axis=1).astype(jnp.bfloat16)
    return jnp.dot(pair, stacked, preferred_element_type=jnp.float32)


def both_parts(w):
    return jnp.concatenate(parts_of(w, 2), axis=1)


def choice_times(choice, x, count=2):
    width = x.shape[1]
    stacked = jnp.concatenate(parts_of(x, count), axis=1)
    y = jnp.dot(choice, stacked, preferred_element_type=jnp.float32)
    return functools.reduce(lambda a, b: a + b, [y[:, i * width : (i + 1) * width] for i in range(count)])


def one_hot(condition):
    return jnp.where(condition, 1.0, 0.0).astype(jnp.bfloat16)


def decode(picked, cells):
    face = cells * cells
    zero = jnp.zeros_like(picked)
    one = zero + 1
    block = jnp.where(picked >= 3 * face, one, zero) + jnp.where(picked >= 6 * face, one, zero)
    rest = picked - 3 * face * block
    component = jnp.where(rest >= face, one, zero) + jnp.where(rest >= 2 * face, one, zero)
    spot = rest - face * component
    first = lax.div(spot, zero + cells)
    second = spot - first * cells
    end = cells - 1
    x = jnp.where(block == 0, end, first)
    y = jnp.where(block == 0, first, jnp.where(block == 1, end, second))
    z = jnp.where(block == 2, end, second)
    return 3 * block + component, spot, component * cells + x, y * cells + z


def faces_of(rows):
    return [jnp.concatenate([rows[3 * d + c] for c in range(3)], axis=0) for d in range(3)]


def lane_gather(x, lanes):
    return jnp.take_along_axis(x, lanes, axis=1, mode="promise_in_bounds")


def grid(cells, count, tile):
    shape = (count * cells, LANES)
    y, z = split_index(iota(shape, 1) + tile * LANES, cells, 2)
    return iota(shape, 0) & (cells - 1), y, z


def rows_of_tiles(x, rows):
    count, width = x.shape
    tiles = width // LANES
    return jnp.concatenate(
        [
            jnp.broadcast_to(x[c : c + 1, i * LANES : (i + 1) * LANES], (rows // tiles, LANES))
            for c in range(count)
            for i in range(tiles)
        ],
        axis=0,
    )


def unfold(on_y, on_z, cells, upper):
    count, face = on_y.shape
    end = cells - 1 if upper else 0
    wide_y = rows_of_tiles(on_y, cells)
    wide_z = rows_of_tiles(on_z, cells)
    tiles = []
    for tile in range(face // LANES):
        x, y, z = grid(cells, count, tile)
        start = (x * cells) & (LANES - 1)
        field = jnp.where(z == end, lane_gather(wide_z, start + y), 0.0)
        if end * cells // LANES == tile:
            field = field + jnp.where(y == end, lane_gather(wide_y, start + z), 0.0)
        tiles.append(field)
    return jnp.concatenate(tiles, axis=1)


def fold(field, cells, upper):
    face = cells * cells
    end = cells - 1 if upper else 0
    rows = LANES // cells
    tiles = [field[:, i * LANES : (i + 1) * LANES] for i in range(face // LANES)]
    x, first, second = grid(cells, 3, 0)
    on_y = lane_gather(tiles[end * cells // LANES], ((end * cells) & (LANES - 1)) + second)
    on_z = jnp.zeros_like(on_y)
    for i, tile in enumerate(tiles):
        values = lane_gather(tile, ((second * cells) & (LANES - 1)) + end)
        on_z = jnp.where(second // rows == i, values, on_z)
    here = first == (x & (rows - 1))
    faces = [jnp.concatenate([field[c * cells + end : c * cells + end + 1] for c in range(3)], axis=0)]
    for values in (on_y, on_z):
        values = jnp.where(here, values, 0.0)
        sums = [jnp.sum(values[i * rows : (i + 1) * rows], axis=0, keepdims=True) for i in range(3 * cells // rows)]
        per = face // LANES
        faces.append(
            jnp.concatenate([jnp.concatenate(sums[c * per : (c + 1) * per], axis=1) for c in range(3)], axis=0)
        )
    return faces


def column_of(line):
    count = line.shape[1]
    wide = jnp.broadcast_to(line.astype(jnp.float32), (count, count))
    diagonal = iota((count, count), 0) == iota((count, count), 1)
    return jnp.sum(jnp.where(diagonal, wide, 0.0), axis=1, keepdims=True).astype(jnp.int32)


def shift(field, by, dim):
    size = field.shape[dim]
    return pltpu.roll(field, by % size, dim)


def positions(rows, cells):
    shape = (rows, cells * cells)
    return (iota(shape, 0) & (cells - 1), *split_index(iota(shape, 1), cells, 2))


def bits(cells):
    return cells.bit_length() - 1


def split_index(flat, cells, dims):
    return [(flat >> (bits(cells) * (dims - 1 - i))) & (cells - 1) for i in range(dims)]


def plane_blocks(y, z, far_y, far_z, steps=1):
    inside = [(y >> steps) == far_y, (z >> steps) == far_z]
    nearby = [(f >> 1) + 2 * (f & 1) - 1 == b for f, b in ((y, far_y), (z, far_z))]
    same = inside[0] & inside[1]
    near = (nearby[0] & inside[1]) | (inside[0] & nearby[1])
    return one_hot(same), jnp.where(same, 2.0, jnp.where(near, 1.0, 0.0)).astype(jnp.bfloat16)


def gather_matrix(cells, steps=1):
    size = cells >> steps
    shape = (cells * cells, min(size**3, LANES))
    y, z = split_index(iota(shape, 0), cells, 2)
    _, far_y, far_z = split_index(iota(shape, 1), size, 3)
    return plane_blocks(y, z, far_y, far_z, steps)


def block_matrices(cells, blocks_first):
    half = cells // 2
    shape = (half**3, cells**3) if blocks_first else (cells**3, half**3)
    fine = split_index(iota(shape, 1 if blocks_first else 0), cells, 3)
    block = split_index(iota(shape, 0 if blocks_first else 1), half, 3)
    inside = [(f >> 1) == b for f, b in zip(fine, block)]
    nearby = [(f >> 1) + 2 * (f & 1) - 1 == b for f, b in zip(fine, block)]
    same = inside[0] & inside[1] & inside[2]
    near = (
        (nearby[0] & inside[1] & inside[2])
        | (inside[0] & nearby[1] & inside[2])
        | (inside[0] & inside[1] & nearby[2])
    )
    return one_hot(same), jnp.where(same, 3.0, jnp.where(near, 1.0, 0.0)).astype(jnp.bfloat16)


def plane_restrict(field, gather, cells, count, steps=1):
    size = cells >> steps
    width = gather.shape[1]
    per = width // (size * size) << steps
    spread_out = times_choice(field, gather)
    shape = (cells, width)
    own = split_index(iota(shape, 1), size, 3)[0] == ((iota(shape, 0) & (per - 1)) >> steps)
    group = iota(shape, 0) // per
    rows = []
    for c in range(count):
        values = jnp.where(own, spread_out[c * cells : (c + 1) * cells], 0.0)
        tiles = [
            jnp.sum(jnp.where(group == i, values, 0.0), axis=0, keepdims=True) for i in range(cells // per)
        ]
        rows.append(tiles[0] if len(tiles) == 1 else jnp.concatenate(tiles, axis=1))
    return 0.125**steps * (rows[0] if count == 1 else jnp.concatenate(rows, axis=0))


def plane_prolong(coarse, cells, count):
    half = cells // 2
    wide = rows_of_tiles(coarse[:count], cells)
    fine, nearby = [], []
    for tile in range(cells * cells // LANES):
        x, y, z = grid(cells, count, tile)
        start = ((x >> 1) * half * half) & (LANES - 1)
        half_y, half_z = y >> 1, z >> 1
        other_y, other_z = half_y + 2 * (y & 1) - 1, half_z + 2 * (z & 1) - 1
        inside_y, inside_z = (other_y & (half - 1)) == other_y, (other_z & (half - 1)) == other_z
        values = lane_gather(wide, start + half_y * half + half_z)
        beside_y = lane_gather(wide, start + (other_y & (half - 1)) * half + half_z)
        beside_z = lane_gather(wide, start + half_y * half + (other_z & (half - 1)))
        fine.append(values)
        nearby.append(2.0 * values + jnp.where(inside_y, beside_y, 0.0) + jnp.where(inside_z, beside_z, 0.0))
    return jnp.concatenate(fine, axis=1), jnp.concatenate(nearby, axis=1)


def sweep_power(scale, cells, weight):
    size = cells**3
    shape = (size, size)
    here = split_index(iota(shape, 0), cells, 3)
    there = split_index(iota(shape, 1), cells, 3)
    distance = functools.reduce(lambda a, b: a + b, [jnp.abs(a - b) for a, b in zip(here, there)])
    one = jnp.where(distance == 0, 1.0, 0.0)
    return (1.0 - damping) * one + jnp.where(distance == 1, weight * scale, 0.0), one


def square(power):
    return times_parts(power, both_parts(power))


def powers_sum(total, power):
    done = 2
    while done < COARSE_SWEEPS:
        total = total + times_parts(total, both_parts(power))
        done *= 2
        if done < COARSE_SWEEPS:
            power = square(power)
    return total


def turn(k, count):
    return (k + 1) * (LANES - count) % LANES


def free_lanes(rows, count):
    shape = (rows, LANES)
    return (iota(shape, 1) // (LANES - count) == iota(shape, 0)) & (iota(shape, 0) < LANES // (LANES - count))


def load(pairs, semaphores):
    copies = [pltpu.make_async_copy(a, b, semaphores.at[i]) for i, (a, b) in enumerate(pairs)]
    for copy in copies:
        copy.start()
    return copies


def before_kernel(
    cells,
    sizes,
    direction_in,
    residual_in,
    reaction_in,
    primal_index_in,
    region_inverse_in,
    coarse_map_in,
    direction,
    residual,
    source_out,
    front_out,
    inverse_out,
    half_out,
    quarter_out,
    gather_out,
    coarsen_out,
    sweeps_out,
    reaction,
    primal_index,
    region_inverse,
    coarse_map,
    semaphores,
):
    copies = load(
        [
            (direction_in, direction),
            (reaction_in, reaction),
            (primal_index_in, primal_index),
            (residual_in, residual),
            (coarse_map_in, coarse_map),
            (region_inverse_in, region_inverse),
        ],
        semaphores,
    )
    face = cells * cells
    n_sub = sizes[1]
    half = cells // 2
    gather, gather_near = gather_matrix(cells)
    gather_out[...] = jnp.concatenate([gather, gather_near], axis=0)
    quarter_gather = gather_matrix(cells, 2)[0]
    coarsen, coarsen_near = block_matrices(half, False)
    coarsen_out[...] = jnp.concatenate([jnp.concatenate([x, x], axis=1) for x in (coarsen, coarsen_near)], axis=0)
    refine = jnp.concatenate(block_matrices(half, True), axis=1)
    for copy in copies[:3]:
        copy.wait()
    react = reaction[0]
    scale = damping / (plane_restrict(react, quarter_gather, cells, 1, 2) + 6.0 * 0.0625)
    quarter_out[...] = 0.125 * jnp.concatenate([scale, scale], axis=1)
    power, one = sweep_power(scale, half // 2, 0.0625)
    second_power = square(power)
    diagonal = react + 6.0
    inverse_out[0] = damping / diagonal
    inverse_out[1] = diagonal
    half_scale = damping / (plane_restrict(react, gather, cells, 1) + 6.0 * 0.25)
    half_out[...] = half_scale
    faces = faces_of(direction)
    count = primal_index.shape[1]
    group, spot, _, _ = decode(column_of(primal_index[...]), cells)
    nine = jnp.concatenate(faces + [jnp.zeros((7, face), jnp.float32)], axis=0)
    gathered = choice_times(one_hot(iota((count, 16), 1) == group), nine)
    primal = jnp.sum(jnp.where(iota((count, face), 1) == spot, gathered, 0.0), axis=1, keepdims=True)
    lane = iota((1, LANES), 1)
    line = jnp.sum(
        jnp.where(iota((count, LANES), 0) == iota((count, LANES), 1), primal, 0.0), axis=0, keepdims=True
    )
    for copy in copies[3:]:
        copy.wait()
    refined = times_choice(powers_sum(one + power, second_power), refine)
    sweeps_out[...] = stacked_parts(
        (1.0 - damping) * refined[:, : half**3] + 0.25 * half_scale * refined[:, half**3 :]
    )
    row_x = iota((cells, face), 0)
    source = unfold(faces[1], faces[2], cells, True)
    own_x = jnp.concatenate(
        [jnp.where(row_x == cells - 1, jnp.broadcast_to(faces[0][c : c + 1], (cells, face)), 0.0) for c in range(3)],
        axis=0,
    )
    source_out[...] = source + own_x
    share = jnp.sum(primal * coarse_map[0], axis=0, keepdims=True)
    product = jnp.sum(primal * region_inverse[0], axis=0, keepdims=True)
    blank = jnp.zeros((1, LANES - count), jnp.float32)
    blocks = jnp.concatenate(
        [jnp.concatenate([product[:, q * count : (q + 1) * count], blank], axis=1) for q in range(n_sub)], axis=0
    )
    me_sub = lax.axis_index("sub")
    own = jnp.sum(jnp.where(iota(blocks.shape, 0) == me_sub, blocks, 0.0), axis=0, keepdims=True)
    own = jnp.sum(own * line, axis=1, keepdims=True)
    blocks = pltpu.roll(blocks, n_sub - 1 - me_sub, 0)
    opposite = n_sub // 2
    twice = jnp.where(iota((opposite, LANES), 0) == (opposite - 1 if n_sub % 2 == 0 else opposite), 1.0, 2.0)
    squares = jnp.concatenate([residual[i] for i in range(9)], axis=0)
    squares = jnp.sum(jnp.sum(squares * squares, axis=0, keepdims=True), axis=1, keepdims=True)
    line = jnp.where(lane == count, own, jnp.where(lane == count + 1, squares, line))
    front_out[...] = jnp.zeros_like(front_out)
    blocks = blocks[:opposite] * twice
    for k in range(opposite):
        front_out[k : k + 1, :] = pltpu.roll(blocks[k : k + 1], turn(k, count), 1)
    front_out[opposite : opposite + 1, :] = line
    for i in range(share.shape[1] // LANES):
        front_out[opposite + 1 + i : opposite + 2 + i, :] = share[:, i * LANES : (i + 1) * LANES]


def solve_kernel(
    cells,
    sizes,
    count,
    source_own,
    from_x,
    from_y,
    from_z,
    inverses,
    front,
    halves,
    quarter,
    gather,
    coarsen,
    sweeps,
    base_out,
    send_out,
    buffer,
    semaphores,
):
    face = cells * cells
    rows = 3 * cells
    below_x, below_y, below_z = [faces_of(ref)[d] for d, ref in enumerate((from_x, from_y, from_z))]
    n_region, n_sub = sizes
    row_x = iota((cells, face), 0)
    source = source_own[...] - unfold(below_y, below_z, cells, False)
    source = source - jnp.concatenate(
        [jnp.where(row_x == 0, jnp.broadcast_to(below_x[c : c + 1], (cells, face)), 0.0) for c in range(3)],
        axis=0,
    )
    where_x, where_y, where_z = positions(rows, cells)
    last = cells - 1

    def tall(x):
        return jnp.concatenate([x] * 3, axis=0)

    inverse = tall(inverses[0])
    diagonal = tall(inverses[1])

    def beside_x(field):
        total = jnp.where(where_x < last, shift(field, -1, 0), 0.0)
        return total + jnp.where(where_x > 0, shift(field, 1, 0), 0.0)

    def beside(field):
        total = jnp.where(where_y < last, shift(field, -cells, 1), 0.0)
        total = total + jnp.where(where_y > 0, shift(field, cells, 1), 0.0)
        total = total + jnp.where(where_z < last, shift(field, -1, 1), 0.0)
        total = total + jnp.where(where_z > 0, shift(field, 1, 1), 0.0)
        return beside_x(field) + total

    half = cells // 2
    lane = iota((8, half**3), 1)
    half_at = split_index(lane, half, 3)
    half_scale = halves[...]

    def half_beside(field):
        total = jnp.zeros_like(field)
        for position, reach in zip(half_at, (half * half, half, 1)):
            total = total + jnp.where(position < half - 1, shift(field, -reach, 1), 0.0)
            total = total + jnp.where(position > 0, shift(field, reach, 1), 0.0)
        return total

    def half_cycle(right):
        swept = half_scale * right
        remain = times_choice(jnp.concatenate([(1.0 - damping) * right, 0.25 * swept], axis=1), coarsen[...])
        local = (2.0 - damping) * swept + 0.25 * half_scale * half_beside(swept)
        return local + times_stacked(remain * quarter[...], sweeps[...])

    def correct(residual):
        swept = inverse * residual
        remain = (1.0 - damping) * residual
        right = plane_restrict(
            jnp.concatenate([remain + beside_x(swept), swept], axis=1), gather[...], cells, 3
        )
        right = jnp.concatenate([right, jnp.zeros((5, half**3), jnp.float32)], axis=0)
        remain = remain + beside(swept)
        correction, nearby = plane_prolong(half_cycle(right), cells, 3)
        return swept + correction, remain - diagonal * correction + beside_x(correction) + nearby

    field, residual = correct(source)
    swept = inverse * residual
    ahead = jnp.where(where_x < last, shift(swept, -1, 0), 0.0)
    ahead = ahead + jnp.where(where_y < last, shift(swept, -cells, 1), 0.0)
    ahead = ahead + jnp.where(where_z < last, shift(swept, -1, 1), 0.0)
    energy = (source + residual) * field + swept * (2.0 * residual - diagonal * swept + 2.0 * ahead)
    energy = jnp.sum(energy, axis=0, keepdims=True)
    energy = functools.reduce(lambda a, b: a + b, [energy[:, i * LANES : (i + 1) * LANES] for i in range(face // LANES)])
    message = front[...]
    message = message + jnp.where(free_lanes(message.shape[0], count), energy, 0.0)
    for device in range(sizes[0] * sizes[1]):
        buffer[device] = message
    (copy,) = load([(buffer, send_out)], semaphores)
    then = (1.0 - damping) * residual + beside(swept)
    field = field + swept
    more, residual = correct(then)
    base_out[...] = field + more + inverse * residual
    copy.wait()


def ends_kernel(cells, base, lower_x, lower_y, lower_z):
    lower_x[...], lower_y[...], lower_z[...] = fold(base[...], cells, False)


def between_kernel(
    cells,
    base,
    primal_index,
    region_inverse,
    coarse_map,
    global_inverse,
    ends_out,
    region_out,
    through_out,
    global_out,
    field_map_out,
    face_map_out,
    ahead_map_out,
):
    face = cells * cells
    ends_out[...] = jnp.concatenate(fold(base[...], cells, True) + [jnp.zeros((7, face), jnp.float32)], axis=0)
    count = primal_index.shape[1]
    group, _, place, _ = decode(primal_index[...], cells)
    choose = jnp.concatenate(
        [one_hot(iota((3 * cells, count), 0) == place), one_hot(iota((16, count), 0) == group)], axis=0
    )
    _, spot, _, lane = decode(column_of(primal_index[...]), cells)
    at = iota((count, face), 1)
    number = iota((count, 2 * face), 0) + 1
    spots = jnp.where(jnp.concatenate([at == lane, at == spot], axis=1), number, 0).astype(jnp.float32)
    maps = choice_times(choose, spots).astype(jnp.int32)
    maps = jnp.where(maps > 0, maps - 1, LANES - 1)
    field_map = maps[: 3 * cells, :face]
    field_map_out[...] = field_map
    face_map_out[...] = maps[3 * cells :, face:]
    _, where_y, where_z = positions(cells, cells)
    end = cells - 1
    ahead_map_out[...] = jnp.concatenate(
        [
            jnp.where(where_y == end, LANES - 1, shift(field_map[cells : 2 * cells], -cells, 1)),
            jnp.where(where_z == end, LANES - 1, shift(field_map[2 * cells :], -1, 1)),
        ],
        axis=0,
    )
    blank = jnp.zeros((count, LANES - count), jnp.float32)
    for q in range(region_out.shape[0]):
        region_out[q] = jnp.concatenate([region_inverse[0, :, q * count : (q + 1) * count], blank], axis=1)
    both = both_parts(global_inverse[...])
    global_out[...] = both
    through_out[...] = times_parts(coarse_map[0], both)


def after_kernel(
    cells,
    sizes,
    count,
    received,
    base,
    ends,
    after_x,
    after_y,
    after_z,
    field_map,
    face_map,
    ahead_map,
    region_blocks,
    through,
    global_parts,
    direction,
    multipliers,
    residual,
    viscosity,
    multipliers_out,
    residual_out,
    velocity_out,
    pressure_out,
):
    face = cells * cells
    n_region, n_sub = sizes
    half = n_sub // 2
    columns = through.shape[1]
    me_region = lax.axis_index("region")
    everything = jnp.sum(received[...], axis=0)
    totals = [everything[half + 1 + i : half + 2 + i] for i in range(columns // LANES)]
    lines = received[:, half, :]
    lines = jnp.where(iota(lines.shape, 1) < count, lines, 0.0).reshape(n_region, n_sub, LANES)
    groups = LANES // (LANES - count)
    turned = [pltpu.roll(lines, turn(k, count), 2) for k in range(min(groups, half))]
    quadratic = jnp.zeros((n_region, n_sub, LANES), jnp.float32)
    for k in range(half):
        products = received[:, k, :].reshape(n_region, n_sub, LANES)
        quadratic = quadratic + products * pltpu.roll(turned[k % groups], n_sub - 1 - k, 1)
    after = [after_x[...], after_y[...], after_z[...]]
    field = base[...]
    field_x, field_y, field_z = [field[c * cells : (c + 1) * cells] for c in range(3)]
    where_x, where_y, where_z = positions(cells, cells)
    end = cells - 1
    step = jnp.where(where_x == end, jnp.broadcast_to(after[0][0:1], (cells, face)), shift(field_x, -1, 0)) - field_x
    step = step + jnp.where(where_y == end, 0.0, shift(field_y, -cells, 1)) - field_y
    step = step + jnp.where(where_z == end, 0.0, shift(field_z, -1, 1)) - field_z
    step = step + unfold(after[1][1:2], after[2][2:3], cells, True)
    jump = ends[:9] - jnp.concatenate(after, axis=0)
    added = jnp.zeros((count, LANES), jnp.float32)
    for i, part in enumerate(totals):
        added = added + through[:, i * LANES : (i + 1) * LANES] * part
    for q in range(n_sub):
        added = added + region_blocks[q] * received[me_region * n_sub + q, half : half + 1, :]
    lifted = jnp.sum(added, axis=1, keepdims=True)
    own_lane = iota((count, LANES), 0) == iota((count, LANES), 1)
    lifted = jnp.sum(jnp.where(own_lane, lifted, 0.0), axis=0, keepdims=True)

    def placed(numbers):
        wide = jnp.broadcast_to(lifted, (numbers.shape[0], LANES))
        return jnp.concatenate(
            [lane_gather(wide, numbers[:, i * LANES : (i + 1) * LANES]) for i in range(face // LANES)], axis=1
        )

    added = placed(field_map)
    ahead = placed(ahead_map)
    velocity = field + added
    for c in range(3):
        velocity_out[0, c] = velocity[c * cells : (c + 1) * cells]
    added_x = added[:cells]
    step = step + jnp.where(where_x == end, 0.0, shift(added_x, -1, 0)) - added_x
    step = step + ahead[:cells] - added[cells : 2 * cells] + ahead[cells:] - added[2 * cells :]
    pressure_out[0] = -viscosity[0] * step
    jump = jump + placed(face_map)[:9]
    total = jnp.concatenate(totals, axis=1)
    piece = total.astype(jnp.bfloat16).astype(jnp.float32)
    row = iota((16, columns), 0)
    parts = jnp.where(row == 0, piece, jnp.where(row == 1, total - piece, 0.0)).astype(jnp.bfloat16)
    top = jnp.dot(parts, global_parts[...], preferred_element_type=jnp.float32)
    top = top[0:1, :columns] + top[1:2, :columns] + top[0:1, columns:]
    own_line = everything[half : half + 1]
    lane = iota((1, LANES), 1)
    quadratic = jnp.sum(quadratic.reshape(n_region * n_sub, LANES), axis=0, keepdims=True)
    energy = jnp.where(free_lanes(everything.shape[0], count), everything, 0.0)
    curvature = quadratic + jnp.where(lane == count, own_line, 0.0) + jnp.sum(energy, axis=0, keepdims=True)
    for i in range(columns // LANES):
        curvature = curvature + totals[i] * top[:, i * LANES : (i + 1) * LANES]
    curvature = jnp.sum(curvature, axis=1, keepdims=True)
    squares = jnp.sum(jnp.where(lane == count + 1, own_line, 0.0), axis=1, keepdims=True)
    alpha = squares / curvature
    for i in range(9):
        residual_out[i] = residual[i] - alpha * jump[i : i + 1]
        multipliers_out[i] = multipliers[i] + alpha * direction[i]


def body(
    sizes,
    multipliers,
    direction,
    residual,
    reaction,
    viscosity,
    primal_index,
    region_inverse,
    coarse_map,
    global_inverse,
):
    n_region, n_sub = sizes
    assert LANES % (LANES - primal_index.shape[1]) == 0 and n_sub // 2 >= LANES // (LANES - primal_index.shape[1])
    cells = reaction.shape[1]
    face = reaction.shape[2]
    count = primal_index.shape[1]
    columns = coarse_map.shape[2]
    height = -(-(n_sub // 2 + 1 + columns // LANES) // 8) * 8
    rows = 3 * cells
    shape = direction.shape
    lines = (9, 1, face)
    f32 = jnp.float32
    bf16 = jnp.bfloat16
    vmem = pl.BlockSpec(memory_space=pltpu.VMEM)
    hbm = pl.BlockSpec(memory_space=pltpu.HBM)

    def like(shape, kind=f32):
        return jax.ShapeDtypeStruct(shape, kind)

    def call(kernel, out_shape, operands, in_hbm=(), scratch=(), out_hbm=0):
        return pl.pallas_call(
            kernel,
            out_shape=out_shape,
            in_specs=[vmem] * len(operands) + [hbm] * len(in_hbm),
            out_specs=[vmem] * (len(out_shape) - out_hbm) + [hbm] * out_hbm,
            scratch_shapes=[pltpu.VMEM(x.shape, x.dtype) for x in scratch]
            + ([pltpu.SemaphoreType.DMA((len(in_hbm) + out_hbm,))] if in_hbm or out_hbm else []),
            compiler_params=pltpu.CompilerParams(vmem_limit_bytes=32 * 1024 * 1024),
        )(*operands, *[pltpu.with_memory_space_constraint(x, pltpu.HBM) for x in in_hbm])

    below_x = shifted_2(direction, "region", 1).reshape(lines)
    below_y = shifted_2(direction, "sub", DOM_Z).reshape(lines)
    below_z = shifted_2(direction, "sub", 1).reshape(lines)
    multipliers, direction, residual = [x.reshape(lines) for x in (multipliers, direction, residual)]
    half_cells = (cells // 2) ** 3
    direction, residual, source, front, inverses, halves, quarter, gather, coarsen, sweeps = call(
        functools.partial(before_kernel, cells, sizes),
        [
            like(lines),
            like(lines),
            like((rows, face)),
            like((height, LANES)),
            like((2, cells, face)),
            like((1, half_cells)),
            like((1, half_cells // 4)),
            like((2 * face, min(half_cells, LANES)), bf16),
            like((2 * half_cells, half_cells // 4), bf16),
            like((half_cells // 2, half_cells), bf16),
        ],
        [],
        [direction, residual, reaction, primal_index, region_inverse, coarse_map],
        [reaction, primal_index, region_inverse, coarse_map],
    )
    base, sent = call(
        functools.partial(solve_kernel, cells, sizes, count),
        [like((rows, face)), like((n_region * n_sub, height, LANES))],
        [source, below_x, below_y, below_z, inverses, front, halves, quarter, gather, coarsen, sweeps],
        scratch=[like((n_region * n_sub, height, LANES))],
        out_hbm=1,
    )
    received = lax.all_to_all(sent, ("region", "sub"), 0, 0, tiled=True)
    lower_x, lower_y, lower_z = call(
        functools.partial(ends_kernel, cells), [like((3, face))] * 3, [base]
    )
    after_x = shifted_2(lower_x, "region", -1)
    after_y = shifted_2(lower_y, "sub", -DOM_Z)
    after_z = shifted_2(lower_z, "sub", -1)
    ends, region_blocks, through, global_parts, field_map, face_map, ahead_map = call(
        functools.partial(between_kernel, cells),
        [
            like((16, face)),
            like((n_sub, count, LANES)),
            like((count, columns)),
            like((columns, 2 * columns), bf16),
            like((rows, face), jnp.int32),
            like((16, face), jnp.int32),
            like((2 * cells, face), jnp.int32),
        ],
        [base, primal_index, region_inverse, coarse_map, global_inverse],
    )
    new_multipliers, new_residual, velocity, pressure = call(
        functools.partial(after_kernel, cells, sizes, count),
        [like(lines), like(lines), like((1, 3, cells, face)), like((1, cells, face))],
        [
            received,
            base,
            ends,
            after_x,
            after_y,
            after_z,
            field_map,
            face_map,
            ahead_map,
            region_blocks,
            through,
            global_parts,
            direction,
            multipliers,
            residual,
            viscosity,
        ],
    )
    return new_multipliers.reshape(shape), new_residual.reshape(shape), velocity, pressure


def solution(mesh):
    sizes = (mesh.shape["region"], mesh.shape["sub"])
    whole = P(("region", "sub"))
    in_specs = (whole,) * 6 + (P("region", "sub"), whole, P())
    return jax.shard_map(
        functools.partial(body, sizes), mesh=mesh, in_specs=in_specs, out_specs=(whole,) * 4, check_vma=False
    )
```

```python
import functools

import jax
import jax.numpy as jnp
from jax import lax
from jax.experimental import pallas as pl
from jax.experimental.pallas import tpu as pltpu
from jax.sharding import PartitionSpec as P

DOM_Z = 4
COARSE_SWEEPS = 8
LANES = 128

damping = 0.8


def shifted_2(x, axis, by):
    count = lax.axis_size(axis)
    return lax.ppermute(x, axis, [(i, (i + by) % count) for i in range(count)])


def iota(shape, dim):
    return lax.broadcasted_iota(jnp.int32, shape, dim)


def parts_of(x, count=3):
    result = []
    for step in range(count):
        piece = x.astype(jnp.bfloat16)
        result.append(piece)
        if step < count - 1:
            x = x - piece.astype(jnp.float32)
    return result


def times_choice(x, choice, count=2):
    rows = x.shape[0]
    stacked = jnp.concatenate(parts_of(x, count), axis=0)
    y = jnp.dot(stacked, choice, preferred_element_type=jnp.float32)
    return functools.reduce(lambda a, b: a + b, [y[i * rows : (i + 1) * rows] for i in range(count)])


def times_parts(x, both):
    rows = x.shape[0]
    width = both.shape[1] // 2
    y = jnp.dot(jnp.concatenate(parts_of(x, 2), axis=0), both, preferred_element_type=jnp.float32)
    return y[:rows, :width] + (y[rows:, :width] + y[:rows, width:])


def stacked_parts(w):
    first, second = parts_of(w, 2)
    return jnp.concatenate([first, first, second, jnp.zeros_like(first)], axis=0)


def times_stacked(x, stacked):
    first, second = parts_of(x, 2)
    left = iota(x.shape, 1) < x.shape[1] // 2
    zero = jnp.zeros_like(x)
    pair = jnp.where(left, first.astype(jnp.float32), second.astype(jnp.float32))
    other = jnp.where(left, first.astype(jnp.float32), zero)
    pair = jnp.concatenate([pair, other], axis=1).astype(jnp.bfloat16)
    return jnp.dot(pair, stacked, preferred_element_type=jnp.float32)


def both_parts(w):
    return jnp.concatenate(parts_of(w, 2), axis=1)


def choice_times(choice, x, count=2):
    width = x.shape[1]
    stacked = jnp.concatenate(parts_of(x, count), axis=1)
    y = jnp.dot(choice, stacked, preferred_element_type=jnp.float32)
    return functools.reduce(lambda a, b: a + b, [y[:, i * width : (i + 1) * width] for i in range(count)])


def one_hot(condition):
    return jnp.where(condition, 1.0, 0.0).astype(jnp.bfloat16)


def decode(picked, cells):
    face = cells * cells
    zero = jnp.zeros_like(picked)
    one = zero + 1
    block = jnp.where(picked >= 3 * face, one, zero) + jnp.where(picked >= 6 * face, one, zero)
    rest = picked - 3 * face * block
    component = jnp.where(rest >= face, one, zero) + jnp.where(rest >= 2 * face, one, zero)
    spot = rest - face * component
    first = lax.div(spot, zero + cells)
    second = spot - first * cells
    end = cells - 1
    x = jnp.where(block == 0, end, first)
    y = jnp.where(block == 0, first, jnp.where(block == 1, end, second))
    z = jnp.where(block == 2, end, second)
    return 3 * block + component, spot, component * cells + x, y * cells + z


def faces_of(rows):
    return [jnp.concatenate([rows[3 * d + c] for c in range(3)], axis=0) for d in range(3)]


def lane_gather(x, lanes):
    return jnp.take_along_axis(x, lanes, axis=1, mode="promise_in_bounds")


def grid(cells, count, tile):
    shape = (count * cells, LANES)
    y, z = split_index(iota(shape, 1) + tile * LANES, cells, 2)
    return iota(shape, 0) & (cells - 1), y, z


def rows_of_tiles(x, rows):
    count, width = x.shape
    tiles = width // LANES
    return jnp.concatenate(
        [
            jnp.broadcast_to(x[c : c + 1, i * LANES : (i + 1) * LANES], (rows // tiles, LANES))
            for c in range(count)
            for i in range(tiles)
        ],
        axis=0,
    )


def unfold(on_y, on_z, cells, upper):
    count, face = on_y.shape
    end = cells - 1 if upper else 0
    wide_y = rows_of_tiles(on_y, cells)
    wide_z = rows_of_tiles(on_z, cells)
    tiles = []
    for tile in range(face // LANES):
        x, y, z = grid(cells, count, tile)
        start = (x * cells) & (LANES - 1)
        field = jnp.where(z == end, lane_gather(wide_z, start + y), 0.0)
        if end * cells // LANES == tile:
            field = field + jnp.where(y == end, lane_gather(wide_y, start + z), 0.0)
        tiles.append(field)
    return jnp.concatenate(tiles, axis=1)


def fold(field, cells, upper):
    face = cells * cells
    end = cells - 1 if upper else 0
    rows = LANES // cells
    tiles = [field[:, i * LANES : (i + 1) * LANES] for i in range(face // LANES)]
    x, first, second = grid(cells, 3, 0)
    on_y = lane_gather(tiles[end * cells // LANES], ((end * cells) & (LANES - 1)) + second)
    on_z = jnp.zeros_like(on_y)
    for i, tile in enumerate(tiles):
        values = lane_gather(tile, ((second * cells) & (LANES - 1)) + end)
        on_z = jnp.where(second // rows == i, values, on_z)
    here = first == (x & (rows - 1))
    faces = [jnp.concatenate([field[c * cells + end : c * cells + end + 1] for c in range(3)], axis=0)]
    for values in (on_y, on_z):
        values = jnp.where(here, values, 0.0)
        sums = [jnp.sum(values[i * rows : (i + 1) * rows], axis=0, keepdims=True) for i in range(3 * cells // rows)]
        per = face // LANES
        faces.append(
            jnp.concatenate([jnp.concatenate(sums[c * per : (c + 1) * per], axis=1) for c in range(3)], axis=0)
        )
    return faces


def column_of(line):
    count = line.shape[1]
    wide = jnp.broadcast_to(line.astype(jnp.float32), (count, count))
    diagonal = iota((count, count), 0) == iota((count, count), 1)
    return jnp.sum(jnp.where(diagonal, wide, 0.0), axis=1, keepdims=True).astype(jnp.int32)


def shift(field, by, dim):
    size = field.shape[dim]
    return pltpu.roll(field, by % size, dim)


def positions(rows, cells):
    shape = (rows, cells * cells)
    return (iota(shape, 0) & (cells - 1), *split_index(iota(shape, 1), cells, 2))


def bits(cells):
    return cells.bit_length() - 1


def split_index(flat, cells, dims):
    return [(flat >> (bits(cells) * (dims - 1 - i))) & (cells - 1) for i in range(dims)]


def plane_blocks(y, z, far_y, far_z, steps=1):
    inside = [(y >> steps) == far_y, (z >> steps) == far_z]
    nearby = [(f >> 1) + 2 * (f & 1) - 1 == b for f, b in ((y, far_y), (z, far_z))]
    same = inside[0] & inside[1]
    near = (nearby[0] & inside[1]) | (inside[0] & nearby[1])
    return one_hot(same), jnp.where(same, 2.0, jnp.where(near, 1.0, 0.0)).astype(jnp.bfloat16)


def gather_matrix(cells, steps=1):
    size = cells >> steps
    shape = (cells * cells, min(size**3, LANES))
    y, z = split_index(iota(shape, 0), cells, 2)
    _, far_y, far_z = split_index(iota(shape, 1), size, 3)
    return plane_blocks(y, z, far_y, far_z, steps)


def block_matrices(cells, blocks_first):
    half = cells // 2
    shape = (half**3, cells**3) if blocks_first else (cells**3, half**3)
    fine = split_index(iota(shape, 1 if blocks_first else 0), cells, 3)
    block = split_index(iota(shape, 0 if blocks_first else 1), half, 3)
    inside = [(f >> 1) == b for f, b in zip(fine, block)]
    nearby = [(f >> 1) + 2 * (f & 1) - 1 == b for f, b in zip(fine, block)]
    same = inside[0] & inside[1] & inside[2]
    near = (
        (nearby[0] & inside[1] & inside[2])
        | (inside[0] & nearby[1] & inside[2])
        | (inside[0] & inside[1] & nearby[2])
    )
    return one_hot(same), jnp.where(same, 3.0, jnp.where(near, 1.0, 0.0)).astype(jnp.bfloat16)


def plane_restrict(field, gather, cells, count, steps=1):
    size = cells >> steps
    width = gather.shape[1]
    per = width // (size * size) << steps
    spread_out = times_choice(field, gather)
    shape = (cells, width)
    own = split_index(iota(shape, 1), size, 3)[0] == ((iota(shape, 0) & (per - 1)) >> steps)
    group = iota(shape, 0) // per
    rows = []
    for c in range(count):
        values = jnp.where(own, spread_out[c * cells : (c + 1) * cells], 0.0)
        tiles = [
            jnp.sum(jnp.where(group == i, values, 0.0), axis=0, keepdims=True) for i in range(cells // per)
        ]
        rows.append(tiles[0] if len(tiles) == 1 else jnp.concatenate(tiles, axis=1))
    return 0.125**steps * (rows[0] if count == 1 else jnp.concatenate(rows, axis=0))


def plane_prolong(coarse, cells, count):
    half = cells // 2
    wide = rows_of_tiles(coarse[:count], cells)
    fine, nearby = [], []
    for tile in range(cells * cells // LANES):
        x, y, z = grid(cells, count, tile)
        start = ((x >> 1) * half * half) & (LANES - 1)
        half_y, half_z = y >> 1, z >> 1
        other_y, other_z = half_y + 2 * (y & 1) - 1, half_z + 2 * (z & 1) - 1
        inside_y, inside_z = (other_y & (half - 1)) == other_y, (other_z & (half - 1)) == other_z
        values = lane_gather(wide, start + half_y * half + half_z)
        beside_y = lane_gather(wide, start + (other_y & (half - 1)) * half + half_z)
        beside_z = lane_gather(wide, start + half_y * half + (other_z & (half - 1)))
        fine.append(values)
        nearby.append(2.0 * values + jnp.where(inside_y, beside_y, 0.0) + jnp.where(inside_z, beside_z, 0.0))
    return jnp.concatenate(fine, axis=1), jnp.concatenate(nearby, axis=1)


def sweep_power(scale, cells, weight):
    size = cells**3
    shape = (size, size)
    here = split_index(iota(shape, 0), cells, 3)
    there = split_index(iota(shape, 1), cells, 3)
    distance = functools.reduce(lambda a, b: a + b, [jnp.abs(a - b) for a, b in zip(here, there)])
    one = jnp.where(distance == 0, 1.0, 0.0)
    return (1.0 - damping) * one + jnp.where(distance == 1, weight * scale, 0.0), one


def square(power):
    return times_parts(power, both_parts(power))


def powers_sum(total, power):
    done = 2
    while done < COARSE_SWEEPS:
        total = total + times_parts(total, both_parts(power))
        done *= 2
        if done < COARSE_SWEEPS:
            power = square(power)
    return total


def turn(k, count):
    return (k + 1) * (LANES - count) % LANES


def free_lanes(rows, count):
    shape = (rows, LANES)
    return (iota(shape, 1) // (LANES - count) == iota(shape, 0)) & (iota(shape, 0) < LANES // (LANES - count))


def load(pairs, semaphores):
    copies = [pltpu.make_async_copy(a, b, semaphores.at[i]) for i, (a, b) in enumerate(pairs)]
    for copy in copies:
        copy.start()
    return copies


def before_kernel(
    cells,
    sizes,
    direction_in,
    residual_in,
    reaction_in,
    primal_index_in,
    region_inverse_in,
    coarse_map_in,
    direction,
    residual,
    source_out,
    front_out,
    inverse_out,
    half_out,
    quarter_out,
    gather_out,
    coarsen_out,
    sweeps_out,
    reaction,
    primal_index,
    region_inverse,
    coarse_map,
    semaphores,
):
    copies = load(
        [
            (direction_in, direction),
            (reaction_in, reaction),
            (primal_index_in, primal_index),
            (residual_in, residual),
            (coarse_map_in, coarse_map),
            (region_inverse_in, region_inverse),
        ],
        semaphores,
    )
    face = cells * cells
    n_sub = sizes[1]
    half = cells // 2
    gather, gather_near = gather_matrix(cells)
    gather_out[...] = jnp.concatenate([gather, gather_near], axis=0)
    quarter_gather = gather_matrix(cells, 2)[0]
    coarsen, coarsen_near = block_matrices(half, False)
    coarsen_out[...] = jnp.concatenate([jnp.concatenate([x, x], axis=1) for x in (coarsen, coarsen_near)], axis=0)
    refine = jnp.concatenate(block_matrices(half, True), axis=1)
    for copy in copies[:3]:
        copy.wait()
    react = reaction[0]
    scale = damping / (plane_restrict(react, quarter_gather, cells, 1, 2) + 6.0 * 0.0625)
    quarter_out[...] = 0.125 * jnp.concatenate([scale, scale], axis=1)
    power, one = sweep_power(scale, half // 2, 0.0625)
    second_power = square(power)
    diagonal = react + 6.0
    inverse_out[0] = damping / diagonal
    inverse_out[1] = diagonal
    half_scale = damping / (plane_restrict(react, gather, cells, 1) + 6.0 * 0.25)
    half_out[...] = half_scale
    faces = faces_of(direction)
    count = primal_index.shape[1]
    group, spot, _, _ = decode(column_of(primal_index[...]), cells)
    nine = jnp.concatenate(faces + [jnp.zeros((7, face), jnp.float32)], axis=0)
    gathered = choice_times(one_hot(iota((count, 16), 1) == group), nine)
    primal = jnp.sum(jnp.where(iota((count, face), 1) == spot, gathered, 0.0), axis=1, keepdims=True)
    lane = iota((1, LANES), 1)
    line = jnp.sum(
        jnp.where(iota((count, LANES), 0) == iota((count, LANES), 1), primal, 0.0), axis=0, keepdims=True
    )
    for copy in copies[3:]:
        copy.wait()
    refined = times_choice(powers_sum(one + power, second_power), refine)
    sweeps_out[...] = stacked_parts(
        (1.0 - damping) * refined[:, : half**3] + 0.25 * half_scale * refined[:, half**3 :]
    )
    row_x = iota((cells, face), 0)
    source = unfold(faces[1], faces[2], cells, True)
    own_x = jnp.concatenate(
        [jnp.where(row_x == cells - 1, jnp.broadcast_to(faces[0][c : c + 1], (cells, face)), 0.0) for c in range(3)],
        axis=0,
    )
    source_out[...] = source + own_x
    share = jnp.sum(primal * coarse_map[0], axis=0, keepdims=True)
    product = jnp.sum(primal * region_inverse[0], axis=0, keepdims=True)
    blank = jnp.zeros((1, LANES - count), jnp.float32)
    blocks = jnp.concatenate(
        [jnp.concatenate([product[:, q * count : (q + 1) * count], blank], axis=1) for q in range(n_sub)], axis=0
    )
    me_sub = lax.axis_index("sub")
    own = jnp.sum(jnp.where(iota(blocks.shape, 0) == me_sub, blocks, 0.0), axis=0, keepdims=True)
    own = jnp.sum(own * line, axis=1, keepdims=True)
    blocks = pltpu.roll(blocks, n_sub - 1 - me_sub, 0)
    opposite = n_sub // 2
    twice = jnp.where(iota((opposite, LANES), 0) == (opposite - 1 if n_sub % 2 == 0 else opposite), 1.0, 2.0)
    squares = jnp.concatenate([residual[i] for i in range(9)], axis=0)
    squares = jnp.sum(jnp.sum(squares * squares, axis=0, keepdims=True), axis=1, keepdims=True)
    line = jnp.where(lane == count, own, jnp.where(lane == count + 1, squares, line))
    front_out[...] = jnp.zeros_like(front_out)
    blocks = blocks[:opposite] * twice
    for k in range(opposite):
        front_out[k : k + 1, :] = pltpu.roll(blocks[k : k + 1], turn(k, count), 1)
    front_out[opposite : opposite + 1, :] = line
    for i in range(share.shape[1] // LANES):
        front_out[opposite + 1 + i : opposite + 2 + i, :] = share[:, i * LANES : (i + 1) * LANES]


def solve_kernel(
    cells,
    sizes,
    count,
    source_own,
    from_x,
    from_y,
    from_z,
    inverses,
    front,
    halves,
    quarter,
    gather,
    coarsen,
    sweeps,
    base_out,
    send_out,
    buffer,
    semaphores,
):
    face = cells * cells
    rows = 3 * cells
    r = lax.axis_index("region")
    n_region = sizes[0]
    straight = r < n_region // 2
    below_x = faces_of(from_x)[0]
    y_faces, z_faces = faces_of(from_y), faces_of(from_z)
    below_y = jnp.where(straight, y_faces[1], z_faces[1])
    below_z = jnp.where(straight, z_faces[2], y_faces[2])
    n_region, n_sub = sizes
    row_x = iota((cells, face), 0)
    source = source_own[...] - unfold(below_y, below_z, cells, False)
    source = source - jnp.concatenate(
        [jnp.where(row_x == 0, jnp.broadcast_to(below_x[c : c + 1], (cells, face)), 0.0) for c in range(3)],
        axis=0,
    )
    where_x, where_y, where_z = positions(rows, cells)
    last = cells - 1

    def tall(x):
        return jnp.concatenate([x] * 3, axis=0)

    inverse = tall(inverses[0])
    diagonal = tall(inverses[1])

    def beside_x(field):
        total = jnp.where(where_x < last, shift(field, -1, 0), 0.0)
        return total + jnp.where(where_x > 0, shift(field, 1, 0), 0.0)

    def beside(field):
        total = jnp.where(where_y < last, shift(field, -cells, 1), 0.0)
        total = total + jnp.where(where_y > 0, shift(field, cells, 1), 0.0)
        total = total + jnp.where(where_z < last, shift(field, -1, 1), 0.0)
        total = total + jnp.where(where_z > 0, shift(field, 1, 1), 0.0)
        return beside_x(field) + total

    half = cells // 2
    lane = iota((8, half**3), 1)
    half_at = split_index(lane, half, 3)
    half_scale = halves[...]

    def half_beside(field):
        total = jnp.zeros_like(field)
        for position, reach in zip(half_at, (half * half, half, 1)):
            total = total + jnp.where(position < half - 1, shift(field, -reach, 1), 0.0)
            total = total + jnp.where(position > 0, shift(field, reach, 1), 0.0)
        return total

    def half_cycle(right):
        swept = half_scale * right
        remain = times_choice(jnp.concatenate([(1.0 - damping) * right, 0.25 * swept], axis=1), coarsen[...])
        local = (2.0 - damping) * swept + 0.25 * half_scale * half_beside(swept)
        return local + times_stacked(remain * quarter[...], sweeps[...])

    def correct(residual):
        swept = inverse * residual
        remain = (1.0 - damping) * residual
        right = plane_restrict(
            jnp.concatenate([remain + beside_x(swept), swept], axis=1), gather[...], cells, 3
        )
        right = jnp.concatenate([right, jnp.zeros((5, half**3), jnp.float32)], axis=0)
        remain = remain + beside(swept)
        correction, nearby = plane_prolong(half_cycle(right), cells, 3)
        return swept + correction, remain - diagonal * correction + beside_x(correction) + nearby

    field, residual = correct(source)
    swept = inverse * residual
    ahead = jnp.where(where_x < last, shift(swept, -1, 0), 0.0)
    ahead = ahead + jnp.where(where_y < last, shift(swept, -cells, 1), 0.0)
    ahead = ahead + jnp.where(where_z < last, shift(swept, -1, 1), 0.0)
    energy = (source + residual) * field + swept * (2.0 * residual - diagonal * swept + 2.0 * ahead)
    energy = jnp.sum(energy, axis=0, keepdims=True)
    energy = functools.reduce(lambda a, b: a + b, [energy[:, i * LANES : (i + 1) * LANES] for i in range(face // LANES)])
    message = front[...]
    message = message + jnp.where(free_lanes(message.shape[0], count), energy, 0.0)
    for device in range(sizes[0] * sizes[1]):
        buffer[device] = message
    (copy,) = load([(buffer, send_out)], semaphores)
    then = (1.0 - damping) * residual + beside(swept)
    field = field + swept
    more, residual = correct(then)
    base_out[...] = field + more + inverse * residual
    copy.wait()


def ends_kernel(cells, base, lower_x, lower_y, lower_z):
    lower_x[...], lower_y[...], lower_z[...] = fold(base[...], cells, False)


def between_kernel(
    cells,
    base,
    primal_index,
    region_inverse,
    coarse_map,
    global_inverse,
    ends_out,
    region_out,
    through_out,
    global_out,
    field_map_out,
    face_map_out,
    ahead_map_out,
):
    face = cells * cells
    ends_out[...] = jnp.concatenate(fold(base[...], cells, True) + [jnp.zeros((7, face), jnp.float32)], axis=0)
    count = primal_index.shape[1]
    group, _, place, _ = decode(primal_index[...], cells)
    choose = jnp.concatenate(
        [one_hot(iota((3 * cells, count), 0) == place), one_hot(iota((16, count), 0) == group)], axis=0
    )
    _, spot, _, lane = decode(column_of(primal_index[...]), cells)
    at = iota((count, face), 1)
    number = iota((count, 2 * face), 0) + 1
    spots = jnp.where(jnp.concatenate([at == lane, at == spot], axis=1), number, 0).astype(jnp.float32)
    maps = choice_times(choose, spots).astype(jnp.int32)
    maps = jnp.where(maps > 0, maps - 1, LANES - 1)
    field_map = maps[: 3 * cells, :face]
    field_map_out[...] = field_map
    face_map_out[...] = maps[3 * cells :, face:]
    _, where_y, where_z = positions(cells, cells)
    end = cells - 1
    ahead_map_out[...] = jnp.concatenate(
        [
            jnp.where(where_y == end, LANES - 1, shift(field_map[cells : 2 * cells], -cells, 1)),
            jnp.where(where_z == end, LANES - 1, shift(field_map[2 * cells :], -1, 1)),
        ],
        axis=0,
    )
    blank = jnp.zeros((count, LANES - count), jnp.float32)
    for q in range(region_out.shape[0]):
        region_out[q] = jnp.concatenate([region_inverse[0, :, q * count : (q + 1) * count], blank], axis=1)
    both = both_parts(global_inverse[...])
    global_out[...] = both
    through_out[...] = times_parts(coarse_map[0], both)


def after_kernel(
    cells,
    sizes,
    count,
    received,
    base,
    ends,
    after_x,
    after_y,
    after_z,
    field_map,
    face_map,
    ahead_map,
    region_blocks,
    through,
    global_parts,
    direction,
    multipliers,
    residual,
    viscosity,
    multipliers_out,
    residual_out,
    velocity_out,
    pressure_out,
):
    face = cells * cells
    n_region, n_sub = sizes
    half = n_sub // 2
    columns = through.shape[1]
    me_region = lax.axis_index("region")
    everything = jnp.sum(received[...], axis=0)
    totals = [everything[half + 1 + i : half + 2 + i] for i in range(columns // LANES)]
    lines = received[:, half, :]
    lines = jnp.where(iota(lines.shape, 1) < count, lines, 0.0).reshape(n_region, n_sub, LANES)
    groups = LANES // (LANES - count)
    turned = [pltpu.roll(lines, turn(k, count), 2) for k in range(min(groups, half))]
    quadratic = jnp.zeros((n_region, n_sub, LANES), jnp.float32)
    for k in range(half):
        products = received[:, k, :].reshape(n_region, n_sub, LANES)
        quadratic = quadratic + products * pltpu.roll(turned[k % groups], n_sub - 1 - k, 1)
    after = [after_x[...], after_y[...], after_z[...]]
    field = base[...]
    field_x, field_y, field_z = [field[c * cells : (c + 1) * cells] for c in range(3)]
    where_x, where_y, where_z = positions(cells, cells)
    end = cells - 1
    step = jnp.where(where_x == end, jnp.broadcast_to(after[0][0:1], (cells, face)), shift(field_x, -1, 0)) - field_x
    step = step + jnp.where(where_y == end, 0.0, shift(field_y, -cells, 1)) - field_y
    step = step + jnp.where(where_z == end, 0.0, shift(field_z, -1, 1)) - field_z
    step = step + unfold(after[1][1:2], after[2][2:3], cells, True)
    jump = ends[:9] - jnp.concatenate(after, axis=0)
    added = jnp.zeros((count, LANES), jnp.float32)
    for i, part in enumerate(totals):
        added = added + through[:, i * LANES : (i + 1) * LANES] * part
    for q in range(n_sub):
        added = added + region_blocks[q] * received[me_region * n_sub + q, half : half + 1, :]
    lifted = jnp.sum(added, axis=1, keepdims=True)
    own_lane = iota((count, LANES), 0) == iota((count, LANES), 1)
    lifted = jnp.sum(jnp.where(own_lane, lifted, 0.0), axis=0, keepdims=True)

    def placed(numbers):
        wide = jnp.broadcast_to(lifted, (numbers.shape[0], LANES))
        return jnp.concatenate(
            [lane_gather(wide, numbers[:, i * LANES : (i + 1) * LANES]) for i in range(face // LANES)], axis=1
        )

    added = placed(field_map)
    ahead = placed(ahead_map)
    velocity = field + added
    for c in range(3):
        velocity_out[0, c] = velocity[c * cells : (c + 1) * cells]
    added_x = added[:cells]
    step = step + jnp.where(where_x == end, 0.0, shift(added_x, -1, 0)) - added_x
    step = step + ahead[:cells] - added[cells : 2 * cells] + ahead[cells:] - added[2 * cells :]
    pressure_out[0] = -viscosity[0] * step
    jump = jump + placed(face_map)[:9]
    total = jnp.concatenate(totals, axis=1)
    piece = total.astype(jnp.bfloat16).astype(jnp.float32)
    row = iota((16, columns), 0)
    parts = jnp.where(row == 0, piece, jnp.where(row == 1, total - piece, 0.0)).astype(jnp.bfloat16)
    top = jnp.dot(parts, global_parts[...], preferred_element_type=jnp.float32)
    top = top[0:1, :columns] + top[1:2, :columns] + top[0:1, columns:]
    own_line = everything[half : half + 1]
    lane = iota((1, LANES), 1)
    quadratic = jnp.sum(quadratic.reshape(n_region * n_sub, LANES), axis=0, keepdims=True)
    energy = jnp.where(free_lanes(everything.shape[0], count), everything, 0.0)
    curvature = quadratic + jnp.where(lane == count, own_line, 0.0) + jnp.sum(energy, axis=0, keepdims=True)
    for i in range(columns // LANES):
        curvature = curvature + totals[i] * top[:, i * LANES : (i + 1) * LANES]
    curvature = jnp.sum(curvature, axis=1, keepdims=True)
    squares = jnp.sum(jnp.where(lane == count + 1, own_line, 0.0), axis=1, keepdims=True)
    alpha = squares / curvature
    for i in range(9):
        residual_out[i] = residual[i] - alpha * jump[i : i + 1]
        multipliers_out[i] = multipliers[i] + alpha * direction[i]


def body(
    sizes,
    multipliers,
    direction,
    residual,
    reaction,
    viscosity,
    primal_index,
    region_inverse,
    coarse_map,
    global_inverse,
):
    n_region, n_sub = sizes
    assert LANES % (LANES - primal_index.shape[1]) == 0 and n_sub // 2 >= LANES // (LANES - primal_index.shape[1])
    cells = reaction.shape[1]
    face = reaction.shape[2]
    count = primal_index.shape[1]
    columns = coarse_map.shape[2]
    height = -(-(n_sub // 2 + 1 + columns // LANES) // 8) * 8
    rows = 3 * cells
    shape = direction.shape
    lines = (9, 1, face)
    f32 = jnp.float32
    bf16 = jnp.bfloat16
    vmem = pl.BlockSpec(memory_space=pltpu.VMEM)
    hbm = pl.BlockSpec(memory_space=pltpu.HBM)

    def like(shape, kind=f32):
        return jax.ShapeDtypeStruct(shape, kind)

    def call(kernel, out_shape, operands, in_hbm=(), scratch=(), out_hbm=0):
        return pl.pallas_call(
            kernel,
            out_shape=out_shape,
            in_specs=[vmem] * len(operands) + [hbm] * len(in_hbm),
            out_specs=[vmem] * (len(out_shape) - out_hbm) + [hbm] * out_hbm,
            scratch_shapes=[pltpu.VMEM(x.shape, x.dtype) for x in scratch]
            + ([pltpu.SemaphoreType.DMA((len(in_hbm) + out_hbm,))] if in_hbm or out_hbm else []),
            compiler_params=pltpu.CompilerParams(vmem_limit_bytes=32 * 1024 * 1024),
        )(*operands, *[pltpu.with_memory_space_constraint(x, pltpu.HBM) for x in in_hbm])

    below_x = shifted_2(direction, "region", 1).reshape(lines)
    def mixed(flip):
        pairs = []
        for r in range(n_region):
            by = DOM_Z if (r < n_region // 2) == flip else 1
            pairs += [(r * n_sub + q, r * n_sub + (q + by) % n_sub) for q in range(n_sub)]
        return lax.ppermute(direction, ("region", "sub"), pairs).reshape(lines)

    below_y = mixed(True)
    below_z = mixed(False)
    multipliers, direction, residual = [x.reshape(lines) for x in (multipliers, direction, residual)]
    half_cells = (cells // 2) ** 3
    direction, residual, source, front, inverses, halves, quarter, gather, coarsen, sweeps = call(
        functools.partial(before_kernel, cells, sizes),
        [
            like(lines),
            like(lines),
            like((rows, face)),
            like((height, LANES)),
            like((2, cells, face)),
            like((1, half_cells)),
            like((1, half_cells // 4)),
            like((2 * face, min(half_cells, LANES)), bf16),
            like((2 * half_cells, half_cells // 4), bf16),
            like((half_cells // 2, half_cells), bf16),
        ],
        [],
        [direction, residual, reaction, primal_index, region_inverse, coarse_map],
        [reaction, primal_index, region_inverse, coarse_map],
    )
    base, sent = call(
        functools.partial(solve_kernel, cells, sizes, count),
        [like((rows, face)), like((n_region * n_sub, height, LANES))],
        [source, below_x, below_y, below_z, inverses, front, halves, quarter, gather, coarsen, sweeps],
        scratch=[like((n_region * n_sub, height, LANES))],
        out_hbm=1,
    )
    received = lax.all_to_all(sent, ("region", "sub"), 0, 0, tiled=True)
    lower_x, lower_y, lower_z = call(
        functools.partial(ends_kernel, cells), [like((3, face))] * 3, [base]
    )
    after_x = shifted_2(lower_x, "region", -1)
    after_y = shifted_2(lower_y, "sub", -DOM_Z)
    after_z = shifted_2(lower_z, "sub", -1)
    ends, region_blocks, through, global_parts, field_map, face_map, ahead_map = call(
        functools.partial(between_kernel, cells),
        [
            like((16, face)),
            like((n_sub, count, LANES)),
            like((count, columns)),
            like((columns, 2 * columns), bf16),
            like((rows, face), jnp.int32),
            like((16, face), jnp.int32),
            like((2 * cells, face), jnp.int32),
        ],
        [base, primal_index, region_inverse, coarse_map, global_inverse],
    )
    new_multipliers, new_residual, velocity, pressure = call(
        functools.partial(after_kernel, cells, sizes, count),
        [like(lines), like(lines), like((1, 3, cells, face)), like((1, cells, face))],
        [
            received,
            base,
            ends,
            after_x,
            after_y,
            after_z,
            field_map,
            face_map,
            ahead_map,
            region_blocks,
            through,
            global_parts,
            direction,
            multipliers,
            residual,
            viscosity,
        ],
    )
    return new_multipliers.reshape(shape), new_residual.reshape(shape), velocity, pressure


def solution(mesh):
    sizes = (mesh.shape["region"], mesh.shape["sub"])
    whole = P(("region", "sub"))
    in_specs = (whole,) * 6 + (P("region", "sub"), whole, P())
    return jax.shard_map(
        functools.partial(body, sizes), mesh=mesh, in_specs=in_specs, out_specs=(whole,) * 4, check_vma=False
    )
```
